32 devices in a mesh: dp: 32 (over z, y, x, core).
Axes of the slice: x: 2, y: 2, z: 4, core: 2. Of those that a mesh axis runs over, the one named last changes fastest.
Arguments:
- tokens: bfloat16 [32, 1024, 512], P('dp'), may hold values from -6 to 6
- memory: bfloat16 [32, 1024, 512], P('dp'), may hold values from -6 to 6
- directions: int32 [32], P('dp'), may hold values from 0 to 1
- target_len: int32 [32], P('dp'), may hold values from 256 to 1024, as said below
- memory_len: int32 [32], P('dp'), may hold values from 256 to 1024, as said below
- self_qkv: bfloat16 [786432], P('dp'), may hold values from -0.25 to 0.25
- self_out: bfloat16 [262144], P('dp'), may hold values from -1 to 1
- cross_query: bfloat16 [262144], P('dp'), may hold values from -0.25 to 0.25
- cross_kv: bfloat16 [524288], P('dp'), may hold values from -0.25 to 0.25
- cross_out: bfloat16 [262144], P('dp'), may hold values from -1 to 1
- ffn_in: bfloat16 [1048576], P('dp'), may hold values from -0.25 to 0.25
- ffn_out: bfloat16 [1048576], P('dp'), may hold values from -0.125 to 0.125
- vectors: bfloat16 [9728], P('dp'), may hold values from -1.2 to 1.6
- cotangent: bfloat16 [32, 1024, 512], P('dp'), may hold values from -6 to 6
Outputs:
- out: bfloat16 [32, 1024, 512], P('dp')
- d_tokens: float32 [32, 1024, 512], P('dp')
- d_memory: float32 [32, 1024, 512], P('dp')
- g_self_qkv: float32 [786432], P('dp')
- g_self_out: float32 [262144], P('dp')
- g_cross_query: float32 [262144], P('dp')
- g_cross_kv: float32 [524288], P('dp')
- g_cross_out: float32 [262144], P('dp')
- g_ffn_in: float32 [1048576], P('dp')
- g_ffn_out: float32 [1048576], P('dp')
- g_vectors: float32 [9728], P('dp')
The draws below stay inside these ranges and needn't reach their ends.
Inputs may be any that keep to these rules, and one draw needn't show every extreme that they name: `target_len`: positions from this length on are padding; some sequence has exactly 1024 and some exactly 256. `memory_len`: memory positions from this length on are padding; some sequence has exactly 1024 and some exactly 256.
All inputs are finite; a program needn't handle non-finite values.
Results may differ from the reference program's by a relative error of at most 0.017.
The reference program's roundings to bfloat16 on the way count: a program that leaves them out, or rounds other values in their place, can miss the bound.
Values may be sent and summed in bfloat16 or wider, within the bound.
No kernel may reach another device: no remote copies, remote signals or barrier semaphores. Data moves between devices by JAX's collectives and lax.ppermute only.
A program may use at most 128 MiB of HBM per device.

```python
import jax
import jax.numpy as jnp
from jax import lax

D = 512
HEADS = 8
FF = 2048
HEAD_DIM = 64
TGT_LEN = 1024
MEM_LEN = 1024
SEQS = 32


def ragged_lengths(key, seq_count, longest):
    values = jax.random.randint(key, (seq_count,), longest // 4, longest + 1)
    shuffled = jax.random.permutation(jax.random.fold_in(key, 7), seq_count)
    values = values.at[shuffled[0]].set(longest)
    values = values.at[shuffled[1]].set(longest // 4)
    return values.astype(jnp.int32)


def draw_target_len(key, part):
    key = jax.random.fold_in(key, 11)
    return ragged_lengths(key, SEQS, TGT_LEN)


def draw_memory_len(key, part):
    key = jax.random.fold_in(key, 12)
    return ragged_lengths(key, SEQS, MEM_LEN)


def draw_vectors(key, part):
    key = jax.random.fold_in(key, 13)
    total_len = 15 * D + FF
    row_index = jnp.arange(total_len) // D
    spread = jnp.clip(jax.random.normal(key, (total_len,), jnp.float32) * 0.3, -0.59, 0.59)
    gain_rows = (row_index >= 7) & (row_index <= 9)
    embed_rows = (row_index >= 13) & (row_index <= 14)
    values = jnp.where(gain_rows, 1.0 + spread, jnp.where(embed_rows, 2.0 * spread, spread))
    return values.astype(jnp.bfloat16)


def with_ends(values, rng, smallest, high):
    extent = values.shape
    place = [jax.random.randint(jax.random.fold_in(rng, axis), (), 0, extent[axis]) for axis in range(len(extent))]
    values = values.at[tuple(place)].set(smallest)
    longest = extent.index(max(extent))
    place[longest] = (place[longest] + 1) % extent[longest]
    return values.at[tuple(place)].set(high)


def levels(stream_key, dims, split, least, largest):
    level, own = 1.0, jax.random.fold_in(stream_key, 6)
    for axis_at, shards_of in split:
        steps = jnp.exp(jax.random.uniform(jax.random.fold_in(own, axis_at), (shards_of,), jnp.float32, least / len(split), largest / len(split)))
        level = level * jnp.repeat(steps, dims[axis_at] // shards_of).reshape([-1 if axis == axis_at else 1 for axis in range(len(dims))])
    return level


def noise(key, shape, deviation, bound, split=(), held_as=jnp.bfloat16):
    drawn = jax.random.normal(key, shape, jnp.float32) * deviation
    if len(split) > 0:
        drawn = levels(key, shape, split, -0.22, 0.18) * drawn
    return jnp.clip(drawn, min=-bound, max=bound).astype(held_as)


def setup_inputs(seed: int = 0) -> dict:
    key_of = jax.random.split(jax.random.key(seed), 15)
    tokens = noise(key_of[0], (SEQS, TGT_LEN, D), 1.0, 6.0, ((0, 32),))
    memory = noise(key_of[1], (SEQS, MEM_LEN, D), 1.0, 6.0, ((0, 32),))
    directions = with_ends(jax.random.randint(key_of[2], (SEQS,), 0, 2), jax.random.fold_in(key_of[2], 1), 0, 1).astype(jnp.int32)
    target_len = draw_target_len(jax.random.fold_in(key_of[14], 71), 0)
    memory_len = draw_memory_len(jax.random.fold_in(key_of[14], 71), 0)
    self_qkv = noise(key_of[5], (3 * D * D,), D ** -0.5, 0.25, ((0, 32),))
    self_out = noise(key_of[6], (D * D,), (D // 16) ** -0.5, 1.0, ((0, 32),))
    cross_query = noise(key_of[7], (D * D,), D ** -0.5, 0.25, ((0, 32),))
    cross_kv = noise(key_of[8], (2 * D * D,), D ** -0.5, 0.25, ((0, 32),))
    cross_out = noise(key_of[9], (D * D,), (D // 16) ** -0.5, 1.0, ((0, 32),))
    ffn_in = noise(key_of[10], (D * FF,), D ** -0.5, 0.25, ((0, 32),))
    ffn_out = noise(key_of[11], (FF * D,), FF ** -0.5, 0.125, ((0, 32),))
    vectors = draw_vectors(jax.random.fold_in(key_of[14], 71), 0)
    cotangent = noise(key_of[13], (SEQS, TGT_LEN, D), 1.0, 6.0, ((0, 32),))
    return {"tokens": tokens, "memory": memory, "directions": directions, "target_len": target_len, "memory_len": memory_len, "self_qkv": self_qkv, "self_out": self_out, "cross_query": cross_query, "cross_kv": cross_kv, "cross_out": cross_out, "ffn_in": ffn_in, "ffn_out": ffn_out, "vectors": vectors, "cotangent": cotangent}


mask_fill = -1000000000.0
norm_eps = 1e-05
highest = lax.Precision.HIGHEST

@jax.custom_vjp
def low(v):
    return lax.optimization_barrier(v.astype(jnp.bfloat16)).astype(jnp.float32)

@jax.custom_vjp
def low_back(v):
    return v

def low_keep(v):
    return (low(v), None)

def low_pass(kept, grad):
    return (grad,)

def back_keep(v):
    return (v, None)

def back_low(kept, grad):
    return (low(grad),)
low.defvjp(low_keep, low_pass)
low_back.defvjp(back_keep, back_low)

def matmul(left, right):
    return jnp.dot(left, right, precision=highest, preferred_element_type=jnp.float32)

def norm_layer(values, gain, shift):
    center = lax.optimization_barrier(jnp.mean(values, axis=-1, keepdims=True))
    offsets = values - center
    spread = lax.optimization_barrier(jnp.mean(offsets * offsets, axis=-1, keepdims=True))
    return offsets * lax.rsqrt(spread + norm_eps) * gain + shift

def attend(queries, key_rows, value_rows, allowed):
    length = queries.shape[0]
    others = key_rows.shape[0]
    split_query = queries.reshape(length, HEADS, HEAD_DIM)
    split_key = key_rows.reshape(others, HEADS, HEAD_DIM)
    split_value = value_rows.reshape(others, HEADS, HEAD_DIM)
    scores = jnp.einsum('qhd,khd->hqk', split_query, split_key, precision=highest) * HEAD_DIM ** (-0.5)
    scores = low_back(jnp.where(allowed[None], scores, mask_fill))
    highest_score = lax.optimization_barrier(jnp.max(scores, axis=-1, keepdims=True))
    powered = jnp.exp(scores - highest_score)
    attention = low(powered / lax.optimization_barrier(jnp.sum(powered, axis=-1, keepdims=True)))
    blended = jnp.einsum('hqk,khd->qhd', attention, split_value, precision=highest)
    return blended.reshape(length, HEADS * HEAD_DIM)

def layer_forward(params, tokens, memory, direction, target_count, memory_count):
    w_qkv, w_out, c_query, c_kv, c_out, f_in, f_out, vectors = params
    vector_rows = vectors[:15 * D].reshape(15, D)
    ffn_bias = vectors[15 * D:]
    w_qkv = w_qkv.reshape(D, 3 * D)
    w_out = w_out.reshape(D, D)
    c_query = c_query.reshape(D, D)
    c_kv = c_kv.reshape(D, 2 * D)
    c_out = c_out.reshape(D, D)
    f_in = f_in.reshape(D, FF)
    f_out = f_out.reshape(FF, D)
    embedding = jnp.where(direction == 1, vector_rows[14], vector_rows[13])
    started = tokens + embedding
    shared = low(started)
    projected = matmul(shared, w_qkv)
    queries = low(low_back(projected[:, :D] + vector_rows[0]))
    key_rows = low(low_back(projected[:, D:2 * D]))
    value_rows = low(low_back(projected[:, 2 * D:] + vector_rows[1]))
    position = jnp.arange(TGT_LEN)
    causal = position[None, :] <= position[:, None]
    attended = low(low_back(attend(queries, key_rows, value_rows, causal)))
    branch = low_back(matmul(attended, w_out) + vector_rows[2])
    first = norm_layer(started + branch, vector_rows[7], vector_rows[10])
    first_low = low(first)
    cross_queries = low(low_back(matmul(first_low, c_query) + vector_rows[3]))
    memory_proj = matmul(memory, c_kv)
    cross_keys = low(low_back(memory_proj[:, :D]))
    cross_values = low(low_back(memory_proj[:, D:] + vector_rows[4]))
    visible = jnp.broadcast_to((jnp.arange(MEM_LEN) < memory_count)[None, :], (TGT_LEN, MEM_LEN))
    cross_mixed = low(low_back(attend(cross_queries, cross_keys, cross_values, visible)))
    cross_branch = low_back(matmul(cross_mixed, c_out) + vector_rows[5])
    second = norm_layer(first + cross_branch, vector_rows[8], vector_rows[11])
    hidden_pre = low_back(matmul(low(second), f_in) + ffn_bias)
    hidden_act = low(jax.nn.gelu(hidden_pre, approximate=False))
    ffn_branch = low_back(matmul(hidden_act, f_out) + vector_rows[6])
    valid = (position < target_count).astype(jnp.float32)[:, None]
    return norm_layer(second + ffn_branch, vector_rows[9], vector_rows[12]) * valid

def reference(tokens, memory, directions, target_len, memory_len, self_qkv, self_out, cross_query, cross_kv, cross_out, ffn_in, ffn_out, vectors, cotangent):
    params = tuple((weight.astype(jnp.float32) for weight in (self_qkv, self_out, cross_query, cross_kv, cross_out, ffn_in, ffn_out, vectors)))

    def one_sequence(running, items):
        seq_tokens, seq_memory, direction, target_count, memory_count, seq_cotangent = items

        def run_layer(weights, inputs, encoded):
            return layer_forward(weights, inputs, encoded, direction, target_count, memory_count)
        result, pullback = jax.vjp(run_layer, params, seq_tokens.astype(jnp.float32), seq_memory.astype(jnp.float32))
        grad_params, grad_tokens, grad_memory = pullback(seq_cotangent.astype(jnp.float32))
        running = tuple((total_now + increment for total_now, increment in zip(running, grad_params)))
        return (running, (result.astype(jnp.bfloat16), grad_tokens, grad_memory))
    zeros = tuple((jnp.zeros_like(weight) for weight in params))
    totals, (result, grad_tokens, grad_memory) = lax.scan(one_sequence, zeros, (tokens, memory, directions, target_len, memory_len, cotangent))
    return (result, grad_tokens, grad_memory, totals[0], totals[1], totals[2], totals[3], totals[4], totals[5], totals[6], totals[7])
```

```python
import jax
import jax.numpy as jnp
from jax import lax
from jax.experimental import pallas as pl
from jax.experimental.pallas import tpu as pltpu
from jax.sharding import PartitionSpec as P

HEADS = 8
STEP = 256
PAIR = 2 * STEP
AUG = 16
SAFE_SQUARE = 3600.0
mask_fill = -1000000000.0
norm_eps = 1e-05
low = jnp.bfloat16
full = jnp.float32


def contract(left, right, left_dim, right_dim):
    return lax.dot_general(
        left, right, (((left_dim,), (right_dim,)), ((), ())), preferred_element_type=full
    )


def nn(left, right):
    return contract(left, right, 1, 0)


def tn(left, right):
    return contract(left, right, 0, 0)


def nt(left, right):
    return contract(left, right, 1, 1)


def block(index):
    return slice(index * STEP, (index + 1) * STEP)


def blocks_of(length):
    return (length + STEP - 1) // STEP


def split_three(values):
    first = values.astype(low)
    rest = values - first.astype(full)
    second = rest.astype(low)
    third = (rest - second.astype(full)).astype(low)
    return first, second, third


def normalize(values):
    center = jnp.mean(values, axis=0, keepdims=True)
    offsets = values - center
    spread = jnp.mean(offsets * offsets, axis=0, keepdims=True)
    scale = lax.rsqrt(spread + norm_eps)
    return offsets * scale, scale


def norm_backward(grad, hat, scale, gain):
    scaled = grad * gain
    center = jnp.mean(scaled, axis=0, keepdims=True)
    along = jnp.mean(scaled * hat, axis=0, keepdims=True)
    return (scaled - center - hat * along) * scale


def fold_lanes(values):
    return values[:, :128] + values[:, 128:]


def lane_total(partial):
    ones = jnp.ones((8, 128), full)
    return lax.dot_general(
        ones,
        partial,
        (((1,), (1,)), ((), ())),
        precision=lax.Precision.HIGHEST,
        preferred_element_type=full,
    )[0:1]


def token_total(values):
    return nt(jnp.ones((AUG, values.shape[1]), low), values)[0:1]


def head_rows(head, head_dim):
    return pl.ds(pl.multiple_of(head * head_dim, head_dim), head_dim)


def square_peak(values, head_dim):
    squares = jnp.square(values.astype(full))
    count = values.shape[0] // head_dim
    return jnp.max(jnp.sum(squares.reshape(count, head_dim, values.shape[1]), axis=1))


def attend_forward(q_ref, k_ref, v_ref, mix_ref, sums_ref, mask_rows, head_dim, pairs, keys, shifted):
    causal = mask_rows is None

    def one_head(head, carry):
        rows = head_rows(head, head_dim)
        key_head = k_ref[rows, :keys]
        if not causal:
            key_head = jnp.concatenate([key_head, mask_rows[:, :keys]], 0)
        value_head = jnp.concatenate([v_ref[rows, :keys], jnp.ones((AUG, keys), low)], 0)
        for pair in range(pairs):
            columns = slice(pair * PAIR, (pair + 1) * PAIR)
            query = q_ref[rows, columns]
            if causal:
                main = pair * PAIR + STEP
                scores = tn(key_head[:, :main], query)
                late = tn(key_head[:, main : main + STEP], query[:, STEP:])
                key_pos = lax.broadcasted_iota(jnp.int32, (STEP, STEP), 0)
                query_pos = lax.broadcasted_iota(jnp.int32, (STEP, STEP), 1)
                allowed = key_pos <= query_pos
                edge = scores[main - STEP :]
                edge = jnp.concatenate(
                    [jnp.where(allowed, edge[:, :STEP], mask_fill), edge[:, STEP:]], 1
                )
                scores = edge if main == STEP else jnp.concatenate([scores[: main - STEP], edge], 0)
                late = jnp.where(allowed, late, mask_fill)
            else:
                query = jnp.concatenate([query, jnp.ones((AUG, PAIR), low)], 0)
                scores = tn(key_head, query)
            if shifted:
                highest = jnp.max(scores, axis=0, keepdims=True)
                if causal:
                    second = jnp.maximum(
                        highest[:, STEP:], jnp.max(late, axis=0, keepdims=True)
                    )
                    highest = jnp.concatenate([highest[:, :STEP], second], 1)
                    late = late - second
                scores = scores - highest
            powered = jnp.exp(scores).astype(low)
            if causal:
                mixed = nn(value_head[:, :main], powered)
                extra = nn(value_head[:, main : main + STEP], jnp.exp(late).astype(low))
                mixed = jnp.concatenate([mixed[:, :STEP], mixed[:, STEP:] + extra], 1)
            else:
                mixed = nn(value_head, powered)
            total = mixed[head_dim : head_dim + 1]
            mix_ref[rows, columns] = mixed[:head_dim] / total
            log_sum = jnp.log(total)
            sums_ref[pl.ds(head, 1), columns] = log_sum + highest if shifted else log_sum
        return carry

    lax.fori_loop(0, HEADS, one_head, 0)


def attend_backward(
    q_ref, k_ref, v_ref, mix_ref, sums_ref, grad_ref, dq_ref, dk_ref, dv_ref,
    key_sum, value_sum, mask_rows, head_dim, steps, keys, scale
):
    causal = mask_rows is None
    length = steps * STEP

    def one_head(head, carry):
        rows = head_rows(head, head_dim)
        key_head = k_ref[rows, :keys]
        value_head = v_ref[rows, :keys]
        query = q_ref[rows, :length]
        grad = grad_ref[rows, :length]
        inner = jnp.sum(grad.astype(full) * mix_ref[rows, :length], axis=0, keepdims=True)
        one = jnp.ones((1, length), low)
        blank = jnp.zeros((AUG - 4, length), low)
        query_aug = jnp.concatenate(
            [query, *split_three(sums_ref[pl.ds(head, 1), :length]), one, blank], 0
        )
        grad_aug = jnp.concatenate([grad, *split_three(inner), one, blank], 0)
        minus = jnp.full((3, keys), -1.0, low)
        key_blank = jnp.zeros((AUG - 3, keys), low)
        value_aug = jnp.concatenate([value_head, minus, key_blank], 0)
        if causal:
            key_aug = jnp.concatenate([key_head, minus, key_blank], 0)
        else:
            key_aug = jnp.concatenate(
                [key_head, minus, mask_rows[0:1, :keys], key_blank[1:]], 0
            )
        for step in range(steps):
            span = block(step)
            count = (step + 1) * STEP if causal else keys
            scores = tn(query_aug[:, span], key_aug[:, :count])
            chances = jnp.exp(scores)
            if causal:
                query_pos = lax.broadcasted_iota(jnp.int32, (STEP, STEP), 0)
                key_pos = lax.broadcasted_iota(jnp.int32, (STEP, STEP), 1)
                edge = jnp.where(key_pos <= query_pos, chances[:, count - STEP :], 0.0)
                chances = (
                    edge if count == STEP
                    else jnp.concatenate([chances[:, : count - STEP], edge], 1)
                )
            grad_chances = tn(grad_aug[:, span], value_aug[:, :count])
            grad_scores = (chances * grad_chances).astype(low)
            to_value = nn(grad[:, span], chances.astype(low))
            to_key = nn(query[:, span], grad_scores)
            to_query = nt(key_head[:, :count], grad_scores)
            dq_ref[rows, span] = (to_query * scale).astype(low)
            if step == 0:
                value_sum[:, :count] = to_value
                key_sum[:, :count] = to_key
            elif causal:
                old = count - STEP
                value_sum[:, :old] += to_value[:, :old]
                key_sum[:, :old] += to_key[:, :old]
                value_sum[:, old:count] = to_value[:, old:]
                key_sum[:, old:count] = to_key[:, old:]
            else:
                value_sum[:, :count] += to_value
                key_sum[:, :count] += to_key
        dv_ref[rows, :keys] = value_sum[:, :keys].astype(low)
        dk_ref[rows, :keys] = key_sum[:, :keys].astype(low)
        return carry

    lax.fori_loop(0, HEADS, one_head, 0)


def self_forward_kernel(
    facts, tokens, w_qkv, columns, token_t, q_ref, k_ref, v_ref, mix_ref, sums_ref, peaks
):
    length, width = tokens.shape
    head_dim = width // HEADS
    count = blocks_of(facts[1])
    scale = head_dim ** (-0.5)
    embed = jnp.where(facts[0] == 1, columns[:, 14:15], columns[:, 13:14])
    peaks[0] = 0.0
    peaks[1] = 0.0
    for step in range(length // STEP):

        @pl.when(step < count)
        def project():
            span = block(step)
            flipped = tokens[span, :].T
            token_t[:, span] = flipped
            shared = (flipped.astype(full) + embed).astype(low)
            made = tn(w_qkv[...], shared)
            query = (made[:width] + columns[:, 0:1]).astype(low) * scale
            key = made[width : 2 * width].astype(low)
            q_ref[:, span] = query
            k_ref[:, span] = key
            v_ref[:, span] = (made[2 * width :] + columns[:, 1:2]).astype(low)
            peaks[0] = jnp.maximum(peaks[0], square_peak(query, head_dim))
            peaks[1] = jnp.maximum(peaks[1], square_peak(key, head_dim))

    safe = peaks[0] * peaks[1] <= SAFE_SQUARE
    pairs = (count + 1) // 2
    for wanted in range(1, length // PAIR + 1):
        for shifted in (False, True):

            @pl.when((pairs == wanted) & (safe != shifted))
            def attend():
                attend_forward(
                    q_ref, k_ref, v_ref, mix_ref, sums_ref, None, head_dim, wanted,
                    wanted * PAIR, shifted,
                )


def cross_forward_kernel(
    facts, token_t, memory, mix, w_out, c_query, c_kv, columns,
    hat_ref, scale_ref, memory_t, q_ref, k_ref, v_ref, cross_mix, sums_ref, mask_ref, peaks
):
    length = token_t.shape[1]
    others, width = memory.shape
    head_dim = width // HEADS
    score_scale = head_dim ** (-0.5)
    count = blocks_of(facts[1])
    key_count = blocks_of(facts[2])
    embed = jnp.where(facts[0] == 1, columns[:, 14:15], columns[:, 13:14])
    peaks[0] = 0.0
    peaks[1] = 0.0
    for step in range(others // STEP):

        @pl.when(step < key_count)
        def encode():
            span = block(step)
            flipped = memory[span, :].T
            memory_t[:, span] = flipped
            made = tn(c_kv[...], flipped)
            key = made[:width].astype(low)
            k_ref[:, span] = key
            v_ref[:, span] = (made[width:] + columns[:, 4:5]).astype(low)
            peaks[1] = jnp.maximum(peaks[1], square_peak(key, head_dim))

    for step in range(length // STEP):

        @pl.when(step < count)
        def first():
            span = block(step)
            started = token_t[:, span].astype(full) + embed
            total = started + tn(w_out[...], mix[:, span].astype(low)) + columns[:, 2:3]
            hat, scale = normalize(total)
            hat_ref[:, span] = hat
            scale_ref[:, span] = jnp.broadcast_to(scale, (8, STEP))
            shared = (hat * columns[:, 7:8] + columns[:, 10:11]).astype(low)
            query = (tn(c_query[...], shared) + columns[:, 3:4]).astype(low) * score_scale
            q_ref[:, span] = query
            peaks[0] = jnp.maximum(peaks[0], square_peak(query, head_dim))

    position = lax.broadcasted_iota(jnp.int32, (AUG, others), 1)
    row = lax.broadcasted_iota(jnp.int32, (AUG, others), 0)
    hidden = (position >= facts[2]) & (row == 0)
    mask_ref[...] = jnp.where(hidden, mask_fill, 0.0).astype(low)
    safe = peaks[0] * peaks[1] <= SAFE_SQUARE
    pairs = (count + 1) // 2
    for wanted in range(1, length // PAIR + 1):
        for wanted_keys in range(1, others // STEP + 1):
            for shifted in (False, True):

                @pl.when((pairs == wanted) & (key_count == wanted_keys) & (safe != shifted))
                def attend():
                    attend_forward(
                        q_ref, k_ref, v_ref, cross_mix, sums_ref, mask_ref[...], head_dim,
                        wanted, wanted_keys * STEP, shifted,
                    )


def gelu_parts(values):
    half = 0.5 * (1.0 + lax.erf(values * (0.5**0.5)))
    bell = jnp.exp(-0.5 * values * values) * 0.3989422804014327
    return values * half, half + values * bell


def ffn_kernel(
    facts, hat_one, cross_mix, cotangent, c_out, f_in, f_out, columns,
    out_ref, dr_ref, dmix_ref, g_in, g_out, g_cross_out, g_rows,
    sum_in, sum_out, sum_cross, slope, lanes
):
    length, width = cotangent.shape
    hidden = f_in.shape[1]
    parts = hidden // width
    count = blocks_of(facts[1])
    g_rows[...] = jnp.zeros_like(g_rows)
    lanes[...] = jnp.zeros_like(lanes)
    for step in range(length // STEP):

        @pl.when(step >= count)
        def blank():
            out_ref[block(step), :] = jnp.zeros((STEP, width), low)

        @pl.when(step < count)
        def live():
            span = block(step)

            def gather(ref, value):
                if step == 0:
                    ref[...] = value
                else:
                    ref[...] += value

            mixed = cross_mix[:, span].astype(low)
            first = hat_one[:, span] * columns[:, 7:8] + columns[:, 10:11]
            total = first + tn(c_out[...], mixed) + columns[:, 5:6]
            hat_two, scale_two = normalize(total)
            second = hat_two * columns[:, 8:9] + columns[:, 11:12]
            shared = second.astype(low)
            third = second + columns[:, 6:7]
            acts = []
            for part in range(parts):
                chunk = slice(part * width, (part + 1) * width)
                raw = tn(f_in[:, chunk], shared) + columns[:, 15 + part : 16 + part]
                act, slope_part = gelu_parts(raw)
                slope[chunk, :] = slope_part
                act = act.astype(low)
                acts.append(act)
                third = third + tn(f_out[chunk, :], act)
            hat_three, scale_three = normalize(third)
            position = lax.broadcasted_iota(jnp.int32, (1, STEP), 1) + step * STEP
            valid = (position < facts[1]).astype(full)
            result = (hat_three * columns[:, 9:10] + columns[:, 12:13]) * valid
            out_ref[span, :] = result.astype(low).T
            top = cotangent[span, :].T.astype(full) * valid
            lanes[0] += fold_lanes(top * hat_three)
            lanes[1] += fold_lanes(top)
            grad_third = norm_backward(top, hat_three, scale_three, columns[:, 9:10])
            branch = grad_third.astype(low)
            g_rows[4:5] += token_total(branch)
            grad_second = grad_third
            for part in range(parts):
                chunk = slice(part * width, (part + 1) * width)
                back = nn(f_out[chunk, :], branch)
                gather(sum_out.at[chunk, :], nt(acts[part], branch))
                grad_hidden = (back * slope[chunk, :]).astype(low)
                g_rows[part : part + 1] += token_total(grad_hidden)
                gather(sum_in.at[:, chunk], nt(shared, grad_hidden))
                grad_second = grad_second + nn(f_in[:, chunk], grad_hidden)
            lanes[2] += fold_lanes(grad_second * hat_two)
            lanes[3] += fold_lanes(grad_second)
            grad_two = norm_backward(grad_second, hat_two, scale_two, columns[:, 8:9])
            dr_ref[:, span] = grad_two
            branch_two = grad_two.astype(low)
            g_rows[5:6] += token_total(branch_two)
            gather(sum_cross, nt(mixed, branch_two))
            dmix_ref[:, span] = nn(c_out[...], branch_two).astype(low)

    for index in range(4):
        g_rows[6 + index : 7 + index] = lane_total(lanes[index])
    g_in[...] = sum_in[...].astype(g_in.dtype)
    g_out[...] = sum_out[...].astype(g_out.dtype)
    g_cross_out[...] = sum_cross[...].astype(g_cross_out.dtype)


def cross_backward_kernel(
    facts, q_ref, k_ref, v_ref, cross_mix, sums_ref, dmix, dr_two, hat_one, scale_one, memory_t,
    mix, w_out, c_query, columns,
    dkv_ref, dr_ref, dself, g_query, g_kv, g_out, g_rows,
    dq_ref, key_sum, value_sum, mask_ref, sum_query, sum_kv, sum_out, lanes
):
    width, length = q_ref.shape
    others = k_ref.shape[1]
    head_dim = width // HEADS
    score_scale = head_dim ** (-0.5)
    count = blocks_of(facts[1])
    key_count = blocks_of(facts[2])
    position = lax.broadcasted_iota(jnp.int32, (AUG, others), 1)
    mask_ref[...] = jnp.where(position >= facts[2], mask_fill, 0.0).astype(low)
    for wanted in range(1, length // STEP + 1):
        for wanted_keys in range(1, others // STEP + 1):

            @pl.when((count == wanted) & (key_count == wanted_keys))
            def attend():
                attend_backward(
                    q_ref, k_ref, v_ref, cross_mix, sums_ref, dmix,
                    dq_ref, dkv_ref.at[:width], dkv_ref.at[width:], key_sum, value_sum,
                    mask_ref[...], head_dim, wanted, wanted_keys * STEP, score_scale,
                )

    g_rows[...] = jnp.zeros_like(g_rows)
    lanes[...] = jnp.zeros_like(lanes)
    for step in range(others // STEP):

        @pl.when(step < key_count)
        def encode():
            span = block(step)
            made = nt(memory_t[:, span], dkv_ref[:, span])
            g_rows[1:2] += token_total(dkv_ref[width:, span])
            if step == 0:
                sum_kv[...] = made
            else:
                sum_kv[...] += made

        @pl.when(step >= key_count)
        def blank():
            dkv_ref[:, block(step)] = jnp.zeros((2 * width, STEP), low)

    for step in range(length // STEP):

        @pl.when(step < count)
        def first():
            span = block(step)

            def gather(ref, value):
                if step == 0:
                    ref[...] = value
                else:
                    ref[...] += value

            hat = hat_one[:, span]
            shared = (hat * columns[:, 7:8] + columns[:, 10:11]).astype(low)
            grad_query = dq_ref[:, span]
            g_rows[0:1] += token_total(grad_query)
            gather(sum_query, nt(shared, grad_query))
            grad = dr_two[:, span] + nn(c_query[...], grad_query)
            lanes[0] += fold_lanes(grad * hat)
            lanes[1] += fold_lanes(grad)
            grad_one = norm_backward(grad, hat, scale_one[0:1, span], columns[:, 7:8])
            dr_ref[:, span] = grad_one
            branch = grad_one.astype(low)
            g_rows[2:3] += token_total(branch)
            gather(sum_out, nt(mix[:, span].astype(low), branch))
            dself[:, span] = nn(w_out[...], branch).astype(low)

    g_rows[3:4] = lane_total(lanes[0])
    g_rows[4:5] = lane_total(lanes[1])
    g_query[...] = sum_query[...].astype(g_query.dtype)
    g_kv[...] = sum_kv[...].astype(g_kv.dtype)
    g_out[...] = sum_out[...].astype(g_out.dtype)


def self_backward_kernel(
    facts, token_t, q_ref, k_ref, v_ref, mix, sums_ref, dself, columns,
    grads, g_qkv, g_rows, key_sum, value_sum, sum_qkv
):
    width, length = q_ref.shape
    head_dim = width // HEADS
    score_scale = head_dim ** (-0.5)
    count = blocks_of(facts[1])
    embed = jnp.where(facts[0] == 1, columns[:, 14:15], columns[:, 13:14])
    for wanted in range(1, length // STEP + 1):

        @pl.when(count == wanted)
        def attend():
            attend_backward(
                q_ref, k_ref, v_ref, mix, sums_ref, dself,
                grads.at[:width], grads.at[width : 2 * width], grads.at[2 * width :],
                key_sum, value_sum, None, head_dim, wanted, wanted * STEP, score_scale,
            )

    g_rows[...] = jnp.zeros_like(g_rows)
    for step in range(length // STEP):

        @pl.when(step < count)
        def weights():
            span = block(step)
            shared = (token_t[:, span].astype(full) + embed).astype(low)
            made = nt(shared, grads[:, span])
            g_rows[0:1] += token_total(grads[:width, span])
            g_rows[1:2] += token_total(grads[2 * width :, span])
            if step == 0:
                sum_qkv[...] = made
            else:
                sum_qkv[...] += made

    g_qkv[...] = sum_qkv[...].astype(g_qkv.dtype)


def input_grad_kernel(
    facts, grads, dr_one, w_qkv, dkv, c_kv, d_tokens, d_memory, g_rows, lanes
):
    length, width = d_tokens.shape
    others = d_memory.shape[0]
    count = blocks_of(facts[1])
    key_count = blocks_of(facts[2])
    lanes[...] = jnp.zeros_like(lanes)
    for step in range(length // STEP):

        @pl.when(step < count)
        def live():
            span = block(step)
            made = dr_one[:, span] + nn(w_qkv[...], grads[:, span])
            lanes[...] += fold_lanes(made)
            d_tokens[span, :] = made.T

        @pl.when(step >= count)
        def blank():
            d_tokens[block(step), :] = jnp.zeros((STEP, width), full)

    for step in range(others // STEP):

        @pl.when(step < key_count)
        def encode():
            span = block(step)
            d_memory[span, :] = nn(c_kv[...], dkv[:, span]).T

        @pl.when(step >= key_count)
        def hidden():
            d_memory[block(step), :] = jnp.zeros((STEP, width), full)

    total = lane_total(lanes[...])
    g_rows[...] = jnp.zeros_like(g_rows)
    g_rows[0:1] = jnp.where(facts[0] == 1, 0.0, total)
    g_rows[1:2] = jnp.where(facts[0] == 1, total, 0.0)


def call(kernel, outs, scratch, *args):
    specs = [pl.BlockSpec(memory_space=pltpu.SMEM)]
    specs += [pl.BlockSpec(memory_space=pltpu.VMEM)] * (len(args) - 1)
    return pl.pallas_call(
        kernel,
        out_shape=[jax.ShapeDtypeStruct(shape, dtype) for shape, dtype in outs],
        in_specs=specs,
        out_specs=[pl.BlockSpec(memory_space=pltpu.VMEM)] * len(outs),
        scratch_shapes=scratch,
        compiler_params=pltpu.CompilerParams(vmem_limit_bytes=56 * 2**20),
        name=kernel.__name__,
    )(*args)


def layer(facts, tokens, memory, weights, columns, cotangent, grad_type):
    w_qkv, w_out, c_query, c_kv, c_out, f_in, f_out = weights
    length, width = tokens.shape
    others = memory.shape[0]
    hidden = f_in.shape[1]
    head_dim = width // HEADS
    low_t = ((width, length), low)
    full_t = ((width, length), full)
    sums = ((HEADS, length), full)
    peaks = pltpu.SMEM((2,), full)
    vm = pltpu.VMEM
    token_t, q, k, v, mix, sums_one = call(
        self_forward_kernel, [low_t, low_t, low_t, low_t, full_t, sums], [peaks],
        facts, tokens, w_qkv, columns,
    )
    low_m = ((width, others), low)
    hat, scale, memory_t, cq, ck, cv, cross_mix, sums_two = call(
        cross_forward_kernel,
        [full_t, ((8, length), full), low_m, low_t, low_m, low_m, full_t, sums],
        [vm((AUG, others), low), peaks],
        facts, token_t, memory, mix, w_out, c_query, c_kv, columns,
    )
    out, dr_two, dcross, g_in, g_out, g_cross_out, rows_ffn = call(
        ffn_kernel,
        [((length, width), low), full_t, low_t, ((width, hidden), grad_type),
         ((hidden, width), grad_type), ((width, width), grad_type), ((16, width), full)],
        [vm((width, hidden), full), vm((hidden, width), full), vm((width, width), full),
         vm((hidden, STEP), full), vm((4, width, 128), full)],
        facts, hat, cross_mix, cotangent, c_out, f_in, f_out, columns,
    )
    dkv, dr_one, dself, g_cross_query, g_cross_kv, g_self_out, rows_cross = call(
        cross_backward_kernel,
        [((2 * width, others), low), full_t, low_t, ((width, width), grad_type),
         ((width, 2 * width), grad_type), ((width, width), grad_type), ((8, width), full)],
        [vm((width, length), low), vm((head_dim, others), full), vm((head_dim, others), full),
         vm((AUG, others), low), vm((width, width), full), vm((width, 2 * width), full),
         vm((width, width), full), vm((2, width, 128), full)],
        facts, cq, ck, cv, cross_mix, sums_two, dcross, dr_two, hat, scale, memory_t, mix, w_out,
        c_query, columns,
    )
    grads, g_qkv, rows_self = call(
        self_backward_kernel,
        [((3 * width, length), low), ((width, 3 * width), grad_type), ((8, width), full)],
        [vm((head_dim, length), full), vm((head_dim, length), full), vm((width, 3 * width), full)],
        facts, token_t, q, k, v, mix, sums_one, dself, columns,
    )
    d_tokens, d_memory, rows_input = call(
        input_grad_kernel,
        [((length, width), full), ((others, width), full), ((8, width), full)],
        [vm((width, 128), full)],
        facts, grads, dr_one, w_qkv, dkv, c_kv,
    )
    g_vectors = jnp.concatenate(
        [
            rows_self[0:2],
            rows_cross[2:3],
            rows_cross[0:2],
            rows_ffn[5:6],
            rows_ffn[4:5],
            rows_cross[3:4],
            rows_ffn[8:9],
            rows_ffn[6:7],
            rows_cross[4:5],
            rows_ffn[9:10],
            rows_ffn[7:8],
            rows_input[0:2],
            rows_ffn[0:4],
        ],
        0,
    )
    return (
        out, d_tokens, d_memory,
        (g_qkv, g_self_out, g_cross_query, g_cross_kv, g_cross_out, g_in, g_out), g_vectors,
    )


def body(
    tokens, memory, directions, target_len, memory_len, self_qkv, self_out, cross_query, cross_kv,
    cross_out, ffn_in, ffn_out, vectors, cotangent,
):
    width = tokens.shape[2]
    hidden = (vectors.shape[0] * lax.axis_size("dp")) - 15 * width

    def collect(shard, columns):
        return lax.all_gather(shard.reshape(-1, columns), "dp", axis=0, tiled=True)

    weights = (
        collect(self_qkv, 3 * width),
        collect(self_out, width),
        collect(cross_query, width),
        collect(cross_kv, 2 * width),
        collect(cross_out, width),
        collect(ffn_in, hidden),
        collect(ffn_out, width),
    )
    vector_full = lax.all_gather(vectors, "dp", axis=0, tiled=True).astype(full)
    columns = jnp.pad(vector_full.reshape(-1, width).T, ((0, 0), (0, 109)))
    facts = jnp.concatenate([directions, target_len, memory_len])
    out, d_tokens, d_memory, grads, g_vectors = layer(
        facts, tokens[0], memory[0], weights, columns, cotangent[0], full
    )

    def share(grad):
        return lax.psum_scatter(grad, "dp", scatter_dimension=0, tiled=True).reshape(-1)

    return (
        out[None], d_tokens[None], d_memory[None],
        *[share(grad) for grad in grads],
        share(g_vectors.reshape(-1)),
    )


def solution(mesh):
    rows, flat = P("dp", None, None), P("dp")
    return jax.shard_map(
        body,
        mesh=mesh,
        in_specs=(rows, rows) + (flat,) * 11 + (rows,),
        out_specs=(rows,) * 3 + (flat,) * 8,
        check_vma=False,
    )
```

```python
import jax
import jax.numpy as jnp
from jax import lax
from jax.experimental import pallas as pl
from jax.experimental.pallas import tpu as pltpu
from jax.sharding import PartitionSpec as P

HEADS = 8
STEP = 256
PAIR = 2 * STEP
AUG = 16
UNIT = 16
SAFE_SQUARE = 3600.0
mask_fill = -1000000000.0
norm_eps = 1e-05
low = jnp.bfloat16
full = jnp.float32


def contract(left, right, left_dim, right_dim):
    return lax.dot_general(
        left, right, (((left_dim,), (right_dim,)), ((), ())), preferred_element_type=full
    )


def nn(left, right):
    return contract(left, right, 1, 0)


def tn(left, right):
    return contract(left, right, 0, 0)


def nt(left, right):
    return contract(left, right, 1, 1)


def block(index):
    return slice(index * STEP, (index + 1) * STEP)


def blocks_of(length):
    return (length + STEP - 1) // STEP


def split_three(values):
    first = values.astype(low)
    rest = values - first.astype(full)
    second = rest.astype(low)
    third = (rest - second.astype(full)).astype(low)
    return first, second, third


def normalize(values):
    center = jnp.mean(values, axis=0, keepdims=True)
    offsets = values - center
    spread = jnp.mean(offsets * offsets, axis=0, keepdims=True)
    scale = lax.rsqrt(spread + norm_eps)
    return offsets * scale, scale


def norm_backward(grad, hat, scale, gain):
    scaled = grad * gain
    center = jnp.mean(scaled, axis=0, keepdims=True)
    along = jnp.mean(scaled * hat, axis=0, keepdims=True)
    return (scaled - center - hat * along) * scale


def fold_lanes(values):
    return values[:, :128] + values[:, 128:]


def lane_total(partial):
    ones = jnp.ones((8, 128), full)
    return lax.dot_general(
        ones,
        partial,
        (((1,), (1,)), ((), ())),
        precision=lax.Precision.HIGHEST,
        preferred_element_type=full,
    )[0:1]


def token_total(values):
    return nt(jnp.ones((AUG, values.shape[1]), low), values)[0:1]


def head_rows(head, head_dim):
    return pl.ds(pl.multiple_of(head * head_dim, head_dim), head_dim)


def square_peak(values, head_dim):
    squares = jnp.square(values.astype(full))
    count = values.shape[0] // head_dim
    return jnp.max(jnp.sum(squares.reshape(count, head_dim, values.shape[1]), axis=1))


def place_order():
    return [side ^ deep for side in (0, 2, 4, 6) for deep in (0, 8, 16, 24)]


def start_fetch(me, near, far, moves, sem):
    for index, relative in enumerate(place_order()):
        for source, place in ((near, relative), (far, relative ^ 1)):
            owner = jnp.bitwise_xor(me, place)
            for target, first, stop, by_row in moves:
                if by_row:
                    spot = target.at[owner]
                else:
                    spot = target.at[:, pl.ds(pl.multiple_of(owner * UNIT, UNIT), UNIT), :]
                pltpu.make_async_copy(source.at[index, first:stop], spot, sem).start()


def wait_fetch(moves, sem):
    for target, first, stop, by_row in moves:
        pltpu.make_async_copy(target, target, sem).wait()


def start_store(me, near, far, moves, sem):
    for index, relative in enumerate(place_order()):
        for sink, place in ((near, relative), (far, relative ^ 1)):
            owner = jnp.bitwise_xor(me, place)
            for source, first, stop, by_row in moves:
                if by_row:
                    spot = source.at[owner]
                else:
                    spot = source.at[:, pl.ds(pl.multiple_of(owner * UNIT, UNIT), UNIT), :]
                pltpu.make_async_copy(spot, sink.at[index, first:stop], sem).start()


def attend_forward(q_ref, k_ref, v_ref, mix_ref, sums_ref, mask_rows, head_dim, pairs, keys, shifted):
    causal = mask_rows is None

    def one_head(head, carry):
        rows = head_rows(head, head_dim)
        key_head = k_ref[rows, :keys]
        if not causal:
            key_head = jnp.concatenate([key_head, mask_rows[:, :keys]], 0)
        value_head = jnp.concatenate([v_ref[rows, :keys], jnp.ones((AUG, keys), low)], 0)
        for pair in range(pairs):
            columns = slice(pair * PAIR, (pair + 1) * PAIR)
            query = q_ref[rows, columns]
            if causal:
                main = pair * PAIR + STEP
                scores = tn(key_head[:, :main], query)
                late = tn(key_head[:, main : main + STEP], query[:, STEP:])
                key_pos = lax.broadcasted_iota(jnp.int32, (STEP, STEP), 0)
                query_pos = lax.broadcasted_iota(jnp.int32, (STEP, STEP), 1)
                allowed = key_pos <= query_pos
                edge = scores[main - STEP :]
                edge = jnp.concatenate(
                    [jnp.where(allowed, edge[:, :STEP], mask_fill), edge[:, STEP:]], 1
                )
                scores = edge if main == STEP else jnp.concatenate([scores[: main - STEP], edge], 0)
                late = jnp.where(allowed, late, mask_fill)
            else:
                query = jnp.concatenate([query, jnp.ones((AUG, PAIR), low)], 0)
                scores = tn(key_head, query)
            if shifted:
                highest = jnp.max(scores, axis=0, keepdims=True)
                if causal:
                    second = jnp.maximum(
                        highest[:, STEP:], jnp.max(late, axis=0, keepdims=True)
                    )
                    highest = jnp.concatenate([highest[:, :STEP], second], 1)
                    late = late - second
                scores = scores - highest
            powered = jnp.exp(scores).astype(low)
            if causal:
                mixed = nn(value_head[:, :main], powered)
                extra = nn(value_head[:, main : main + STEP], jnp.exp(late).astype(low))
                mixed = jnp.concatenate([mixed[:, :STEP], mixed[:, STEP:] + extra], 1)
            else:
                mixed = nn(value_head, powered)
            total = mixed[head_dim : head_dim + 1]
            mix_ref[rows, columns] = mixed[:head_dim] / total
            log_sum = jnp.log(total)
            sums_ref[pl.ds(head, 1), columns] = log_sum + highest if shifted else log_sum
        return carry

    lax.fori_loop(0, HEADS, one_head, 0)


def attend_backward(
    q_ref, k_ref, v_ref, mix_ref, sums_ref, grad_ref, dq_ref, dk_ref, dv_ref,
    key_sum, value_sum, mask_rows, head_dim, steps, keys, scale
):
    causal = mask_rows is None
    length = steps * STEP

    def one_head(head, carry):
        rows = head_rows(head, head_dim)
        key_head = k_ref[rows, :keys]
        value_head = v_ref[rows, :keys]
        query = q_ref[rows, :length]
        grad = grad_ref[rows, :length]
        inner = jnp.sum(grad.astype(full) * mix_ref[rows, :length], axis=0, keepdims=True)
        one = jnp.ones((1, length), low)
        blank = jnp.zeros((AUG - 4, length), low)
        query_aug = jnp.concatenate(
            [query, *split_three(sums_ref[pl.ds(head, 1), :length]), one, blank], 0
        )
        grad_aug = jnp.concatenate([grad, *split_three(inner), one, blank], 0)
        minus = jnp.full((3, keys), -1.0, low)
        key_blank = jnp.zeros((AUG - 3, keys), low)
        value_aug = jnp.concatenate([value_head, minus, key_blank], 0)
        if causal:
            key_aug = jnp.concatenate([key_head, minus, key_blank], 0)
        else:
            key_aug = jnp.concatenate(
                [key_head, minus, mask_rows[0:1, :keys], key_blank[1:]], 0
            )
        for step in range(steps):
            span = block(step)
            count = (step + 1) * STEP if causal else keys
            scores = tn(query_aug[:, span], key_aug[:, :count])
            chances = jnp.exp(scores)
            if causal:
                query_pos = lax.broadcasted_iota(jnp.int32, (STEP, STEP), 0)
                key_pos = lax.broadcasted_iota(jnp.int32, (STEP, STEP), 1)
                edge = jnp.where(key_pos <= query_pos, chances[:, count - STEP :], 0.0)
                chances = (
                    edge if count == STEP
                    else jnp.concatenate([chances[:, : count - STEP], edge], 1)
                )
            grad_chances = tn(grad_aug[:, span], value_aug[:, :count])
            grad_scores = (chances * grad_chances).astype(low)
            to_value = nn(grad[:, span], chances.astype(low))
            to_key = nn(query[:, span], grad_scores)
            to_query = nt(key_head[:, :count], grad_scores)
            dq_ref[rows, span] = (to_query * scale).astype(low)
            if step == 0:
                value_sum[:, :count] = to_value
                key_sum[:, :count] = to_key
            elif causal:
                old = count - STEP
                value_sum[:, :old] += to_value[:, :old]
                key_sum[:, :old] += to_key[:, :old]
                value_sum[:, old:count] = to_value[:, old:]
                key_sum[:, old:count] = to_key[:, old:]
            else:
                value_sum[:, :count] += to_value
                key_sum[:, :count] += to_key
        dv_ref[rows, :keys] = value_sum[:, :keys].astype(low)
        dk_ref[rows, :keys] = key_sum[:, :keys].astype(low)
        return carry

    lax.fori_loop(0, HEADS, one_head, 0)


def self_forward_kernel(
    facts, tokens, near, far, columns, token_t, q_ref, k_ref, v_ref, mix_ref, sums_ref,
    held, sem, peaks
):
    moves = [(held, 0, 3, False)]
    start_fetch(facts[3], near, far, moves, sem)
    length, width = tokens.shape
    head_dim = width // HEADS
    count = blocks_of(facts[1])
    scale = head_dim ** (-0.5)
    embed = jnp.where(facts[0] == 1, columns[:, 14:15], columns[:, 13:14])
    peaks[0] = 0.0
    peaks[1] = 0.0
    wait_fetch(moves, sem)
    for step in range(length // STEP):

        @pl.when(step < count)
        def project():
            span = block(step)
            flipped = tokens[span, :].T
            token_t[:, span] = flipped
            shared = (flipped.astype(full) + embed).astype(low)
            query = (tn(held[0], shared) + columns[:, 0:1]).astype(low) * scale
            key = tn(held[1], shared).astype(low)
            q_ref[:, span] = query
            k_ref[:, span] = key
            v_ref[:, span] = (tn(held[2], shared) + columns[:, 1:2]).astype(low)
            peaks[0] = jnp.maximum(peaks[0], square_peak(query, head_dim))
            peaks[1] = jnp.maximum(peaks[1], square_peak(key, head_dim))

    safe = peaks[0] * peaks[1] <= SAFE_SQUARE
    pairs = (count + 1) // 2
    for wanted in range(1, length // PAIR + 1):
        for shifted in (False, True):

            @pl.when((pairs == wanted) & (safe != shifted))
            def attend():
                attend_forward(
                    q_ref, k_ref, v_ref, mix_ref, sums_ref, None, head_dim, wanted,
                    wanted * PAIR, shifted,
                )


def cross_forward_kernel(
    facts, token_t, memory, mix, near, far, columns,
    hat_ref, scale_ref, memory_t, q_ref, k_ref, v_ref, cross_mix, sums_ref,
    held, sem, mask_ref, peaks
):
    moves = [(held, 0, 4, False)]
    start_fetch(facts[3], near, far, moves, sem)
    length = token_t.shape[1]
    others, width = memory.shape
    head_dim = width // HEADS
    score_scale = head_dim ** (-0.5)
    count = blocks_of(facts[1])
    key_count = blocks_of(facts[2])
    embed = jnp.where(facts[0] == 1, columns[:, 14:15], columns[:, 13:14])
    peaks[0] = 0.0
    peaks[1] = 0.0
    wait_fetch(moves, sem)
    for step in range(others // STEP):

        @pl.when(step < key_count)
        def encode():
            span = block(step)
            flipped = memory[span, :].T
            memory_t[:, span] = flipped
            key = tn(held[2], flipped).astype(low)
            k_ref[:, span] = key
            v_ref[:, span] = (tn(held[3], flipped) + columns[:, 4:5]).astype(low)
            peaks[1] = jnp.maximum(peaks[1], square_peak(key, head_dim))

    for step in range(length // STEP):

        @pl.when(step < count)
        def first():
            span = block(step)
            started = token_t[:, span].astype(full) + embed
            total = started + tn(held[0], mix[:, span].astype(low)) + columns[:, 2:3]
            hat, scale = normalize(total)
            hat_ref[:, span] = hat
            scale_ref[:, span] = jnp.broadcast_to(scale, (8, STEP))
            shared = (hat * columns[:, 7:8] + columns[:, 10:11]).astype(low)
            query = (tn(held[1], shared) + columns[:, 3:4]).astype(low) * score_scale
            q_ref[:, span] = query
            peaks[0] = jnp.maximum(peaks[0], square_peak(query, head_dim))

    position = lax.broadcasted_iota(jnp.int32, (AUG, others), 1)
    row = lax.broadcasted_iota(jnp.int32, (AUG, others), 0)
    hidden = (position >= facts[2]) & (row == 0)
    mask_ref[...] = jnp.where(hidden, mask_fill, 0.0).astype(low)
    safe = peaks[0] * peaks[1] <= SAFE_SQUARE
    pairs = (count + 1) // 2
    for wanted in range(1, length // PAIR + 1):
        for wanted_keys in range(1, others // STEP + 1):
            for shifted in (False, True):

                @pl.when((pairs == wanted) & (key_count == wanted_keys) & (safe != shifted))
                def attend():
                    attend_forward(
                        q_ref, k_ref, v_ref, cross_mix, sums_ref, mask_ref[...], head_dim,
                        wanted, wanted_keys * STEP, shifted,
                    )


def gelu_parts(values):
    half = 0.5 * (1.0 + lax.erf(values * (0.5**0.5)))
    bell = jnp.exp(-0.5 * values * values) * 0.3989422804014327
    return values * half, half + values * bell


def ffn_kernel(
    facts, hat_one, cross_mix, cotangent, near_two, far_two, near, far, columns,
    out_ref, dr_ref, dmix_ref, keep, send, g_cross_out, g_rows,
    c_out, f_in, f_out, low_in, low_out, sum_in, sum_out, sum_cross, slope, lanes,
    sem, sem_two
):
    moves_two = [(c_out, 4, 5, False)]
    parts = f_in.shape[0]
    moves = [(f_in, 0, parts, False), (f_out, parts, 2 * parts, True)]
    start_fetch(facts[3], near_two, far_two, moves_two, sem_two)
    start_fetch(facts[3], near, far, moves, sem)
    length, width = cotangent.shape
    rows_of = width // parts // UNIT
    count = blocks_of(facts[1])
    g_rows[...] = jnp.zeros_like(g_rows)
    lanes[...] = jnp.zeros_like(lanes)
    wait_fetch(moves_two, sem_two)
    wait_fetch(moves, sem)

    def out_part(part):
        return f_out[part * rows_of : (part + 1) * rows_of].reshape(width, width)

    for step in range(length // STEP):

        @pl.when(step >= count)
        def blank():
            out_ref[block(step), :] = jnp.zeros((STEP, width), low)

        @pl.when(step < count)
        def live():
            span = block(step)

            def gather(ref, value):
                if step == 0:
                    ref[...] = value
                else:
                    ref[...] += value

            mixed = cross_mix[:, span].astype(low)
            first = hat_one[:, span] * columns[:, 7:8] + columns[:, 10:11]
            total = first + tn(c_out[0], mixed) + columns[:, 5:6]
            hat_two, scale_two = normalize(total)
            second = hat_two * columns[:, 8:9] + columns[:, 11:12]
            shared = second.astype(low)
            third = second + columns[:, 6:7]
            acts = []
            for part in range(parts):
                chunk = slice(part * width, (part + 1) * width)
                raw = tn(f_in[part], shared) + columns[:, 15 + part : 16 + part]
                act, slope_part = gelu_parts(raw)
                slope[chunk, :] = slope_part
                act = act.astype(low)
                acts.append(act)
                third = third + tn(out_part(part), act)
            hat_three, scale_three = normalize(third)
            position = lax.broadcasted_iota(jnp.int32, (1, STEP), 1) + step * STEP
            valid = (position < facts[1]).astype(full)
            result = (hat_three * columns[:, 9:10] + columns[:, 12:13]) * valid
            out_ref[span, :] = result.astype(low).T
            top = cotangent[span, :].T.astype(full) * valid
            lanes[0] += fold_lanes(top * hat_three)
            lanes[1] += fold_lanes(top)
            grad_third = norm_backward(top, hat_three, scale_three, columns[:, 9:10])
            branch = grad_third.astype(low)
            g_rows[4:5] += token_total(branch)
            grad_second = grad_third
            for part in range(parts):
                chunk = slice(part * width, (part + 1) * width)
                back = nn(out_part(part), branch)
                gather(sum_out.at[chunk, :], nt(acts[part], branch))
                grad_hidden = (back * slope[chunk, :]).astype(low)
                g_rows[part : part + 1] += token_total(grad_hidden)
                gather(sum_in.at[part], nt(shared, grad_hidden))
                grad_second = grad_second + nn(f_in[part], grad_hidden)
            lanes[2] += fold_lanes(grad_second * hat_two)
            lanes[3] += fold_lanes(grad_second)
            grad_two = norm_backward(grad_second, hat_two, scale_two, columns[:, 8:9])
            dr_ref[:, span] = grad_two
            branch_two = grad_two.astype(low)
            g_rows[5:6] += token_total(branch_two)
            gather(sum_cross, nt(mixed, branch_two))
            dmix_ref[:, span] = nn(c_out[0], branch_two).astype(low)

    for index in range(4):
        g_rows[6 + index : 7 + index] = lane_total(lanes[index])
    g_cross_out[...] = sum_cross[...].astype(low)
    low_in[...] = sum_in[...].astype(low)
    low_out[...] = sum_out[...].astype(low).reshape(low_out.shape)
    stores = [(low_in, 0, parts, False), (low_out, parts, 2 * parts, True)]
    start_store(facts[3], keep, send, stores, sem)
    wait_fetch(stores, sem)


def cross_backward_kernel(
    facts, q_ref, k_ref, v_ref, cross_mix, sums_ref, dmix, dr_two, hat_one, scale_one, memory_t,
    mix, near, far, g_cross_out, columns,
    dkv_ref, dr_ref, dself, keep, send, g_rows,
    held, made_low, dq_ref, key_sum, value_sum, mask_ref, sum_query, sum_kv, sum_out, lanes, sem
):
    moves = [(held, 0, 2, False)]
    start_fetch(facts[3], near, far, moves, sem)
    width, length = q_ref.shape
    others = k_ref.shape[1]
    head_dim = width // HEADS
    score_scale = head_dim ** (-0.5)
    count = blocks_of(facts[1])
    key_count = blocks_of(facts[2])
    position = lax.broadcasted_iota(jnp.int32, (AUG, others), 1)
    mask_ref[...] = jnp.where(position >= facts[2], mask_fill, 0.0).astype(low)
    for wanted in range(1, length // STEP + 1):
        for wanted_keys in range(1, others // STEP + 1):

            @pl.when((count == wanted) & (key_count == wanted_keys))
            def attend():
                attend_backward(
                    q_ref, k_ref, v_ref, cross_mix, sums_ref, dmix,
                    dq_ref, dkv_ref.at[:width], dkv_ref.at[width:], key_sum, value_sum,
                    mask_ref[...], head_dim, wanted, wanted_keys * STEP, score_scale,
                )

    g_rows[...] = jnp.zeros_like(g_rows)
    lanes[...] = jnp.zeros_like(lanes)
    wait_fetch(moves, sem)
    for step in range(others // STEP):

        @pl.when(step < key_count)
        def encode():
            span = block(step)
            made = nt(memory_t[:, span], dkv_ref[:, span])
            g_rows[1:2] += token_total(dkv_ref[width:, span])
            if step == 0:
                sum_kv[...] = made
            else:
                sum_kv[...] += made

        @pl.when(step >= key_count)
        def blank():
            dkv_ref[:, block(step)] = jnp.zeros((2 * width, STEP), low)

    for step in range(length // STEP):

        @pl.when(step < count)
        def first():
            span = block(step)

            def gather(ref, value):
                if step == 0:
                    ref[...] = value
                else:
                    ref[...] += value

            hat = hat_one[:, span]
            shared = (hat * columns[:, 7:8] + columns[:, 10:11]).astype(low)
            grad_query = dq_ref[:, span]
            g_rows[0:1] += token_total(grad_query)
            gather(sum_query, nt(shared, grad_query))
            grad = dr_two[:, span] + nn(held[1], grad_query)
            lanes[0] += fold_lanes(grad * hat)
            lanes[1] += fold_lanes(grad)
            grad_one = norm_backward(grad, hat, scale_one[0:1, span], columns[:, 7:8])
            dr_ref[:, span] = grad_one
            branch = grad_one.astype(low)
            g_rows[2:3] += token_total(branch)
            gather(sum_out, nt(mix[:, span].astype(low), branch))
            dself[:, span] = nn(held[0], branch).astype(low)

    g_rows[3:4] = lane_total(lanes[0])
    g_rows[4:5] = lane_total(lanes[1])
    made_low[0] = sum_out[...].astype(low)
    made_low[1] = sum_query[...].astype(low)
    made_low[2] = sum_kv[:, :width].astype(low)
    made_low[3] = sum_kv[:, width:].astype(low)
    made_low[4] = g_cross_out[...]
    stores = [(made_low, 0, 5, False)]
    start_store(facts[3], keep, send, stores, sem)
    wait_fetch(stores, sem)


def self_backward_kernel(
    facts, token_t, q_ref, k_ref, v_ref, mix, sums_ref, dself, columns,
    grads, keep, send, g_rows, key_sum, value_sum, sum_qkv, made_low, sem
):
    width, length = q_ref.shape
    head_dim = width // HEADS
    score_scale = head_dim ** (-0.5)
    count = blocks_of(facts[1])
    embed = jnp.where(facts[0] == 1, columns[:, 14:15], columns[:, 13:14])
    for wanted in range(1, length // STEP + 1):

        @pl.when(count == wanted)
        def attend():
            attend_backward(
                q_ref, k_ref, v_ref, mix, sums_ref, dself,
                grads.at[:width], grads.at[width : 2 * width], grads.at[2 * width :],
                key_sum, value_sum, None, head_dim, wanted, wanted * STEP, score_scale,
            )

    g_rows[...] = jnp.zeros_like(g_rows)
    for step in range(length // STEP):

        @pl.when(step < count)
        def weights():
            span = block(step)
            shared = (token_t[:, span].astype(full) + embed).astype(low)
            made = nt(shared, grads[:, span])
            g_rows[0:1] += token_total(grads[:width, span])
            g_rows[1:2] += token_total(grads[2 * width :, span])
            if step == 0:
                sum_qkv[...] = made
            else:
                sum_qkv[...] += made

    for part in range(3):
        made_low[part] = sum_qkv[:, part * width : (part + 1) * width].astype(low)
    stores = [(made_low, 0, 3, False)]
    start_store(facts[3], keep, send, stores, sem)
    wait_fetch(stores, sem)


def memory_grad_kernel(facts, dkv, near, far, d_memory, held, sem):
    moves = [(held, 2, 4, False)]
    start_fetch(facts[3], near, far, moves, sem)
    others, width = d_memory.shape
    key_count = blocks_of(facts[2])
    wait_fetch(moves, sem)
    for step in range(others // STEP):

        @pl.when(step < key_count)
        def encode():
            span = block(step)
            made = nn(held[0], dkv[:width, span]) + nn(held[1], dkv[width:, span])
            d_memory[span, :] = made.T

        @pl.when(step >= key_count)
        def hidden():
            d_memory[block(step), :] = jnp.zeros((STEP, width), full)


def token_grad_kernel(facts, grads, dr_one, near, far, d_tokens, g_rows, held, lanes, sem):
    moves = [(held, 0, 3, False)]
    start_fetch(facts[3], near, far, moves, sem)
    length, width = d_tokens.shape
    count = blocks_of(facts[1])
    lanes[...] = jnp.zeros_like(lanes)
    wait_fetch(moves, sem)
    for step in range(length // STEP):

        @pl.when(step < count)
        def live():
            span = block(step)
            made = dr_one[:, span]
            for part in range(3):
                made = made + nn(held[part], grads[part * width : (part + 1) * width, span])
            lanes[...] += fold_lanes(made)
            d_tokens[span, :] = made.T

        @pl.when(step >= count)
        def blank():
            d_tokens[block(step), :] = jnp.zeros((STEP, width), full)

    total = lane_total(lanes[...])
    g_rows[...] = jnp.zeros_like(g_rows)
    g_rows[0:1] = jnp.where(facts[0] == 1, 0.0, total)
    g_rows[1:2] = jnp.where(facts[0] == 1, total, 0.0)


def call(kernel, outs, scratch, cost, *args):
    def place(item):
        return pl.BlockSpec(memory_space=pl.ANY if isinstance(item, list) else pltpu.VMEM)

    specs = [pl.BlockSpec(memory_space=pltpu.SMEM)] + [place(item) for item in args[1:]]
    args = [item[0] if isinstance(item, list) else item for item in args]
    shapes = [item[0] if isinstance(item, list) else item for item in outs]
    return pl.pallas_call(
        kernel,
        out_shape=[jax.ShapeDtypeStruct(shape, dtype) for shape, dtype in shapes],
        in_specs=specs,
        out_specs=[place(item) for item in outs],
        scratch_shapes=scratch,
        compiler_params=pltpu.CompilerParams(vmem_limit_bytes=56 * 2**20),
        cost_estimate=pl.CostEstimate(
            flops=int(cost * 1.0e9), bytes_accessed=4 * 2**20, transcendentals=0
        ),
        name=kernel.__name__,
    )(*args)


SIDES = (0, 2, 4, 6)
DEPTHS = (0, 8, 16, 24)


def swap(values, mask):
    count = lax.axis_size("dp")
    return lax.ppermute(values, "dp", [(spot, spot ^ mask) for spot in range(count)])


def collect(piece):
    held = piece[None]
    held = jnp.concatenate([held] + [swap(held, mask) for mask in DEPTHS[1:]], 0)
    held = jnp.concatenate([held] + [swap(held, mask) for mask in SIDES[1:]], 0)
    return held, swap(held, 1)


def scatter(keep, send):
    wire = keep.dtype
    got = swap(send, 1)
    own, moved = None, []
    for side in range(4):
        span = slice(4 * side, 4 * side + 4)
        total = keep[span].astype(full) + got[span].astype(full)
        if side == 0:
            own = total
        else:
            moved.append(swap(total.astype(wire), SIDES[side]))
    for part in moved:
        own = own + part.astype(full)
    result = own[0]
    for deep in range(1, 4):
        result = result + swap(own[deep].astype(wire), DEPTHS[deep]).astype(full)
    return result


def layer(facts, tokens, memory, one, two, three, columns, cotangent, reduce):
    length, width = tokens.shape
    others = memory.shape[0]
    parts = three[0].shape[1] // 2
    hidden = parts * width
    head_dim = width // HEADS
    low_t, full_t = ((width, length), low), ((width, length), full)
    low_m = ((width, others), low)
    sums = ((HEADS, length), full)
    peaks = pltpu.SMEM((2,), full)
    sem = pltpu.SemaphoreType.DMA
    vm = pltpu.VMEM

    def units(count):
        return vm((count, width, width), low)

    def stored(count):
        return [((16, count, UNIT, width), low)]

    token_t, q, k, v, mix, sums_one = call(
        self_forward_kernel,
        [low_t, low_t, low_t, low_t, full_t, sums],
        [units(3), sem, peaks],
        8.0,
        facts, tokens, [one[0]], [one[1]], columns,
    )
    hat, scale, memory_t, cq, ck, cv, cross_mix, sums_two = call(
        cross_forward_kernel,
        [full_t, ((8, length), full), low_m, low_t, low_m, low_m, full_t, sums],
        [units(4), sem, vm((AUG, others), low), peaks],
        12.0,
        facts, token_t, memory, mix, [two[0]], [two[1]], columns,
    )
    out, dr_two, dcross, keep_three, send_three, g_cross_out, rows_ffn = call(
        ffn_kernel,
        [((length, width), low), full_t, low_t, stored(2 * parts), stored(2 * parts),
         ((width, width), low), ((16, width), full)],
        [units(1), units(parts), vm((32, parts, UNIT, width), low), units(parts),
         vm((32, parts, UNIT, width), low), vm((parts, width, width), full),
         vm((hidden, width), full), vm((width, width), full), vm((hidden, STEP), full),
         vm((4, width, 128), full), sem, sem],
        20.0,
        facts, hat, cross_mix, cotangent, [two[0]], [two[1]], [three[0]], [three[1]], columns,
    )
    g_three = reduce(keep_three, send_three, parts)
    dkv, dr_one, dself, keep_two, send_two, rows_cross = call(
        cross_backward_kernel,
        [((2 * width, others), low), full_t, low_t, stored(5), stored(5), ((8, width), full)],
        [units(2), units(5), vm((width, length), low), vm((head_dim, others), full),
         vm((head_dim, others), full), vm((AUG, others), low), vm((width, width), full),
         vm((width, 2 * width), full), vm((width, width), full), vm((2, width, 128), full), sem],
        20.0,
        facts, cq, ck, cv, cross_mix, sums_two, dcross, dr_two, hat, scale, memory_t, mix,
        [two[0]], [two[1]], g_cross_out, columns,
    )
    g_two = reduce(keep_two, send_two, 0)
    (d_memory,) = call(
        memory_grad_kernel, [((others, width), full)], [units(2), sem], 2.0,
        facts, dkv, [two[0]], [two[1]],
    )
    grads, keep_one, send_one, rows_self = call(
        self_backward_kernel,
        [((3 * width, length), low), stored(3), stored(3), ((8, width), full)],
        [vm((head_dim, length), full), vm((head_dim, length), full),
         vm((width, 3 * width), full), units(3), sem],
        14.0,
        facts, token_t, q, k, v, mix, sums_one, dself, columns,
    )
    g_one = reduce(keep_one, send_one, 0)
    d_tokens, rows_input = call(
        token_grad_kernel,
        [((length, width), full), ((8, width), full)],
        [units(3), vm((width, 128), full), sem],
        3.0,
        facts, grads, dr_one, [one[0]], [one[1]],
    )
    g_vectors = jnp.concatenate(
        [
            rows_self[0:2],
            rows_cross[2:3],
            rows_cross[0:2],
            rows_ffn[5:6],
            rows_ffn[4:5],
            rows_cross[3:4],
            rows_ffn[8:9],
            rows_ffn[6:7],
            rows_cross[4:5],
            rows_ffn[9:10],
            rows_ffn[7:8],
            rows_input[0:2],
            rows_ffn[0:4],
        ],
        0,
    )
    return out, d_tokens, d_memory, g_one, g_two, g_three, g_vectors.reshape(-1)


def body(
    tokens, memory, directions, target_len, memory_len, self_qkv, self_out, cross_query, cross_kv,
    cross_out, ffn_in, ffn_out, vectors, cotangent,
):
    width = tokens.shape[2]
    devices = lax.axis_size("dp")
    rows = self_out.shape[0] // width
    chunks = width // UNIT
    order = place_order()
    order = order + [place ^ 1 for place in order]
    nearby = devices == chunks == len(order)
    me = lax.axis_index("dp") if nearby else jnp.int32(0)

    def stack(flat, by_row=False):
        if by_row:
            return flat.reshape(-1, rows, width)
        return flat.reshape(rows, -1, width).transpose(1, 0, 2)

    one = stack(self_qkv)
    two = jnp.concatenate([stack(w) for w in (self_out, cross_query, cross_kv, cross_out)], 0)
    three = jnp.concatenate([stack(ffn_in), stack(ffn_out, True)], 0)
    parts = three.shape[0] // 2

    def arrange(gathered, by_row):
        group = devices // chunks
        split = gathered.reshape(chunks, group, -1, rows, width)
        if not by_row:
            split = split.transpose(0, 2, 1, 3, 4)
        return split.reshape(chunks, -1, UNIT, width)

    def spread(ordered, by_row):
        group = devices // chunks
        count = ordered.shape[1]
        if by_row:
            return ordered.reshape(devices, count, rows, width)
        split = ordered.reshape(chunks, count, group, rows, width).transpose(0, 2, 1, 3, 4)
        return split.reshape(devices, count, rows, width)

    def share(piece, plain):
        if nearby:
            return collect(piece)
        gathered = lax.all_gather(piece, "dp", axis=0)
        ordered = jnp.concatenate(
            [arrange(gathered[:, :plain], False), arrange(gathered[:, plain:], True)], 1
        ) if plain < piece.shape[0] else arrange(gathered, False)
        placed = jnp.take(ordered, jnp.array(order), axis=0)
        return placed[: chunks // 2], placed[chunks // 2 :]

    def reduce(keep, send, late):
        if nearby:
            return scatter(keep, send)
        back = [order.index(place) for place in range(chunks)]
        ordered = jnp.take(jnp.concatenate([keep, send], 0), jnp.array(back), axis=0)
        plain = ordered.shape[1] - late
        split = spread(ordered[:, :plain], False)
        if late:
            split = jnp.concatenate([split, spread(ordered[:, plain:], True)], 1)
        return lax.psum_scatter(split.astype(full), "dp", scatter_dimension=0, tiled=False)

    if nearby:
        near, far = collect(jnp.pad(vectors.astype(full), (0, -vectors.shape[0] % 128))[None])
        held = jnp.concatenate([near, far], 0)[:, 0, : vectors.shape[0]]
        wanted = jnp.bitwise_xor(me, lax.iota(jnp.int32, chunks))
        choice = (wanted[:, None] == jnp.array(order, jnp.int32)[None, :]).astype(full)
        vector_full = lax.dot(choice, held, precision=lax.Precision.HIGHEST)
    else:
        vector_full = lax.all_gather(vectors, "dp", axis=0, tiled=True).astype(full)
    columns = jnp.pad(vector_full.reshape(-1, width).T, ((0, 0), (0, 109)))
    facts = jnp.concatenate([directions, target_len, memory_len, me[None]])
    out, d_tokens, d_memory, g_one, g_two, g_three, g_vectors = layer(
        facts, tokens[0], memory[0], share(one, one.shape[0]), share(two, two.shape[0]),
        share(three, parts), columns, cotangent[0], reduce,
    )
    if nearby:
        split = lax.dot(
            choice.T, g_vectors.reshape(chunks, -1), precision=lax.Precision.HIGHEST
        )
        split = split.reshape(2, chunks // 2, -1)
        g_vectors = scatter(split[0], split[1])
    else:
        g_vectors = lax.psum_scatter(g_vectors, "dp", scatter_dimension=0, tiled=True)

    def flat(grad):
        return grad.transpose(1, 0, 2).reshape(-1)

    return (
        out[None], d_tokens[None], d_memory[None],
        flat(g_one), flat(g_two[0:1]), flat(g_two[1:2]), flat(g_two[2:4]), flat(g_two[4:5]),
        flat(g_three[:parts]), g_three[parts:].reshape(-1), g_vectors,
    )


def solution(mesh):
    rows, flat = P("dp", None, None), P("dp")
    return jax.shard_map(
        body,
        mesh=mesh,
        in_specs=(rows, rows) + (flat,) * 11 + (rows,),
        out_specs=(rows,) * 3 + (flat,) * 8,
        check_vma=False,
    )
```

```python
import jax
import jax.numpy as jnp
from jax import lax
from jax.experimental import pallas as pl
from jax.experimental.pallas import tpu as pltpu
from jax.sharding import PartitionSpec as P

HEADS = 8
STEP = 256
PAIR = 2 * STEP
AUG = 16
UNIT = 16
SAFE_SQUARE = 3600.0
mask_fill = -1000000000.0
norm_eps = 1e-05
low = jnp.bfloat16
full = jnp.float32


def contract(left, right, left_dim, right_dim):
    return lax.dot_general(
        left, right, (((left_dim,), (right_dim,)), ((), ())), preferred_element_type=full
    )


def nn(left, right):
    return contract(left, right, 1, 0)


def tn(left, right):
    return contract(left, right, 0, 0)


def nt(left, right):
    return contract(left, right, 1, 1)


def block(index):
    return slice(index * STEP, (index + 1) * STEP)


def blocks_of(length):
    return (length + STEP - 1) // STEP


def split_three(values):
    first = values.astype(low)
    rest = values - first.astype(full)
    second = rest.astype(low)
    third = (rest - second.astype(full)).astype(low)
    return first, second, third


def normalize(values):
    center = jnp.mean(values, axis=0, keepdims=True)
    offsets = values - center
    spread = jnp.mean(offsets * offsets, axis=0, keepdims=True)
    scale = lax.rsqrt(spread + norm_eps)
    return offsets * scale, scale


def norm_backward(grad, hat, scale, gain):
    scaled = grad * gain
    center = jnp.mean(scaled, axis=0, keepdims=True)
    along = jnp.mean(scaled * hat, axis=0, keepdims=True)
    return (scaled - center - hat * along) * scale


def fold_lanes(values):
    return values[:, :128] + values[:, 128:]


def lane_total(partial):
    ones = jnp.ones((8, 128), full)
    return lax.dot_general(
        ones,
        partial,
        (((1,), (1,)), ((), ())),
        precision=lax.Precision.HIGHEST,
        preferred_element_type=full,
    )[0:1]


def token_total(values):
    return nt(jnp.ones((AUG, values.shape[1]), low), values)[0:1]


def head_rows(head, head_dim):
    return pl.ds(pl.multiple_of(head * head_dim, head_dim), head_dim)


def square_peak(values, head_dim):
    squares = jnp.square(values.astype(full))
    count = values.shape[0] // head_dim
    return jnp.max(jnp.sum(squares.reshape(count, head_dim, values.shape[1]), axis=1))


def place_order():
    return [side ^ deep for side in (0, 2, 4, 6) for deep in (0, 8, 16, 24)]


def unit_spot(whole, owner, by_row):
    if by_row:
        return whole.at[owner]
    return whole.at[:, pl.ds(pl.multiple_of(owner * UNIT, UNIT), UNIT), :]


def unit_part(buffer, index, first, stop):
    part = buffer.at[index, first * UNIT : stop * UNIT]
    return part.reshape(stop - first, UNIT, buffer.shape[2])


def start_fetch(me, near, far, moves, sem):
    for index, relative in enumerate(place_order()):
        for source, place in ((near, relative), (far, relative ^ 1)):
            owner = jnp.bitwise_xor(me, place)
            for target, first, stop, by_row in moves:
                spot = unit_spot(target, owner, by_row)
                part = unit_part(source, index, first, stop)
                pltpu.make_async_copy(part, spot, sem).start()


def wait_fetch(moves, sem):
    for target, first, stop, by_row in moves:
        pltpu.make_async_copy(target, target, sem).wait()


def start_store(me, near, far, moves, sem):
    for index, relative in enumerate(place_order()):
        for sink, place in ((near, relative), (far, relative ^ 1)):
            owner = jnp.bitwise_xor(me, place)
            for source, first, stop, by_row in moves:
                spot = unit_spot(source, owner, by_row)
                part = unit_part(sink, index, first, stop)
                pltpu.make_async_copy(spot, part, sem).start()


def attend_forward(
    q_ref, k_ref, v_ref, mix_ref, sums_ref, head, mask_rows, pairs, keys, shifted
):
    causal = mask_rows is None
    head_dim = q_ref.shape[0]
    key_head = k_ref[:, :keys]
    if not causal:
        key_head = jnp.concatenate([key_head, mask_rows[:, :keys]], 0)
    value_head = jnp.concatenate([v_ref[:, :keys], jnp.ones((AUG, keys), low)], 0)
    for pair in range(pairs):
        columns = slice(pair * PAIR, (pair + 1) * PAIR)
        query = q_ref[:, columns]
        if causal:
            main = pair * PAIR + STEP
            scores = tn(key_head[:, :main], query)
            late = tn(key_head[:, main : main + STEP], query[:, STEP:])
            key_pos = lax.broadcasted_iota(jnp.int32, (STEP, STEP), 0)
            query_pos = lax.broadcasted_iota(jnp.int32, (STEP, STEP), 1)
            allowed = key_pos <= query_pos
            edge = scores[main - STEP :]
            edge = jnp.concatenate(
                [jnp.where(allowed, edge[:, :STEP], mask_fill), edge[:, STEP:]], 1
            )
            scores = edge if main == STEP else jnp.concatenate([scores[: main - STEP], edge], 0)
            late = jnp.where(allowed, late, mask_fill)
        else:
            query = jnp.concatenate([query, jnp.ones((AUG, PAIR), low)], 0)
            scores = tn(key_head, query)
        if shifted:
            highest = jnp.max(scores, axis=0, keepdims=True)
            if causal:
                second = jnp.maximum(highest[:, STEP:], jnp.max(late, axis=0, keepdims=True))
                highest = jnp.concatenate([highest[:, :STEP], second], 1)
                late = late - second
            scores = scores - highest
        powered = jnp.exp(scores).astype(low)
        if causal:
            mixed = nn(value_head[:, :main], powered)
            extra = nn(value_head[:, main : main + STEP], jnp.exp(late).astype(low))
            mixed = jnp.concatenate([mixed[:, :STEP], mixed[:, STEP:] + extra], 1)
        else:
            mixed = nn(value_head, powered)
        total = mixed[head_dim : head_dim + 1]
        mix_ref[:, columns] = mixed[:head_dim] / total
        log_sum = jnp.log(total)
        sums_ref[pl.ds(head, 1), columns] = log_sum + highest if shifted else log_sum


def attend_backward(
    q_ref, k_ref, v_ref, mix_ref, sums_ref, head, grad_ref, dq_ref, dk_ref, dv_ref,
    key_sum, value_sum, mask_rows, steps, keys
):
    causal = mask_rows is None
    length = steps * STEP
    scale = q_ref.shape[0] ** (-0.5)
    key_head = k_ref[:, :keys]
    value_head = v_ref[:, :keys]
    query = q_ref[:, :length]
    grad = grad_ref[:, :length]
    inner = jnp.sum(grad.astype(full) * mix_ref[:, :length], axis=0, keepdims=True)
    one = jnp.ones((1, length), low)
    blank = jnp.zeros((AUG - 4, length), low)
    query_aug = jnp.concatenate(
        [query, *split_three(sums_ref[pl.ds(head, 1), :length]), one, blank], 0
    )
    grad_aug = jnp.concatenate([grad, *split_three(inner), one, blank], 0)
    minus = jnp.full((3, keys), -1.0, low)
    key_blank = jnp.zeros((AUG - 3, keys), low)
    value_aug = jnp.concatenate([value_head, minus, key_blank], 0)
    if causal:
        key_aug = jnp.concatenate([key_head, minus, key_blank], 0)
    else:
        key_aug = jnp.concatenate([key_head, minus, mask_rows[0:1, :keys], key_blank[1:]], 0)
    for step in range(steps):
        span = block(step)
        count = (step + 1) * STEP if causal else keys
        scores = tn(query_aug[:, span], key_aug[:, :count])
        chances = jnp.exp(scores)
        if causal:
            query_pos = lax.broadcasted_iota(jnp.int32, (STEP, STEP), 0)
            key_pos = lax.broadcasted_iota(jnp.int32, (STEP, STEP), 1)
            edge = jnp.where(key_pos <= query_pos, chances[:, count - STEP :], 0.0)
            chances = (
                edge if count == STEP
                else jnp.concatenate([chances[:, : count - STEP], edge], 1)
            )
        grad_chances = tn(grad_aug[:, span], value_aug[:, :count])
        grad_scores = (chances * grad_chances).astype(low)
        to_value = nn(grad[:, span], chances.astype(low))
        to_key = nn(query[:, span], grad_scores)
        to_query = nt(key_head[:, :count], grad_scores)
        dq_ref[:, span] = (to_query * scale).astype(low)
        if step == 0:
            value_sum[:, :count] = to_value
            key_sum[:, :count] = to_key
        elif causal:
            old = count - STEP
            value_sum[:, :old] += to_value[:, :old]
            key_sum[:, :old] += to_key[:, :old]
            value_sum[:, old:count] = to_value[:, old:]
            key_sum[:, old:count] = to_key[:, old:]
        else:
            value_sum[:, :count] += to_value
            key_sum[:, :count] += to_key
    dv_ref[:, :keys] = value_sum[:, :keys].astype(low)
    dk_ref[:, :keys] = key_sum[:, :keys].astype(low)


def gather_into(first, ref, value):
    if first:
        ref[...] = value
    else:
        ref[...] += value


def project_kernel(
    facts, tokens, near, far, columns, token_t, q_ref, k_ref, v_ref, peaks, held, sem
):
    step = pl.program_id(0)
    width = tokens.shape[1]
    head_dim = width // HEADS
    moves = [(held, 0, 3, False)]

    @pl.when(step == 0)
    def prepare():
        start_fetch(facts[3], near, far, moves, sem)
        peaks[0] = 0.0
        peaks[1] = 0.0
        wait_fetch(moves, sem)

    @pl.when(step < blocks_of(facts[1]))
    def live():
        embed = jnp.where(facts[0] == 1, columns[:, 14:15], columns[:, 13:14])
        flipped = tokens[...].T
        token_t[...] = flipped
        shared = (flipped.astype(full) + embed).astype(low)
        query = (tn(held[0], shared) + columns[:, 0:1]).astype(low) * (head_dim ** (-0.5))
        key = tn(held[1], shared).astype(low)
        q_ref[...] = query
        k_ref[...] = key
        v_ref[...] = (tn(held[2], shared) + columns[:, 1:2]).astype(low)
        peaks[0] = jnp.maximum(peaks[0], square_peak(query, head_dim))
        peaks[1] = jnp.maximum(peaks[1], square_peak(key, head_dim))


def self_forward_kernel(facts, peaks, q_ref, k_ref, v_ref, mix_ref, sums_ref):
    head = pl.program_id(0)
    length = q_ref.shape[1]
    safe = peaks[0] * peaks[1] <= SAFE_SQUARE
    pairs = (blocks_of(facts[1]) + 1) // 2
    for wanted in range(1, length // PAIR + 1):
        for shifted in (False, True):

            @pl.when((pairs == wanted) & (safe != shifted))
            def attend():
                attend_forward(
                    q_ref, k_ref, v_ref, mix_ref, sums_ref, head, None, wanted, wanted * PAIR,
                    shifted,
                )


def encode_kernel(
    facts, token_t, memory, mix, near, far, columns,
    hat_ref, scale_ref, memory_t, q_ref, k_ref, v_ref, peaks, held, sem
):
    step = pl.program_id(0)
    width = memory.shape[1]
    head_dim = width // HEADS
    moves = [(held, 0, 4, False)]

    @pl.when(step == 0)
    def prepare():
        start_fetch(facts[3], near, far, moves, sem)
        peaks[0] = 0.0
        peaks[1] = 0.0
        wait_fetch(moves, sem)

    @pl.when(step < blocks_of(facts[2]))
    def encode():
        flipped = memory[...].T
        memory_t[...] = flipped
        key = tn(held[2], flipped).astype(low)
        k_ref[...] = key
        v_ref[...] = (tn(held[3], flipped) + columns[:, 4:5]).astype(low)
        peaks[1] = jnp.maximum(peaks[1], square_peak(key, head_dim))

    @pl.when(step < blocks_of(facts[1]))
    def first():
        embed = jnp.where(facts[0] == 1, columns[:, 14:15], columns[:, 13:14])
        started = token_t[...].astype(full) + embed
        total = started + tn(held[0], mix[...].astype(low)) + columns[:, 2:3]
        hat, scale = normalize(total)
        hat_ref[...] = hat
        scale_ref[...] = jnp.broadcast_to(scale, scale_ref.shape)
        shared = (hat * columns[:, 7:8] + columns[:, 10:11]).astype(low)
        query = (tn(held[1], shared) + columns[:, 3:4]).astype(low) * (head_dim ** (-0.5))
        q_ref[...] = query
        peaks[0] = jnp.maximum(peaks[0], square_peak(query, head_dim))


def fill_mask(mask_ref, visible):
    position = lax.broadcasted_iota(jnp.int32, mask_ref.shape, 1)
    row = lax.broadcasted_iota(jnp.int32, mask_ref.shape, 0)
    hidden = (position >= visible) & (row == 0)
    mask_ref[...] = jnp.where(hidden, mask_fill, 0.0).astype(low)


def cross_forward_kernel(facts, peaks, q_ref, k_ref, v_ref, mix_ref, sums_ref, mask_ref):
    head = pl.program_id(0)
    length = q_ref.shape[1]
    others = k_ref.shape[1]

    @pl.when(head == 0)
    def prepare():
        fill_mask(mask_ref, facts[2])

    safe = peaks[0] * peaks[1] <= SAFE_SQUARE
    pairs = (blocks_of(facts[1]) + 1) // 2
    key_count = blocks_of(facts[2])
    for wanted in range(1, length // PAIR + 1):
        for wanted_keys in range(1, others // STEP + 1):
            for shifted in (False, True):

                @pl.when((pairs == wanted) & (key_count == wanted_keys) & (safe != shifted))
                def attend():
                    attend_forward(
                        q_ref, k_ref, v_ref, mix_ref, sums_ref, head, mask_ref[...], wanted,
                        wanted_keys * STEP, shifted,
                    )


def gelu_parts(values):
    half = 0.5 * (1.0 + lax.erf(values * (0.5**0.5)))
    bell = jnp.exp(-0.5 * values * values) * 0.3989422804014327
    return values * half, half + values * bell


def ffn_kernel(
    facts, hat_one, cross_mix, cotangent, near_two, far_two, near, far, columns,
    out_ref, dr_ref, dmix_ref, keep, send, g_cross_out, g_rows,
    c_out, f_in, f_out, low_in, low_out, sum_in, sum_out, sum_cross, slope, lanes,
    sem, sem_two
):
    step = pl.program_id(0)
    count = blocks_of(facts[1])
    width = cotangent.shape[1]
    parts = f_in.shape[0]
    rows_of = width // parts // UNIT
    moves_two = [(c_out, 4, 5, False)]
    moves = [(f_in, 0, parts, False), (f_out, parts, 2 * parts, True)]

    def out_part(part):
        return f_out[part * rows_of : (part + 1) * rows_of].reshape(width, width)

    @pl.when(step == 0)
    def prepare():
        start_fetch(facts[3], near_two, far_two, moves_two, sem_two)
        start_fetch(facts[3], near, far, moves, sem)
        g_rows[...] = jnp.zeros_like(g_rows)
        lanes[...] = jnp.zeros_like(lanes)
        wait_fetch(moves_two, sem_two)
        wait_fetch(moves, sem)

    @pl.when(step >= count)
    def blank():
        out_ref[...] = jnp.zeros_like(out_ref)

    def live(initial):
        mixed = cross_mix[...].astype(low)
        first = hat_one[...] * columns[:, 7:8] + columns[:, 10:11]
        total = first + tn(c_out[0], mixed) + columns[:, 5:6]
        hat_two, scale_two = normalize(total)
        second = hat_two * columns[:, 8:9] + columns[:, 11:12]
        shared = second.astype(low)
        third = second + columns[:, 6:7]
        acts = []
        for part in range(parts):
            chunk = slice(part * width, (part + 1) * width)
            raw = tn(f_in[part], shared) + columns[:, 15 + part : 16 + part]
            act, slope_part = gelu_parts(raw)
            slope[chunk, :] = slope_part
            act = act.astype(low)
            acts.append(act)
            third = third + tn(out_part(part), act)
        hat_three, scale_three = normalize(third)
        position = lax.broadcasted_iota(jnp.int32, (1, STEP), 1) + step * STEP
        valid = (position < facts[1]).astype(full)
        result = (hat_three * columns[:, 9:10] + columns[:, 12:13]) * valid
        out_ref[...] = result.astype(low).T
        top = cotangent[...].T.astype(full) * valid
        lanes[0] += fold_lanes(top * hat_three)
        lanes[1] += fold_lanes(top)
        grad_third = norm_backward(top, hat_three, scale_three, columns[:, 9:10])
        branch = grad_third.astype(low)
        g_rows[4:5] += token_total(branch)
        grad_second = grad_third
        for part in range(parts):
            chunk = slice(part * width, (part + 1) * width)
            back = nn(out_part(part), branch)
            gather_into(initial, sum_out.at[chunk, :], nt(acts[part], branch))
            grad_hidden = (back * slope[chunk, :]).astype(low)
            g_rows[part : part + 1] += token_total(grad_hidden)
            gather_into(initial, sum_in.at[part], nt(shared, grad_hidden))
            grad_second = grad_second + nn(f_in[part], grad_hidden)
        lanes[2] += fold_lanes(grad_second * hat_two)
        lanes[3] += fold_lanes(grad_second)
        grad_two = norm_backward(grad_second, hat_two, scale_two, columns[:, 8:9])
        dr_ref[...] = grad_two
        branch_two = grad_two.astype(low)
        g_rows[5:6] += token_total(branch_two)
        gather_into(initial, sum_cross, nt(mixed, branch_two))
        dmix_ref[...] = nn(c_out[0], branch_two).astype(low)

    pl.when(step == 0)(lambda: live(True))
    pl.when((step > 0) & (step < count))(lambda: live(False))

    @pl.when(step == pl.num_programs(0) - 1)
    def close():
        low_in[...] = sum_in[...].astype(low)
        low_out[...] = sum_out[...].astype(low).reshape(low_out.shape)
        stores = [(low_in, 0, parts, False), (low_out, parts, 2 * parts, True)]
        start_store(facts[3], keep, send, stores, sem)
        for index in range(4):
            g_rows[6 + index : 7 + index] = lane_total(lanes[index])
        g_cross_out[...] = sum_cross[...].astype(low)
        wait_fetch(stores, sem)


def cross_backward_kernel(
    facts, q_ref, k_ref, v_ref, cross_mix, sums_ref, dmix, dq_ref, dk_ref, dv_ref,
    key_sum, value_sum, mask_ref
):
    head = pl.program_id(0)
    length = q_ref.shape[1]
    others = k_ref.shape[1]
    count = blocks_of(facts[1])
    key_count = blocks_of(facts[2])

    @pl.when(head == 0)
    def prepare():
        fill_mask(mask_ref, facts[2])

    for wanted in range(1, length // STEP + 1):
        for wanted_keys in range(1, others // STEP + 1):

            @pl.when((count == wanted) & (key_count == wanted_keys))
            def attend():
                attend_backward(
                    q_ref, k_ref, v_ref, cross_mix, sums_ref, head, dmix,
                    dq_ref, dk_ref, dv_ref, key_sum, value_sum, mask_ref[...],
                    wanted, wanted_keys * STEP,
                )


def middle_kernel(
    facts, dq_ref, dk_ref, dv_ref, dr_two, hat_one, scale_one, memory_t, mix, near, far,
    g_cross_out, columns, dr_ref, dself, keep, send, g_rows,
    held, made_low, sum_query, sum_key, sum_value, sum_out, lanes, sem
):
    step = pl.program_id(0)
    moves = [(held, 0, 2, False)]

    @pl.when(step == 0)
    def prepare():
        start_fetch(facts[3], near, far, moves, sem)
        g_rows[...] = jnp.zeros_like(g_rows)
        lanes[...] = jnp.zeros_like(lanes)
        wait_fetch(moves, sem)

    def encode(initial):
        g_rows[1:2] += token_total(dv_ref[...])
        gather_into(initial, sum_key, nt(memory_t[...], dk_ref[...]))
        gather_into(initial, sum_value, nt(memory_t[...], dv_ref[...]))

    def first(initial):
        hat = hat_one[...]
        shared = (hat * columns[:, 7:8] + columns[:, 10:11]).astype(low)
        grad_query = dq_ref[...]
        g_rows[0:1] += token_total(grad_query)
        gather_into(initial, sum_query, nt(shared, grad_query))
        grad = dr_two[...] + nn(held[1], grad_query)
        lanes[0] += fold_lanes(grad * hat)
        lanes[1] += fold_lanes(grad)
        grad_one = norm_backward(grad, hat, scale_one[0:1], columns[:, 7:8])
        dr_ref[...] = grad_one
        branch = grad_one.astype(low)
        g_rows[2:3] += token_total(branch)
        gather_into(initial, sum_out, nt(mix[...].astype(low), branch))
        dself[...] = nn(held[0], branch).astype(low)

    pl.when(step == 0)(lambda: encode(True))
    pl.when((step > 0) & (step < blocks_of(facts[2])))(lambda: encode(False))
    pl.when(step == 0)(lambda: first(True))
    pl.when((step > 0) & (step < blocks_of(facts[1])))(lambda: first(False))

    @pl.when(step == pl.num_programs(0) - 1)
    def close():
        made_low[0] = sum_out[...].astype(low)
        made_low[1] = sum_query[...].astype(low)
        made_low[2] = sum_key[...].astype(low)
        made_low[3] = sum_value[...].astype(low)
        made_low[4] = g_cross_out[...]
        stores = [(made_low, 0, 5, False)]
        start_store(facts[3], keep, send, stores, sem)
        g_rows[3:4] = lane_total(lanes[0])
        g_rows[4:5] = lane_total(lanes[1])
        wait_fetch(stores, sem)


def memory_grad_kernel(facts, dk_ref, dv_ref, near, far, d_memory, held, sem):
    step = pl.program_id(0)
    moves = [(held, 2, 4, False)]

    @pl.when(step == 0)
    def prepare():
        start_fetch(facts[3], near, far, moves, sem)
        wait_fetch(moves, sem)

    @pl.when(step < blocks_of(facts[2]))
    def live():
        d_memory[...] = (nn(held[0], dk_ref[...]) + nn(held[1], dv_ref[...])).T

    @pl.when(step >= blocks_of(facts[2]))
    def blank():
        d_memory[...] = jnp.zeros_like(d_memory)


def self_backward_kernel(
    facts, q_ref, k_ref, v_ref, mix, sums_ref, dself, token_t, columns,
    grads, keep, send, g_rows, key_sum, value_sum, sum_qkv, made_low, sem
):
    head = pl.program_id(0)
    head_dim, length = q_ref.shape
    width = token_t.shape[0]
    count = blocks_of(facts[1])

    def place(part):
        return grads.at[pl.ds(pl.multiple_of(part * width + head * head_dim, head_dim), head_dim)]

    for wanted in range(1, length // STEP + 1):

        @pl.when((head < HEADS) & (count == wanted))
        def attend():
            attend_backward(
                q_ref, k_ref, v_ref, mix, sums_ref, head, dself,
                place(0), place(1), place(2), key_sum, value_sum, None, wanted, wanted * STEP,
            )

    @pl.when(head == HEADS)
    def weights():
        embed = jnp.where(facts[0] == 1, columns[:, 14:15], columns[:, 13:14])
        g_rows[...] = jnp.zeros_like(g_rows)

        def add(step):
            span = block(step)
            shared = (token_t[:, span].astype(full) + embed).astype(low)
            g_rows[0:1] += token_total(grads[:width, span])
            g_rows[1:2] += token_total(grads[2 * width :, span])
            gather_into(step == 0, sum_qkv, nt(shared, grads[:, span]))

        for step in range(length // STEP):
            pl.when(step < count)(lambda: add(step))
        for part in range(3):
            made_low[part] = sum_qkv[:, part * width : (part + 1) * width].astype(low)
        stores = [(made_low, 0, 3, False)]
        start_store(facts[3], keep, send, stores, sem)
        wait_fetch(stores, sem)


def token_grad_kernel(facts, grads, dr_one, near, far, d_tokens, g_rows, held, lanes, sem):
    step = pl.program_id(0)
    width = dr_one.shape[0]
    moves = [(held, 0, 3, False)]

    @pl.when(step == 0)
    def prepare():
        start_fetch(facts[3], near, far, moves, sem)
        lanes[...] = jnp.zeros_like(lanes)
        wait_fetch(moves, sem)

    @pl.when(step < blocks_of(facts[1]))
    def live():
        made = dr_one[...]
        for part in range(3):
            made = made + nn(held[part], grads[part * width : (part + 1) * width, :])
        lanes[...] += fold_lanes(made)
        d_tokens[...] = made.T

    @pl.when(step >= blocks_of(facts[1]))
    def blank():
        d_tokens[...] = jnp.zeros_like(d_tokens)

    @pl.when(step == pl.num_programs(0) - 1)
    def close():
        total = lane_total(lanes[...])
        g_rows[...] = jnp.zeros_like(g_rows)
        g_rows[0:1] = jnp.where(facts[0] == 1, 0.0, total)
        g_rows[1:2] = jnp.where(facts[0] == 1, total, 0.0)


def in_place(shape):
    return pl.BlockSpec(shape, lambda step: (0,) * len(shape))


def columns_block(rows):
    return pl.BlockSpec((rows, STEP), lambda step: (0, step))


def rows_block(columns):
    return pl.BlockSpec((STEP, columns), lambda step: (step, 0))


def head_block(head_dim, columns):
    return pl.BlockSpec((head_dim, columns), lambda step: (jnp.minimum(step, HEADS - 1), 0))


def call(kernel, steps, ins, outs, scratch, cost):
    def spec_of(spec):
        return pl.BlockSpec(memory_space=pl.ANY) if spec is None else spec

    return pl.pallas_call(
        kernel,
        grid=(steps,),
        out_shape=[jax.ShapeDtypeStruct(shape, dtype) for shape, dtype, spec in outs],
        in_specs=[spec_of(spec) for array, spec in ins],
        out_specs=[spec_of(spec) for shape, dtype, spec in outs],
        scratch_shapes=scratch,
        compiler_params=pltpu.CompilerParams(
            vmem_limit_bytes=56 * 2**20, dimension_semantics=("arbitrary",)
        ),
        cost_estimate=pl.CostEstimate(
            flops=int(cost * 1.0e9), bytes_accessed=4 * 2**20, transcendentals=0
        ),
        name=kernel.__name__,
    )(*[array for array, spec in ins])


SIDES = (0, 2, 4, 6)
DEPTHS = (0, 8, 16, 24)


def swap(values, mask):
    count = lax.axis_size("dp")
    return lax.ppermute(values, "dp", [(spot, spot ^ mask) for spot in range(count)])


def spread_along(held, masks):
    return [held] + [swap(held, mask) for mask in masks[1:]]


def after(value, *earlier):
    return lax.optimization_barrier((value, earlier))[0]


class Staged:
    def deep(self, piece, late=0):
        return spread_along(piece[None], DEPTHS)

    def wide(self, held):
        return spread_along(held, SIDES)

    def both(self, held):
        return held, swap(held, 1)

    def join(self, parts):
        return jnp.concatenate(parts, 0)

    def add_core(self, keep, send, late=0):
        return keep, swap(send, 1)

    def sum_core(self, pair):
        keep, got = pair
        sums = [
            keep[4 * side : 4 * side + 4].astype(full) + got[4 * side : 4 * side + 4].astype(full)
            for side in range(4)
        ]
        return [sums[0]] + [part.astype(keep.dtype) for part in sums[1:]]

    def add_wide(self, sums):
        return [sums[0]] + [swap(sums[side], SIDES[side]) for side in range(1, 4)]

    def total(self, parts):
        total = parts[0]
        for part in parts[1:]:
            total = total + part.astype(full)
        return total

    def sum_wide(self, parts):
        wire = parts[1].dtype
        total = self.total(parts)
        return [total[0]] + [total[deep].astype(wire) for deep in range(1, 4)]

    def add_deep(self, sums):
        return [sums[0]] + [swap(sums[deep], DEPTHS[deep]) for deep in range(1, 4)]

    def finish(self, parts):
        return self.total(parts)


class Plain:
    def __init__(self, devices, chunks, rows, width, order):
        self.devices, self.chunks, self.rows, self.width = devices, chunks, rows, width
        self.order = order

    def arrange(self, gathered, by_row):
        group = self.devices // self.chunks
        split = gathered.reshape(self.chunks, group, -1, self.rows, self.width)
        if not by_row:
            split = split.transpose(0, 2, 1, 3, 4)
        return split.reshape(self.chunks, -1, self.width)

    def spread(self, ordered, by_row):
        group = self.devices // self.chunks
        if by_row:
            return ordered.reshape(self.devices, -1, self.width)
        split = ordered.reshape(self.chunks, -1, group, self.rows, self.width)
        return split.transpose(0, 2, 1, 3, 4).reshape(self.devices, -1, self.width)

    def deep(self, piece, late=0):
        gathered = lax.all_gather(piece, "dp", axis=0)
        plain = piece.shape[0] - late
        ordered = self.arrange(gathered[:, :plain], False)
        if late:
            ordered = jnp.concatenate([ordered, self.arrange(gathered[:, plain:], True)], 1)
        return jnp.take(ordered, jnp.array(self.order), axis=0)

    def wide(self, held):
        return held

    def join(self, held):
        return held

    def both(self, held):
        return held[: self.chunks // 2], held[self.chunks // 2 :]

    def add_core(self, keep, send, late=0):
        back = [self.order.index(place) for place in range(self.chunks)]
        ordered = jnp.take(jnp.concatenate([keep, send], 0), jnp.array(back), axis=0)
        plain = ordered.shape[1] - late * UNIT
        split = self.spread(ordered[:, :plain], False)
        if late:
            split = jnp.concatenate([split, self.spread(ordered[:, plain:], True)], 1)
        return lax.psum_scatter(split.astype(full), "dp", scatter_dimension=0, tiled=False)

    def sum_core(self, value):
        return value

    def add_wide(self, value):
        return value

    def sum_wide(self, value):
        return value

    def add_deep(self, value):
        return value

    def finish(self, value):
        return value


def body(
    tokens, memory, directions, target_len, memory_len, self_qkv, self_out, cross_query, cross_kv,
    cross_out, ffn_in, ffn_out, vectors, cotangent,
):
    tokens, memory, cotangent = tokens[0], memory[0], cotangent[0]
    length, width = tokens.shape
    others = memory.shape[0]
    devices = lax.axis_size("dp")
    rows = self_out.shape[0] // width
    chunks = width // UNIT
    parts = ffn_in.shape[0] // (rows * width)
    hidden = parts * width
    head_dim = width // HEADS
    order = place_order()
    order = order + [place ^ 1 for place in order]
    nearby = devices == chunks == len(order)
    me = lax.axis_index("dp") if nearby else jnp.int32(0)
    ways = Staged() if nearby else Plain(devices, chunks, rows, width, order)

    def stack(flat, by_row=False):
        if by_row:
            return flat
        return flat.reshape(rows, -1, width).transpose(1, 0, 2).reshape(-1)

    def piece_of(*flats):
        return jnp.concatenate(flats).reshape(-1, width)

    facts = jnp.concatenate([directions, target_len, memory_len, me[None]])
    one = stack(self_qkv)
    if nearby:
        one = jnp.concatenate([one, jnp.pad(vectors, (0, 8 * width - vectors.shape[0]))])
    one = ways.join(ways.deep(piece_of(one)))
    two = piece_of(*[stack(w) for w in (self_out, cross_query, cross_kv, cross_out)])
    two = ways.deep(after(two, one))
    one = ways.join(ways.wide(one))
    two = ways.join(after(two, one))
    three = piece_of(stack(ffn_in), stack(ffn_out, True))
    three = ways.deep(after(three, two), parts * rows)
    two_sent = ways.wide(two)
    one = ways.both(one)

    if nearby:
        held = jnp.concatenate([part[:, 3 * UNIT, : vectors.shape[0]] for part in one], 0)
        wanted = jnp.bitwise_xor(me, lax.iota(jnp.int32, chunks))
        choice = (wanted[:, None] == jnp.array(order, jnp.int32)[None, :]).astype(full)
        vector_full = lax.dot(choice.astype(low), held, preferred_element_type=full)
    else:
        vector_full = lax.all_gather(vectors, "dp", axis=0, tiled=True).astype(full)
    columns = jnp.pad(vector_full.reshape(-1, width).T, ((0, 0), (0, 109)))

    smem = pl.BlockSpec(memory_space=pltpu.SMEM)
    facts = (facts, smem)
    columns = (columns, in_place((width, 128)))
    sem = pltpu.SemaphoreType.DMA
    vm = pltpu.VMEM
    head_dim = width // HEADS
    steps = length // STEP
    along = columns_block(width)
    by_head, by_head_other = head_block(head_dim, length), head_block(head_dim, others)
    eight = in_place((8, width))

    def units(count):
        return vm((count, width, width), low)

    def stored(count):
        return ((chunks // 2, count * UNIT, width), low, None)

    def remote(pair):
        return [(pair[0], None), (pair[1], None)]

    low_t, full_t = ((width, length), low), ((width, length), full)
    low_m = ((width, others), low)
    sums = ((HEADS, length), full, in_place((HEADS, length)))
    peaks = ((2,), full, smem)

    token_t, q, k, v, peaks_one = call(
        project_kernel, steps,
        [facts, (after(tokens, two), rows_block(width)), *remote(one), columns],
        [(*low_t, along)] * 4 + [peaks],
        [units(3), sem],
        3.0,
    )
    three = ways.join(after(three, peaks_one))
    three_sent = ways.wide(three)
    mix, sums_one = call(
        self_forward_kernel, HEADS,
        [facts, (after(peaks_one, three), smem), (q, by_head), (k, by_head), (v, by_head)],
        [(*full_t, by_head), sums],
        [],
        5.0,
    )
    two = ways.both(ways.join(after(two_sent, sums_one)))
    hat, scale, memory_t, cq, ck, cv, peaks_two = call(
        encode_kernel, steps,
        [facts, (token_t, along), (memory, rows_block(width)), (mix, along), *remote(two),
         columns],
        [(*full_t, along), ((8, length), full, columns_block(8)), (*low_m, along),
         (*low_t, along), (*low_m, along), (*low_m, along), peaks],
        [units(4), sem],
        4.0,
    )
    cross_mix, sums_two = call(
        cross_forward_kernel, HEADS,
        [facts, (peaks_two, smem), (cq, by_head), (ck, by_head_other), (cv, by_head_other)],
        [(*full_t, by_head), sums],
        [vm((AUG, others), low)],
        8.0,
    )
    three = ways.both(ways.join(after(three_sent, sums_two)))
    out, dr_two, dcross, keep_three, send_three, g_cross_out, rows_ffn = call(
        ffn_kernel, steps,
        [facts, (hat, along), (cross_mix, along), (cotangent, rows_block(width)), *remote(two),
         *remote(three), columns],
        [((length, width), low, rows_block(width)), (*full_t, along), (*low_t, along),
         stored(2 * parts), stored(2 * parts),
         ((width, width), low, in_place((width, width))), ((16, width), full, in_place((16, width)))],
        [units(1), units(parts), vm((32, parts, UNIT, width), low), units(parts),
         vm((32, parts, UNIT, width), low), vm((parts, width, width), full),
         vm((hidden, width), full), vm((width, width), full), vm((hidden, STEP), full),
         vm((4, width, 128), full), sem, sem],
        20.0,
    )
    g_three = ways.add_core(keep_three, send_three, parts)
    dcq, dck, dcv = call(
        cross_backward_kernel, HEADS,
        [facts, (cq, by_head), (ck, by_head_other), (cv, by_head_other), (cross_mix, by_head),
         (sums_two, sums[2]), (dcross, by_head)],
        [(*low_t, by_head), (*low_m, by_head_other), (*low_m, by_head_other)],
        [vm((head_dim, others), full), vm((head_dim, others), full), vm((AUG, others), low)],
        16.0,
    )
    g_three = ways.sum_core(after(g_three, dcq))
    dcq = after(dcq, g_three)
    g_three = ways.add_wide(g_three)
    square = vm((width, width), full)
    dr_one, dself, keep_two, send_two, rows_cross = call(
        middle_kernel, steps,
        [facts, (dcq, along), (dck, along), (dcv, along), (dr_two, along), (hat, along),
         (scale, columns_block(8)), (memory_t, along), (mix, along), *remote(two),
         (g_cross_out, in_place((width, width))), columns],
        [(*full_t, along), (*low_t, along), stored(5), stored(5), ((8, width), full, eight)],
        [units(2), units(5), square, square, square, square, vm((2, width, 128), full), sem],
        5.0,
    )
    g_two = ways.add_core(keep_two, send_two)
    (d_memory,) = call(
        memory_grad_kernel, steps,
        [facts, (after(dck, keep_two), along), (dcv, along), *remote(two)],
        [((others, width), full, rows_block(width))],
        [units(2), sem],
        2.0,
    )
    g_two = ways.sum_core(after(g_two, d_memory))
    g_three = ways.sum_wide(after(g_three, d_memory))
    dself = after(dself, g_two, g_three)
    g_two = ways.add_wide(g_two)
    g_three = ways.add_deep(g_three)
    grads, keep_one, send_one, rows_self = call(
        self_backward_kernel, HEADS + 1,
        [facts, (q, by_head), (k, by_head), (v, by_head), (mix, by_head), (sums_one, sums[2]),
         (dself, by_head), (token_t, in_place((width, length))), columns],
        [((3 * width, length), low, in_place((3 * width, length))), stored(3), stored(3),
         ((8, width), full, eight)],
        [vm((head_dim, length), full), vm((head_dim, length), full),
         vm((width, 3 * width), full), units(3), sem],
        12.0,
    )
    g_one = ways.sum_core(ways.add_core(keep_one, send_one))
    grads = after(grads, g_one)
    g_one = ways.add_wide(g_one)
    d_tokens, rows_input = call(
        token_grad_kernel, steps,
        [facts, (grads, columns_block(3 * width)), (dr_one, along), *remote(one)],
        [((length, width), full, rows_block(width)), ((8, width), full, eight)],
        [units(3), vm((width, 128), full), sem],
        3.0,
    )
    g_two = ways.add_deep(ways.sum_wide(after(g_two, rows_input)))
    g_one = ways.add_deep(ways.sum_wide(after(g_one, rows_input)))
    g_three = ways.finish(after(g_three, rows_input))
    g_one = ways.finish(g_one)
    g_two = ways.finish(g_two)
    g_vectors = jnp.concatenate(
        [
            rows_self[0:2],
            rows_cross[2:3],
            rows_cross[0:2],
            rows_ffn[5:6],
            rows_ffn[4:5],
            rows_cross[3:4],
            rows_ffn[8:9],
            rows_ffn[6:7],
            rows_cross[4:5],
            rows_ffn[9:10],
            rows_ffn[7:8],
            rows_input[0:2],
            rows_ffn[0:4],
        ],
        0,
    ).reshape(chunks, -1)
    if nearby:
        split = lax.dot(choice.T, g_vectors, precision=lax.Precision.HIGHEST)
        pair = ways.add_core(split[: chunks // 2], split[chunks // 2 :])
        pair = ways.sum_wide(ways.add_wide(ways.sum_core(pair)))
        g_vectors = ways.finish(ways.add_deep(pair))
    else:
        g_vectors = lax.psum_scatter(g_vectors.reshape(-1), "dp", scatter_dimension=0, tiled=True)

    def flat(grad, first, stop):
        piece = grad[first * rows : stop * rows].reshape(stop - first, rows, width)
        return piece.transpose(1, 0, 2).reshape(-1)

    return (
        out[None], d_tokens[None], d_memory[None],
        flat(g_one, 0, 3), flat(g_two, 0, 1), flat(g_two, 1, 2), flat(g_two, 2, 4),
        flat(g_two, 4, 5), flat(g_three, 0, parts), g_three[parts * rows :].reshape(-1), g_vectors,
    )


def solution(mesh):
    rows, flat = P("dp", None, None), P("dp")
    return jax.shard_map(
        body,
        mesh=mesh,
        in_specs=(rows, rows) + (flat,) * 11 + (rows,),
        out_specs=(rows,) * 3 + (flat,) * 8,
        check_vma=False,
    )
```

```python
import jax
import jax.numpy as jnp
from jax import lax
from jax.experimental import pallas as pl
from jax.experimental.pallas import tpu as pltpu
from jax.sharding import PartitionSpec as P

HEADS = 8
STEP = 256
PAIR = 2 * STEP
AUG = 16
UNIT = 16
SAFE_SQUARE = 3600.0
mask_fill = -1000000000.0
norm_eps = 1e-05
low = jnp.bfloat16
full = jnp.float32


def contract(left, right, left_dim, right_dim):
    return lax.dot_general(
        left, right, (((left_dim,), (right_dim,)), ((), ())), preferred_element_type=full
    )


def nn(left, right):
    return contract(left, right, 1, 0)


def tn(left, right):
    return contract(left, right, 0, 0)


def nt(left, right):
    return contract(left, right, 1, 1)


def block(index):
    return slice(index * STEP, (index + 1) * STEP)


def blocks_of(length):
    return (length + STEP - 1) // STEP


def split_three(values):
    first = values.astype(low)
    rest = values - first.astype(full)
    second = rest.astype(low)
    third = (rest - second.astype(full)).astype(low)
    return first, second, third


def normalize(values):
    center = jnp.mean(values, axis=0, keepdims=True)
    offsets = values - center
    spread = jnp.mean(offsets * offsets, axis=0, keepdims=True)
    scale = lax.rsqrt(spread + norm_eps)
    return offsets * scale, scale


def norm_backward(grad, hat, scale, gain):
    scaled = grad * gain
    center = jnp.mean(scaled, axis=0, keepdims=True)
    along = jnp.mean(scaled * hat, axis=0, keepdims=True)
    return (scaled - center - hat * along) * scale


def fold_lanes(values):
    total = values[:, :128]
    for start in range(128, values.shape[1], 128):
        total = total + values[:, start : start + 128]
    return total


def lane_total(partial):
    ones = jnp.ones((8, 128), full)
    return lax.dot_general(
        ones,
        partial,
        (((1,), (1,)), ((), ())),
        precision=lax.Precision.HIGHEST,
        preferred_element_type=full,
    )[0:1]


def token_total(values):
    return nt(jnp.ones((AUG, values.shape[1]), low), values)[0:1]


def head_rows(head, head_dim):
    return pl.ds(pl.multiple_of(head * head_dim, head_dim), head_dim)


def square_peak(values, head_dim):
    squares = jnp.square(values.astype(full))
    count = values.shape[0] // head_dim
    return jnp.max(jnp.sum(squares.reshape(count, head_dim, values.shape[1]), axis=1))


def place_order():
    return [side ^ deep for side in (0, 2, 4, 6) for deep in (0, 8, 16, 24)]


def unit_spot(whole, owner, by_row):
    if by_row:
        return whole.at[owner]
    return whole.at[:, pl.ds(pl.multiple_of(owner * UNIT, UNIT), UNIT), :]


def unit_part(buffer, index, first, stop):
    part = buffer.at[index, first * UNIT : stop * UNIT]
    return part.reshape(stop - first, UNIT, buffer.shape[2])


def start_fetch(me, near, far, moves, sem):
    for index, relative in enumerate(place_order()):
        for source, place in ((near, relative), (far, relative ^ 1)):
            owner = jnp.bitwise_xor(me, place)
            for target, first, stop, by_row in moves:
                spot = unit_spot(target, owner, by_row)
                part = unit_part(source, index, first, stop)
                pltpu.make_async_copy(part, spot, sem).start()


def wait_fetch(moves, sem):
    for target, first, stop, by_row in moves:
        pltpu.make_async_copy(target, target, sem).wait()


def start_store(me, near, far, moves, sem):
    for index, relative in enumerate(place_order()):
        for sink, place in ((near, relative), (far, relative ^ 1)):
            owner = jnp.bitwise_xor(me, place)
            for source, first, stop, by_row in moves:
                spot = unit_spot(source, owner, by_row)
                part = unit_part(sink, index, first, stop)
                pltpu.make_async_copy(spot, part, sem).start()


def attend_forward(
    q_ref, k_ref, v_ref, mix_ref, sums_ref, head, mask_rows, pairs, keys, shifted
):
    causal = mask_rows is None
    head_dim = q_ref.shape[0]
    key_head = k_ref[:, :keys]
    if not causal:
        key_head = jnp.concatenate([key_head, mask_rows[:, :keys]], 0)
    value_head = jnp.concatenate([v_ref[:, :keys], jnp.ones((AUG, keys), low)], 0)
    for pair in range(pairs):
        columns = slice(pair * PAIR, (pair + 1) * PAIR)
        query = q_ref[:, columns]
        if causal:
            main = pair * PAIR + STEP
            scores = tn(key_head[:, :main], query)
            late = tn(key_head[:, main : main + STEP], query[:, STEP:])
            key_pos = lax.broadcasted_iota(jnp.int32, (STEP, STEP), 0)
            query_pos = lax.broadcasted_iota(jnp.int32, (STEP, STEP), 1)
            allowed = key_pos <= query_pos
            edge = scores[main - STEP :]
            edge = jnp.concatenate(
                [jnp.where(allowed, edge[:, :STEP], mask_fill), edge[:, STEP:]], 1
            )
            scores = edge if main == STEP else jnp.concatenate([scores[: main - STEP], edge], 0)
            late = jnp.where(allowed, late, mask_fill)
        else:
            query = jnp.concatenate([query, jnp.ones((AUG, PAIR), low)], 0)
            scores = tn(key_head, query)
        if shifted:
            highest = jnp.max(scores, axis=0, keepdims=True)
            if causal:
                second = jnp.maximum(highest[:, STEP:], jnp.max(late, axis=0, keepdims=True))
                highest = jnp.concatenate([highest[:, :STEP], second], 1)
                late = late - second
            scores = scores - highest
        powered = jnp.exp(scores).astype(low)
        if causal:
            mixed = nn(value_head[:, :main], powered)
            extra = nn(value_head[:, main : main + STEP], jnp.exp(late).astype(low))
            mixed = jnp.concatenate([mixed[:, :STEP], mixed[:, STEP:] + extra], 1)
        else:
            mixed = nn(value_head, powered)
        total = mixed[head_dim : head_dim + 1]
        mix_ref[:, columns] = mixed[:head_dim] / total
        log_sum = jnp.log(total)
        sums_ref[pl.ds(head, 1), columns] = log_sum + highest if shifted else log_sum


def attend_backward(
    q_ref, k_ref, v_ref, mix_ref, sums_ref, head, grad_ref, dq_ref, dk_ref, dv_ref,
    key_sum, value_sum, mask_rows, steps, keys
):
    causal = mask_rows is None
    length = steps * STEP
    scale = q_ref.shape[0] ** (-0.5)
    key_head = k_ref[:, :keys]
    value_head = v_ref[:, :keys]
    query = q_ref[:, :length]
    grad = grad_ref[:, :length]
    inner = jnp.sum(grad.astype(full) * mix_ref[:, :length], axis=0, keepdims=True)
    one = jnp.ones((1, length), low)
    blank = jnp.zeros((AUG - 4, length), low)
    query_aug = jnp.concatenate(
        [query, *split_three(sums_ref[pl.ds(head, 1), :length]), one, blank], 0
    )
    grad_aug = jnp.concatenate([grad, *split_three(inner), one, blank], 0)
    minus = jnp.full((3, keys), -1.0, low)
    key_blank = jnp.zeros((AUG - 3, keys), low)
    value_aug = jnp.concatenate([value_head, minus, key_blank], 0)
    if causal:
        key_aug = jnp.concatenate([key_head, minus, key_blank], 0)
    else:
        key_aug = jnp.concatenate([key_head, minus, mask_rows[0:1, :keys], key_blank[1:]], 0)
    for step in range(steps):
        span = block(step)
        count = (step + 1) * STEP if causal else keys
        scores = tn(query_aug[:, span], key_aug[:, :count])
        chances = jnp.exp(scores)
        if causal:
            query_pos = lax.broadcasted_iota(jnp.int32, (STEP, STEP), 0)
            key_pos = lax.broadcasted_iota(jnp.int32, (STEP, STEP), 1)
            edge = jnp.where(key_pos <= query_pos, chances[:, count - STEP :], 0.0)
            chances = (
                edge if count == STEP
                else jnp.concatenate([chances[:, : count - STEP], edge], 1)
            )
        grad_chances = tn(grad_aug[:, span], value_aug[:, :count])
        grad_scores = (chances * grad_chances).astype(low)
        to_value = nn(grad[:, span], chances.astype(low))
        to_key = nn(query[:, span], grad_scores)
        to_query = nt(key_head[:, :count], grad_scores)
        dq_ref[:, span] = (to_query * scale).astype(low)
        if step == 0:
            value_sum[:, :count] = to_value
            key_sum[:, :count] = to_key
        elif causal:
            old = count - STEP
            value_sum[:, :old] += to_value[:, :old]
            key_sum[:, :old] += to_key[:, :old]
            value_sum[:, old:count] = to_value[:, old:]
            key_sum[:, old:count] = to_key[:, old:]
        else:
            value_sum[:, :count] += to_value
            key_sum[:, :count] += to_key
    dv_ref[:, :keys] = value_sum[:, :keys].astype(low)
    dk_ref[:, :keys] = key_sum[:, :keys].astype(low)


def gather_into(first, ref, value):
    if first:
        ref[...] = value
    else:
        ref[...] += value


def project_kernel(
    facts, tokens, near, far, columns, token_t, q_ref, k_ref, v_ref, peaks, held, sem
):
    step = pl.program_id(0)
    width = tokens.shape[1]
    head_dim = width // HEADS
    moves = [(held, 0, 3, False)]

    @pl.when(step == 0)
    def prepare():
        start_fetch(facts[3], near, far, moves, sem)
        peaks[0] = 0.0
        peaks[1] = 0.0
        wait_fetch(moves, sem)

    @pl.when(step < blocks_of(facts[1]))
    def live():
        embed = jnp.where(facts[0] == 1, columns[:, 14:15], columns[:, 13:14])
        flipped = tokens[...].T
        token_t[...] = flipped
        shared = (flipped.astype(full) + embed).astype(low)
        query = (tn(held[0], shared) + columns[:, 0:1]).astype(low) * (head_dim ** (-0.5))
        key = tn(held[1], shared).astype(low)
        q_ref[...] = query
        k_ref[...] = key
        v_ref[...] = (tn(held[2], shared) + columns[:, 1:2]).astype(low)
        peaks[0] = jnp.maximum(peaks[0], square_peak(query, head_dim))
        peaks[1] = jnp.maximum(peaks[1], square_peak(key, head_dim))


def self_forward_kernel(facts, peaks, q_ref, k_ref, v_ref, mix_ref, sums_ref):
    head = pl.program_id(0)
    length = q_ref.shape[1]
    safe = peaks[0] * peaks[1] <= SAFE_SQUARE
    pairs = (blocks_of(facts[1]) + 1) // 2
    for wanted in range(1, length // PAIR + 1):
        for shifted in (False, True):

            @pl.when((pairs == wanted) & (safe != shifted))
            def attend():
                attend_forward(
                    q_ref, k_ref, v_ref, mix_ref, sums_ref, head, None, wanted, wanted * PAIR,
                    shifted,
                )


def encode_kernel(
    facts, token_t, memory, mix, near, far, columns,
    hat_ref, scale_ref, memory_t, q_ref, k_ref, v_ref, peaks, held, sem
):
    step = pl.program_id(0)
    width = memory.shape[1]
    head_dim = width // HEADS
    moves = [(held, 0, 4, False)]

    @pl.when(step == 0)
    def prepare():
        start_fetch(facts[3], near, far, moves, sem)
        peaks[0] = 0.0
        peaks[1] = 0.0
        wait_fetch(moves, sem)

    @pl.when(step < blocks_of(facts[2]))
    def encode():
        flipped = memory[...].T
        memory_t[...] = flipped
        key = tn(held[2], flipped).astype(low)
        k_ref[...] = key
        v_ref[...] = (tn(held[3], flipped) + columns[:, 4:5]).astype(low)
        peaks[1] = jnp.maximum(peaks[1], square_peak(key, head_dim))

    @pl.when(step < blocks_of(facts[1]))
    def first():
        embed = jnp.where(facts[0] == 1, columns[:, 14:15], columns[:, 13:14])
        started = token_t[...].astype(full) + embed
        total = started + tn(held[0], mix[...].astype(low)) + columns[:, 2:3]
        hat, scale = normalize(total)
        hat_ref[...] = hat
        scale_ref[...] = jnp.broadcast_to(scale, scale_ref.shape)
        shared = (hat * columns[:, 7:8] + columns[:, 10:11]).astype(low)
        query = (tn(held[1], shared) + columns[:, 3:4]).astype(low) * (head_dim ** (-0.5))
        q_ref[...] = query
        peaks[0] = jnp.maximum(peaks[0], square_peak(query, head_dim))


def fill_mask(mask_ref, visible):
    position = lax.broadcasted_iota(jnp.int32, mask_ref.shape, 1)
    row = lax.broadcasted_iota(jnp.int32, mask_ref.shape, 0)
    hidden = (position >= visible) & (row == 0)
    mask_ref[...] = jnp.where(hidden, mask_fill, 0.0).astype(low)


def cross_forward_kernel(facts, peaks, q_ref, k_ref, v_ref, mix_ref, sums_ref, mask_ref):
    head = pl.program_id(0)
    length = q_ref.shape[1]
    others = k_ref.shape[1]

    @pl.when(head == 0)
    def prepare():
        fill_mask(mask_ref, facts[2])

    safe = peaks[0] * peaks[1] <= SAFE_SQUARE
    pairs = (blocks_of(facts[1]) + 1) // 2
    key_count = blocks_of(facts[2])
    for wanted in range(1, length // PAIR + 1):
        for wanted_keys in range(1, others // STEP + 1):
            for shifted in (False, True):

                @pl.when((pairs == wanted) & (key_count == wanted_keys) & (safe != shifted))
                def attend():
                    attend_forward(
                        q_ref, k_ref, v_ref, mix_ref, sums_ref, head, mask_ref[...], wanted,
                        wanted_keys * STEP, shifted,
                    )


def gelu_parts(values):
    half = 0.5 * (1.0 + lax.erf(values * (0.5**0.5)))
    bell = jnp.exp(-0.5 * values * values) * 0.3989422804014327
    return values * half, half + values * bell


def ffn_kernel(
    facts, hat_one, cross_mix, cotangent, near_two, far_two, near, far, columns,
    out_ref, dr_ref, dmix_ref, keep, send, g_cross_out, g_rows,
    c_out, f_in, f_out, low_in, low_out, slope, acts, top_ref, result_ref, sems
):
    length, width = top_ref.shape
    parts = f_in.shape[0]
    rows_of = width // parts // UNIT
    moves_two = [(c_out, 4, 5, False)]
    moves_in = [(f_in, 0, parts, False)]
    moves_out = [(f_out, parts, 2 * parts, True)]
    stores_in = [(low_in, 0, parts, False)]
    stores_out = [(low_out, parts, 2 * parts, True)]
    fetch_top = pltpu.make_async_copy(cotangent, top_ref, sems.at[3])
    store_result = pltpu.make_async_copy(result_ref, out_ref, sems.at[4])
    start_fetch(facts[3], near_two, far_two, moves_two, sems.at[0])
    start_fetch(facts[3], near, far, moves_in, sems.at[1])
    start_fetch(facts[3], near, far, moves_out, sems.at[2])
    fetch_top.start()
    g_rows[...] = jnp.zeros_like(g_rows)

    def out_part(part):
        return f_out[part * rows_of : (part + 1) * rows_of].reshape(width, width)

    def live(count):
        span = slice(0, count)
        wait_fetch(moves_two, sems.at[0])
        position = lax.broadcasted_iota(jnp.int32, (1, count), 1)
        alive = position < facts[1]
        valid = alive.astype(full)
        mixed = jnp.where(alive, cross_mix[:, span], 0.0).astype(low)
        hat = jnp.where(alive, hat_one[:, span], 0.0)
        first = hat * columns[:, 7:8] + columns[:, 10:11]
        total = first + tn(c_out[0], mixed) + columns[:, 5:6]
        hat_two, scale_two = normalize(total)
        second = hat_two * columns[:, 8:9] + columns[:, 11:12]
        shared = second.astype(low)
        third = second + columns[:, 6:7]
        wait_fetch(moves_in, sems.at[1])
        wait_fetch(moves_out, sems.at[2])
        for part in range(parts):
            chunk = slice(part * width, (part + 1) * width)
            raw = tn(f_in[part], shared) + columns[:, 15 + part : 16 + part]
            act, slope_part = gelu_parts(raw)
            slope[chunk, span] = slope_part
            acts[chunk, span] = act.astype(low)
            third = third + tn(out_part(part), acts[chunk, span])
        hat_three, scale_three = normalize(third)
        result = (hat_three * columns[:, 9:10] + columns[:, 12:13]) * valid
        result_ref[span, :] = result.astype(low).T
        if count < length:
            result_ref[count:, :] = jnp.zeros((length - count, width), low)
        store_result.start()
        fetch_top.wait()
        top = top_ref[span, :].T.astype(full) * valid
        g_rows[7:8] = lane_total(fold_lanes(top * hat_three))
        g_rows[9:10] = lane_total(fold_lanes(top))
        grad_third = norm_backward(top, hat_three, scale_three, columns[:, 9:10])
        branch = grad_third.astype(low)
        g_rows[4:5] = token_total(branch)
        grad_second = grad_third
        for part in range(parts):
            chunk = slice(part * width, (part + 1) * width)
            back = nn(out_part(part), branch)
            rows = slice(part * rows_of, (part + 1) * rows_of)
            low_out[rows] = nt(acts[chunk, span], branch).astype(low).reshape(
                rows_of, parts, UNIT, width
            )
            acts[chunk, span] = (back * slope[chunk, span]).astype(low)
        start_store(facts[3], keep, send, stores_out, sems.at[2])
        for part in range(parts):
            chunk = slice(part * width, (part + 1) * width)
            grad_hidden = acts[chunk, span]
            g_rows[part : part + 1] = token_total(grad_hidden)
            low_in[part] = nt(shared, grad_hidden).astype(low)
            grad_second = grad_second + nn(f_in[part], grad_hidden)
        start_store(facts[3], keep, send, stores_in, sems.at[1])
        g_rows[6:7] = lane_total(fold_lanes(grad_second * hat_two))
        g_rows[8:9] = lane_total(fold_lanes(grad_second))
        grad_two = norm_backward(grad_second, hat_two, scale_two, columns[:, 8:9])
        dr_ref[:, span] = grad_two
        branch_two = grad_two.astype(low)
        g_rows[5:6] = token_total(branch_two)
        g_cross_out[...] = nt(mixed, branch_two).astype(low)
        dmix_ref[:, span] = nn(c_out[0], branch_two).astype(low)

    live(length)
    wait_fetch(stores_out, sems.at[2])
    wait_fetch(stores_in, sems.at[1])
    store_result.wait()


def cross_backward_kernel(
    facts, q_ref, k_ref, v_ref, cross_mix, sums_ref, dmix, dq_ref, dk_ref, dv_ref,
    key_sum, value_sum, mask_ref
):
    head = pl.program_id(0)
    length = q_ref.shape[1]
    others = k_ref.shape[1]
    count = blocks_of(facts[1])
    key_count = blocks_of(facts[2])

    @pl.when(head == 0)
    def prepare():
        fill_mask(mask_ref, facts[2])

    for wanted in range(1, length // STEP + 1):
        for wanted_keys in range(1, others // STEP + 1):

            @pl.when((count == wanted) & (key_count == wanted_keys))
            def attend():
                attend_backward(
                    q_ref, k_ref, v_ref, cross_mix, sums_ref, head, dmix,
                    dq_ref, dk_ref, dv_ref, key_sum, value_sum, mask_ref[...],
                    wanted, wanted_keys * STEP,
                )


def middle_kernel(
    facts, dq_ref, dk_ref, dv_ref, dr_two, hat_one, scale_one, memory_t, mix, near, far,
    g_cross_out, columns, dr_ref, dself, keep, send, g_rows,
    held, made_low, sum_query, sum_key, sum_value, sum_out, lanes, sem
):
    step = pl.program_id(0)
    moves = [(held, 0, 2, False)]

    @pl.when(step == 0)
    def prepare():
        start_fetch(facts[3], near, far, moves, sem)
        g_rows[...] = jnp.zeros_like(g_rows)
        lanes[...] = jnp.zeros_like(lanes)
        wait_fetch(moves, sem)

    def encode(initial):
        g_rows[1:2] += token_total(dv_ref[...])
        gather_into(initial, sum_key, nt(memory_t[...], dk_ref[...]))
        gather_into(initial, sum_value, nt(memory_t[...], dv_ref[...]))

    def first(initial):
        hat = hat_one[...]
        shared = (hat * columns[:, 7:8] + columns[:, 10:11]).astype(low)
        grad_query = dq_ref[...]
        g_rows[0:1] += token_total(grad_query)
        gather_into(initial, sum_query, nt(shared, grad_query))
        grad = dr_two[...] + nn(held[1], grad_query)
        lanes[0] += fold_lanes(grad * hat)
        lanes[1] += fold_lanes(grad)
        grad_one = norm_backward(grad, hat, scale_one[0:1], columns[:, 7:8])
        dr_ref[...] = grad_one
        lanes[2] += fold_lanes(grad_one)
        branch = grad_one.astype(low)
        g_rows[2:3] += token_total(branch)
        gather_into(initial, sum_out, nt(mix[...].astype(low), branch))
        dself[...] = nn(held[0], branch).astype(low)

    pl.when(step == 0)(lambda: encode(True))
    pl.when((step > 0) & (step < blocks_of(facts[2])))(lambda: encode(False))
    pl.when(step == 0)(lambda: first(True))
    pl.when((step > 0) & (step < blocks_of(facts[1])))(lambda: first(False))

    @pl.when(step == pl.num_programs(0) - 1)
    def close():
        made_low[0] = sum_out[...].astype(low)
        made_low[1] = sum_query[...].astype(low)
        made_low[2] = sum_key[...].astype(low)
        made_low[3] = sum_value[...].astype(low)
        made_low[4] = g_cross_out[...]
        stores = [(made_low, 0, 5, False)]
        start_store(facts[3], keep, send, stores, sem)
        g_rows[3:4] = lane_total(lanes[0])
        g_rows[4:5] = lane_total(lanes[1])
        g_rows[5:6] = lane_total(lanes[2])
        wait_fetch(stores, sem)


def memory_grad_kernel(facts, dk_ref, dv_ref, near, far, d_memory, held, sem):
    step = pl.program_id(0)
    moves = [(held, 2, 4, False)]

    @pl.when(step == 0)
    def prepare():
        start_fetch(facts[3], near, far, moves, sem)
        wait_fetch(moves, sem)

    @pl.when(step < blocks_of(facts[2]))
    def live():
        d_memory[...] = (nn(held[0], dk_ref[...]) + nn(held[1], dv_ref[...])).T

    @pl.when(step >= blocks_of(facts[2]))
    def blank():
        d_memory[...] = jnp.zeros_like(d_memory)


def self_backward_kernel(
    facts, q_ref, k_ref, v_ref, mix, sums_ref, dself, dq_ref, dk_ref, dv_ref, key_sum, value_sum
):
    head = pl.program_id(0)
    count = blocks_of(facts[1])
    for wanted in range(1, q_ref.shape[1] // STEP + 1):

        @pl.when(count == wanted)
        def attend():
            attend_backward(
                q_ref, k_ref, v_ref, mix, sums_ref, head, dself, dq_ref, dk_ref, dv_ref,
                key_sum, value_sum, None, wanted, wanted * STEP,
            )


def self_finish_kernel(
    facts, q_ref, k_ref, v_ref, mix, sums_ref, dself, token_t, dq_one, dk_one, dv_one,
    rows_ffn, rows_cross, near, far, columns,
    grads, keep, send, g_rows,
    key_sum, value_sum, sum_qkv, made_low, made_rows, held, sem, sem_out
):
    step_at = pl.program_id(0)
    last = pl.num_programs(0) - 1
    head = step_at + HEADS // 2
    head_dim, length = q_ref.shape
    width = token_t.shape[0]
    half = width // 2
    count = blocks_of(facts[1])
    moves = [(held, 0, 3, False)]

    @pl.when(step_at == 0)
    def prepare():
        start_fetch(facts[3], near, far, moves, sem)

    def place(part):
        start = pl.multiple_of(part * half + step_at * head_dim, head_dim)
        return grads.at[pl.ds(start, head_dim)]

    for wanted in range(1, length // STEP + 1):

        @pl.when((step_at < last) & (count == wanted))
        def attend():
            attend_backward(
                q_ref, k_ref, v_ref, mix, sums_ref, head, dself,
                place(0), place(1), place(2), key_sum, value_sum, None, wanted, wanted * STEP,
            )

    @pl.when(step_at == last)
    def weights():
        embed = jnp.where(facts[0] == 1, columns[:, 14:15], columns[:, 13:14])
        g_rows[...] = jnp.zeros_like(g_rows)

        def add(step):
            span = block(step)
            shared = (token_t[:, span].astype(full) + embed).astype(low)
            for part, early in enumerate((dq_one, dk_one, dv_one)):
                left = early[:, span]
                right = grads[part * half : (part + 1) * half, span]
                g_rows[part : part + 1, :half] += token_total(left)
                g_rows[part : part + 1, half:] += token_total(right)
                gather_into(step == 0, sum_qkv.at[part, :, :half], nt(shared, left))
                gather_into(step == 0, sum_qkv.at[part, :, half:], nt(shared, right))

        for step in range(length // STEP):
            pl.when(step < count)(lambda: add(step))
        made_low[...] = sum_qkv[...].astype(low)
        stores = [(made_low, 0, 3, False)]
        start_store(facts[3], keep, send, stores, sem_out)
        wait_fetch(moves, sem)
        total = rows_cross[5:6]
        for part in range(3):
            pieces = jnp.concatenate(
                [*split_three(g_rows[part : part + 1]), jnp.zeros((AUG - 3, width), low)], 0
            )
            total = total + jnp.sum(nt(pieces, held[part]), axis=0, keepdims=True)
        g_rows[3:4] = jnp.where(facts[0] == 1, 0.0, total)
        g_rows[4:5] = jnp.where(facts[0] == 1, total, 0.0)
        picks = [
            g_rows[0:1], g_rows[2:3], rows_cross[2:3], rows_cross[0:1], rows_cross[1:2],
            rows_ffn[5:6], rows_ffn[4:5], rows_cross[3:4], rows_ffn[6:7], rows_ffn[7:8],
            rows_cross[4:5], rows_ffn[8:9], rows_ffn[9:10], g_rows[3:4], g_rows[4:5],
            *[rows_ffn[part : part + 1] for part in range(4)],
        ]
        share = len(picks) * width // made_rows.shape[0]
        for owner in range(made_rows.shape[0]):
            row, start = divmod(owner * share, width)
            stop = min(start + share, width)
            pieces = [picks[row][:, start:stop]]
            if stop - start < share:
                pieces.append(picks[row + 1][:, : share - (stop - start)])
            pieces.append(jnp.zeros((1, width - share), full))
            line = jnp.concatenate(pieces, 1)
            made_rows[owner, 0] = jnp.concatenate(
                [line, jnp.zeros((UNIT - 1, width), full)], 0
            ).astype(low)
        more = [(made_rows, 3, 4, True)]
        start_store(facts[3], keep, send, more, sem)
        wait_fetch(stores, sem_out)
        wait_fetch(more, sem)


def token_grad_kernel(
    facts, dq_one, dk_one, dv_one, grads, dr_one, near, far, d_tokens, held, sem
):
    step = pl.program_id(0)
    width = dr_one.shape[0]
    moves = [(held, 0, 3, False)]

    @pl.when(step == 0)
    def prepare():
        start_fetch(facts[3], near, far, moves, sem)
        wait_fetch(moves, sem)

    @pl.when(step < blocks_of(facts[1]))
    def live():
        made = dr_one[...]
        half = width // 2
        for part, early in enumerate((dq_one, dk_one, dv_one)):
            both = jnp.concatenate([early[...], grads[part * half : (part + 1) * half, :]], 0)
            made = made + nn(held[part], both)
        d_tokens[...] = made.T

    @pl.when(step >= blocks_of(facts[1]))
    def blank():
        d_tokens[...] = jnp.zeros_like(d_tokens)


def in_place(shape):
    return pl.BlockSpec(shape, lambda step: (0,) * len(shape))


def columns_block(rows, span=STEP):
    return pl.BlockSpec((rows, span), lambda step: (0, step))


def rows_block(columns, span=STEP):
    return pl.BlockSpec((span, columns), lambda step: (step, 0))


def head_block(head_dim, columns, first=0, count=HEADS):
    return pl.BlockSpec(
        (head_dim, columns), lambda step: (first + jnp.minimum(step, count - 1), 0)
    )


def call(kernel, steps, ins, outs, scratch, cost, room=20):
    def spec_of(spec):
        return pl.BlockSpec(memory_space=pl.ANY) if spec is None else spec

    return pl.pallas_call(
        kernel,
        grid=(steps,),
        out_shape=[jax.ShapeDtypeStruct(shape, dtype) for shape, dtype, spec in outs],
        in_specs=[spec_of(spec) for array, spec in ins],
        out_specs=[spec_of(spec) for shape, dtype, spec in outs],
        scratch_shapes=scratch,
        compiler_params=pltpu.CompilerParams(
            vmem_limit_bytes=room * 2**20, dimension_semantics=("arbitrary",)
        ),
        cost_estimate=pl.CostEstimate(
            flops=int(cost * 1.0e9), bytes_accessed=4 * 2**20, transcendentals=0
        ),
        name=kernel.__name__,
    )(*[array for array, spec in ins])


SIDES = (0, 2, 4, 6)
DEPTHS = (0, 8, 16, 24)


def swap(values, mask):
    count = lax.axis_size("dp")
    return lax.ppermute(values, "dp", [(spot, spot ^ mask) for spot in range(count)])


def spread_along(held, masks):
    return [held] + [swap(held, mask) for mask in masks[1:]]


def after(value, *earlier):
    return lax.optimization_barrier((value, earlier))[0]


class Staged:
    def deep(self, piece, late=0):
        return spread_along(piece[None], DEPTHS)

    def wide(self, held):
        return spread_along(held, SIDES)

    def both(self, held):
        return held, swap(held, 1)

    def join(self, parts):
        return jnp.concatenate(parts, 0)

    def add_core(self, keep, send, late=0):
        return keep, swap(send, 1)

    def sum_core(self, pair):
        keep, got = pair
        sums = [
            keep[4 * side : 4 * side + 4].astype(full) + got[4 * side : 4 * side + 4].astype(full)
            for side in range(4)
        ]
        return [sums[0]] + [part.astype(keep.dtype) for part in sums[1:]]

    def add_wide(self, sums):
        return [sums[0]] + [swap(sums[side], SIDES[side]) for side in range(1, 4)]

    def total(self, parts):
        total = parts[0]
        for part in parts[1:]:
            total = total + part.astype(full)
        return total

    def sum_wide(self, parts):
        wire = parts[1].dtype
        total = self.total(parts)
        return [total[0]] + [total[deep].astype(wire) for deep in range(1, 4)]

    def add_deep(self, sums):
        return [sums[0]] + [swap(sums[deep], DEPTHS[deep]) for deep in range(1, 4)]

    def finish(self, parts):
        return self.total(parts)


class Plain:
    def __init__(self, devices, chunks, rows, width, order):
        self.devices, self.chunks, self.rows, self.width = devices, chunks, rows, width
        self.order = order

    def arrange(self, gathered, by_row):
        group = self.devices // self.chunks
        split = gathered.reshape(self.chunks, group, -1, self.rows, self.width)
        if not by_row:
            split = split.transpose(0, 2, 1, 3, 4)
        return split.reshape(self.chunks, -1, self.width)

    def spread(self, ordered, by_row):
        group = self.devices // self.chunks
        if by_row:
            return ordered.reshape(self.devices, -1, self.width)
        split = ordered.reshape(self.chunks, -1, group, self.rows, self.width)
        return split.transpose(0, 2, 1, 3, 4).reshape(self.devices, -1, self.width)

    def deep(self, piece, late=0):
        gathered = lax.all_gather(piece, "dp", axis=0)
        plain = piece.shape[0] - late
        ordered = self.arrange(gathered[:, :plain], False)
        if late:
            ordered = jnp.concatenate([ordered, self.arrange(gathered[:, plain:], True)], 1)
        return jnp.take(ordered, jnp.array(self.order), axis=0)

    def wide(self, held):
        return held

    def join(self, held):
        return held

    def both(self, held):
        return held[: self.chunks // 2], held[self.chunks // 2 :]

    def add_core(self, keep, send, late=0):
        back = [self.order.index(place) for place in range(self.chunks)]
        ordered = jnp.take(jnp.concatenate([keep, send], 0), jnp.array(back), axis=0)
        plain = ordered.shape[1] - late * UNIT
        split = self.spread(ordered[:, :plain], False)
        if late:
            split = jnp.concatenate([split, self.spread(ordered[:, plain:], True)], 1)
        return lax.psum_scatter(split.astype(full), "dp", scatter_dimension=0, tiled=False)

    def sum_core(self, value):
        return value

    def add_wide(self, value):
        return value

    def sum_wide(self, value):
        return value

    def add_deep(self, value):
        return value

    def finish(self, value):
        return value


def body(
    tokens, memory, directions, target_len, memory_len, self_qkv, self_out, cross_query, cross_kv,
    cross_out, ffn_in, ffn_out, vectors, cotangent,
):
    tokens, memory, cotangent = tokens[0], memory[0], cotangent[0]
    length, width = tokens.shape
    others = memory.shape[0]
    devices = lax.axis_size("dp")
    rows = self_out.shape[0] // width
    chunks = width // UNIT
    parts = ffn_in.shape[0] // (rows * width)
    hidden = parts * width
    head_dim = width // HEADS
    order = place_order()
    order = order + [place ^ 1 for place in order]
    nearby = devices == chunks == len(order)
    me = lax.axis_index("dp") if nearby else jnp.int32(0)
    ways = Staged() if nearby else Plain(devices, chunks, rows, width, order)

    def stack(flat, by_row=False):
        if by_row:
            return flat
        return flat.reshape(rows, -1, width).transpose(1, 0, 2).reshape(-1)

    def piece_of(*flats):
        return jnp.concatenate(flats).reshape(-1, width)

    facts = jnp.concatenate([directions, target_len, memory_len, me[None]])
    one = stack(self_qkv)
    if nearby:
        one = jnp.concatenate([one, jnp.pad(vectors, (0, 8 * width - vectors.shape[0]))])
    one = ways.join(ways.deep(piece_of(one)))
    two = piece_of(*[stack(w) for w in (self_out, cross_query, cross_kv, cross_out)])
    two = ways.deep(after(two, one))
    one = ways.join(ways.wide(one))
    two = ways.join(two)
    one = after(one, two)
    three = piece_of(stack(ffn_in), stack(ffn_out, True))
    two = after(two, one)
    three = ways.deep(after(three, two), parts * rows)
    two_sent = ways.wide(two)
    one = ways.both(one)

    if nearby:
        held = jnp.concatenate([part[:, 3 * UNIT, : vectors.shape[0]] for part in one], 0)
        wanted = jnp.bitwise_xor(me, lax.iota(jnp.int32, chunks))
        choice = (wanted[:, None] == jnp.array(order, jnp.int32)[None, :]).astype(full)
        vector_full = lax.dot(choice.astype(low), held, preferred_element_type=full)
    else:
        vector_full = lax.all_gather(vectors, "dp", axis=0, tiled=True).astype(full)
    columns = jnp.pad(vector_full.reshape(-1, width).T, ((0, 0), (0, 109)))

    smem = pl.BlockSpec(memory_space=pltpu.SMEM)
    facts = (facts, smem)
    columns = (columns, in_place((width, 128)))
    sem = pltpu.SemaphoreType.DMA
    vm = pltpu.VMEM
    head_dim = width // HEADS
    steps = length // STEP
    along = columns_block(width)
    by_head, by_head_other = head_block(head_dim, length), head_block(head_dim, others)
    eight = in_place((8, width))

    def units(count):
        return vm((count, width, width), low)

    def stored(count):
        return ((chunks // 2, count * UNIT, width), low, None)

    def remote(pair):
        return [(pair[0], None), (pair[1], None)]

    low_t, full_t = ((width, length), low), ((width, length), full)
    low_m = ((width, others), low)
    sums = ((HEADS, length), full, in_place((HEADS, length)))
    peaks = ((2,), full, smem)

    token_t, q, k, v, peaks_one = call(
        project_kernel, steps,
        [facts, (after(tokens, two), rows_block(width)), *remote(one), columns],
        [(*low_t, along)] * 4 + [peaks],
        [units(3), sem],
        3.0,
    )
    three = ways.join(after(three, peaks_one))
    three_sent = ways.wide(three)
    mix, sums_one = call(
        self_forward_kernel, HEADS,
        [facts, (after(peaks_one, three), smem), (q, by_head), (k, by_head), (v, by_head)],
        [(*full_t, by_head), sums],
        [],
        5.0,
    )
    two = ways.both(ways.join(after(two_sent, sums_one)))
    hat, scale, memory_t, cq, ck, cv, peaks_two = call(
        encode_kernel, steps,
        [facts, (token_t, along), (memory, rows_block(width)), (mix, along), *remote(two),
         columns],
        [(*full_t, along), ((8, length), full, columns_block(8)), (*low_m, along),
         (*low_t, along), (*low_m, along), (*low_m, along), peaks],
        [units(4), sem],
        4.0,
    )
    cross_mix, sums_two = call(
        cross_forward_kernel, HEADS,
        [facts, (peaks_two, smem), (cq, by_head), (ck, by_head_other), (cv, by_head_other)],
        [(*full_t, by_head), sums],
        [vm((AUG, others), low)],
        8.0,
    )
    three = ways.both(ways.join(after(three_sent, sums_two)))
    whole_t = in_place((width, length))
    out, dr_two, dcross, keep_three, send_three, g_cross_out, rows_ffn = call(
        ffn_kernel, 1,
        [facts, (hat, whole_t), (cross_mix, whole_t), (cotangent, None), *remote(two),
         *remote(three), columns],
        [((length, width), low, None), (*full_t, whole_t), (*low_t, whole_t),
         stored(2 * parts), stored(2 * parts),
         ((width, width), low, in_place((width, width))), ((16, width), full, in_place((16, width)))],
        [units(1), units(parts), vm((chunks, parts, UNIT, width), low), units(parts),
         vm((chunks, parts, UNIT, width), low), vm((hidden, length), full),
         vm((hidden, length), low), vm((length, width), low), vm((length, width), low),
         pltpu.SemaphoreType.DMA((5,))],
        20.0,
        56,
    )
    g_three = ways.add_core(keep_three, send_three, parts)
    dcq, dck, dcv = call(
        cross_backward_kernel, HEADS,
        [facts, (cq, by_head), (ck, by_head_other), (cv, by_head_other), (cross_mix, by_head),
         (sums_two, sums[2]), (dcross, by_head)],
        [(*low_t, by_head), (*low_m, by_head_other), (*low_m, by_head_other)],
        [vm((head_dim, others), full), vm((head_dim, others), full), vm((AUG, others), low)],
        16.0,
    )
    g_three = ways.sum_core(after(g_three, dcq))
    dcq = after(dcq, g_three)
    g_three = ways.add_wide(g_three)
    square = vm((width, width), full)
    dr_one, dself, keep_two, send_two, rows_cross = call(
        middle_kernel, steps,
        [facts, (dcq, along), (dck, along), (dcv, along), (dr_two, along), (hat, along),
         (scale, columns_block(8)), (memory_t, along), (mix, along), *remote(two),
         (g_cross_out, in_place((width, width))), columns],
        [(*full_t, along), (*low_t, along), stored(5), stored(5), ((8, width), full, eight)],
        [units(2), units(5), square, square, square, square, vm((3, width, 128), full), sem],
        5.0,
    )
    g_two = ways.add_core(keep_two, send_two)
    g_three = ways.sum_wide(after(g_three, keep_two))
    dself = after(dself, g_three)
    g_three = ways.add_deep(g_three)
    early, late = (head_block(head_dim, length, at, HEADS // 2) for at in (0, HEADS // 2))
    half_t = (width // 2, length)
    dq_one, dk_one, dv_one = call(
        self_backward_kernel, HEADS // 2,
        [facts, (q, early), (k, early), (v, early), (mix, early), (sums_one, sums[2]),
         (dself, early)],
        [(half_t, low, early)] * 3,
        [vm((head_dim, length), full), vm((head_dim, length), full)],
        6.0,
    )
    g_three = ways.finish(after(g_three, dv_one))
    g_two = ways.sum_core(after(g_two, dv_one))
    dself = after(dself, g_two)
    g_two = ways.add_wide(g_two)
    whole = in_place(half_t)
    grads, keep_one, send_one, rows_self = call(
        self_finish_kernel, HEADS // 2 + 1,
        [facts, (q, late), (k, late), (v, late), (mix, late), (sums_one, sums[2]),
         (after(dself, g_three), late), (token_t, in_place((width, length))), (dq_one, whole),
         (dk_one, whole), (dv_one, whole), (rows_ffn, in_place((16, width))),
         (rows_cross, eight), *remote(one), columns],
        [((3 * width // 2, length), low, in_place((3 * width // 2, length))), stored(4), stored(4),
         ((8, width), full, eight)],
        [vm((head_dim, length), full), vm((head_dim, length), full),
         vm((3, width, width), full), units(3), vm((chunks, 1, UNIT, width), low), units(3), sem, sem],
        8.0,
    )
    if not nearby:
        keep_one, send_one = keep_one[:, : 3 * UNIT], send_one[:, : 3 * UNIT]
    g_one = ways.add_core(keep_one, send_one)
    (d_memory,) = call(
        memory_grad_kernel, steps,
        [facts, (after(dck, keep_one), along), (dcv, along), *remote(two)],
        [((others, width), full, rows_block(width))],
        [units(2), sem],
        2.0,
    )
    g_two = ways.sum_wide(after(g_two, keep_one))
    g_one = ways.sum_core(after(g_one, d_memory))
    grads = after(grads, g_one)
    g_two = ways.add_deep(g_two)
    g_one = ways.add_wide(g_one)
    half_along = columns_block(width // 2)
    (d_tokens,) = call(
        token_grad_kernel, steps,
        [facts, (dq_one, half_along), (dk_one, half_along), (dv_one, half_along),
         (grads, columns_block(3 * width // 2)), (dr_one, along), *remote(one)],
        [((length, width), full, rows_block(width))],
        [units(3), sem],
        3.0,
    )
    g_two = ways.finish(after(g_two, d_tokens))
    g_one = ways.finish(ways.add_deep(ways.sum_wide(after(g_one, d_tokens))))
    if nearby:
        g_vectors = g_one[3 * UNIT, : vectors.shape[0]]
    else:
        g_vectors = jnp.concatenate(
            [
                rows_self[0:1], rows_self[2:3], rows_cross[2:3], rows_cross[0:2], rows_ffn[5:6],
                rows_ffn[4:5], rows_cross[3:4], rows_ffn[6:8], rows_cross[4:5], rows_ffn[8:10],
                rows_self[3:5], rows_ffn[0:4],
            ],
            0,
        ).reshape(-1)
        g_vectors = lax.psum_scatter(g_vectors, "dp", scatter_dimension=0, tiled=True)

    def flat(grad, first, stop):
        piece = grad[first * rows : stop * rows].reshape(stop - first, rows, width)
        return piece.transpose(1, 0, 2).reshape(-1)

    return (
        out[None], d_tokens[None], d_memory[None],
        flat(g_one, 0, 3), flat(g_two, 0, 1), flat(g_two, 1, 2), flat(g_two, 2, 4),
        flat(g_two, 4, 5), flat(g_three, 0, parts), g_three[parts * rows :].reshape(-1), g_vectors,
    )


def solution(mesh):
    rows, flat = P("dp", None, None), P("dp")
    return jax.shard_map(
        body,
        mesh=mesh,
        in_specs=(rows, rows) + (flat,) * 11 + (rows,),
        out_specs=(rows,) * 3 + (flat,) * 8,
        check_vma=False,
    )
```

```python
import jax
import jax.numpy as jnp
from jax import lax
from jax.experimental import pallas as pl
from jax.experimental.pallas import tpu as pltpu
from jax.sharding import PartitionSpec as P

HEADS = 8
STEP = 256
PAIR = 2 * STEP
AUG = 16
UNIT = 16
SAFE_SQUARE = 3600.0
mask_fill = -1000000000.0
norm_eps = 1e-05
low = jnp.bfloat16
full = jnp.float32


def contract(left, right, left_dim, right_dim):
    return lax.dot_general(
        left, right, (((left_dim,), (right_dim,)), ((), ())), preferred_element_type=full
    )


def nn(left, right):
    return contract(left, right, 1, 0)


def tn(left, right):
    return contract(left, right, 0, 0)


def nt(left, right):
    return contract(left, right, 1, 1)


def block(index):
    return slice(index * STEP, (index + 1) * STEP)


def blocks_of(length):
    return (length + STEP - 1) // STEP


def split_three(values):
    first = values.astype(low)
    rest = values - first.astype(full)
    second = rest.astype(low)
    third = (rest - second.astype(full)).astype(low)
    return first, second, third


def normalize(values):
    center = jnp.mean(values, axis=0, keepdims=True)
    offsets = values - center
    spread = jnp.mean(offsets * offsets, axis=0, keepdims=True)
    scale = lax.rsqrt(spread + norm_eps)
    return offsets * scale, scale


def norm_backward(grad, hat, scale, gain):
    scaled = grad * gain
    center = jnp.mean(scaled, axis=0, keepdims=True)
    along = jnp.mean(scaled * hat, axis=0, keepdims=True)
    return (scaled - center - hat * along) * scale


def fold_lanes(values):
    total = values[:, :128]
    for start in range(128, values.shape[1], 128):
        total = total + values[:, start : start + 128]
    return total


def lane_total(partial):
    ones = jnp.ones((8, 128), full)
    return lax.dot_general(
        ones,
        partial,
        (((1,), (1,)), ((), ())),
        precision=lax.Precision.HIGHEST,
        preferred_element_type=full,
    )[0:1]


def token_total(values):
    return nt(jnp.ones((AUG, values.shape[1]), low), values)[0:1]


def head_rows(head, head_dim):
    return pl.ds(pl.multiple_of(head * head_dim, head_dim), head_dim)


def square_peak(values, head_dim):
    squares = jnp.square(values.astype(full))
    count = values.shape[0] // head_dim
    return jnp.max(jnp.sum(squares.reshape(count, head_dim, values.shape[1]), axis=1))


def place_order():
    return [side ^ deep for side in (0, 2, 4, 6) for deep in (0, 8, 16, 24)]


def unit_spot(whole, owner, by_row):
    if by_row:
        return whole.at[owner]
    return whole.at[:, pl.ds(pl.multiple_of(owner * UNIT, UNIT), UNIT), :]


def unit_part(buffer, index, first, stop):
    part = buffer.at[index, first * UNIT : stop * UNIT]
    return part.reshape(stop - first, UNIT, buffer.shape[2])


def start_fetch(me, near, far, moves, sem):
    for index, relative in enumerate(place_order()):
        for sources, place in ((near, relative), (far, relative ^ 1)):
            owner = jnp.bitwise_xor(me, place)
            each = sources[0].shape[0]
            for target, first, stop, by_row in moves:
                spot = unit_spot(target, owner, by_row)
                part = unit_part(sources[index // each], index % each, first, stop)
                pltpu.make_async_copy(part, spot, sem).start()


def wait_fetch(moves, sem):
    for target, first, stop, by_row in moves:
        pltpu.make_async_copy(target, target, sem).wait()


def start_store(me, near, far, moves, sem):
    for index, relative in enumerate(place_order()):
        for sink, place in ((near, relative), (far, relative ^ 1)):
            owner = jnp.bitwise_xor(me, place)
            for source, first, stop, by_row in moves:
                spot = unit_spot(source, owner, by_row)
                part = unit_part(sink, index, first, stop)
                pltpu.make_async_copy(spot, part, sem).start()


def attend_forward(
    q_ref, k_ref, v_ref, mix_ref, sums_ref, head, mask_rows, pairs, keys, shifted
):
    causal = mask_rows is None
    head_dim = q_ref.shape[0]
    key_head = k_ref[:, :keys]
    if not causal:
        key_head = jnp.concatenate([key_head, mask_rows[:, :keys]], 0)
    value_head = jnp.concatenate([v_ref[:, :keys], jnp.ones((AUG, keys), low)], 0)
    for pair in range(pairs):
        columns = slice(pair * PAIR, (pair + 1) * PAIR)
        query = q_ref[:, columns]
        if causal:
            main = pair * PAIR + STEP
            scores = tn(key_head[:, :main], query)
            late = tn(key_head[:, main : main + STEP], query[:, STEP:])
            key_pos = lax.broadcasted_iota(jnp.int32, (STEP, STEP), 0)
            query_pos = lax.broadcasted_iota(jnp.int32, (STEP, STEP), 1)
            allowed = key_pos <= query_pos
            edge = scores[main - STEP :]
            edge = jnp.concatenate(
                [jnp.where(allowed, edge[:, :STEP], mask_fill), edge[:, STEP:]], 1
            )
            scores = edge if main == STEP else jnp.concatenate([scores[: main - STEP], edge], 0)
            late = jnp.where(allowed, late, mask_fill)
        else:
            query = jnp.concatenate([query, jnp.ones((AUG, PAIR), low)], 0)
            scores = tn(key_head, query)
        if shifted:
            highest = jnp.max(scores, axis=0, keepdims=True)
            if causal:
                second = jnp.maximum(highest[:, STEP:], jnp.max(late, axis=0, keepdims=True))
                highest = jnp.concatenate([highest[:, :STEP], second], 1)
                late = late - second
            scores = scores - highest
        powered = jnp.exp(scores).astype(low)
        if causal:
            mixed = nn(value_head[:, :main], powered)
            extra = nn(value_head[:, main : main + STEP], jnp.exp(late).astype(low))
            mixed = jnp.concatenate([mixed[:, :STEP], mixed[:, STEP:] + extra], 1)
        else:
            mixed = nn(value_head, powered)
        total = mixed[head_dim : head_dim + 1]
        mix_ref[:, columns] = mixed[:head_dim] / total
        log_sum = jnp.log(total)
        sums_ref[pl.ds(head, 1), columns] = log_sum + highest if shifted else log_sum


def attend_backward(
    q_ref, k_ref, v_ref, mix_ref, sums_ref, head, grad_ref, dq_ref, dk_ref, dv_ref,
    key_sum, value_sum, mask_rows, steps, keys
):
    causal = mask_rows is None
    length = steps * STEP
    scale = q_ref.shape[0] ** (-0.5)
    key_head = k_ref[:, :keys]
    value_head = v_ref[:, :keys]
    query = q_ref[:, :length]
    grad = grad_ref[:, :length]
    inner = jnp.sum(grad.astype(full) * mix_ref[:, :length], axis=0, keepdims=True)
    one = jnp.ones((1, length), low)
    blank = jnp.zeros((AUG - 4, length), low)
    query_aug = jnp.concatenate(
        [query, *split_three(sums_ref[pl.ds(head, 1), :length]), one, blank], 0
    )
    grad_aug = jnp.concatenate([grad, *split_three(inner), one, blank], 0)
    minus = jnp.full((3, keys), -1.0, low)
    key_blank = jnp.zeros((AUG - 3, keys), low)
    value_aug = jnp.concatenate([value_head, minus, key_blank], 0)
    if causal:
        key_aug = jnp.concatenate([key_head, minus, key_blank], 0)
    else:
        key_aug = jnp.concatenate([key_head, minus, mask_rows[0:1, :keys], key_blank[1:]], 0)
    for step in range(steps):
        span = block(step)
        count = (step + 1) * STEP if causal else keys
        scores = tn(query_aug[:, span], key_aug[:, :count])
        chances = jnp.exp(scores)
        if causal:
            query_pos = lax.broadcasted_iota(jnp.int32, (STEP, STEP), 0)
            key_pos = lax.broadcasted_iota(jnp.int32, (STEP, STEP), 1)
            edge = jnp.where(key_pos <= query_pos, chances[:, count - STEP :], 0.0)
            chances = (
                edge if count == STEP
                else jnp.concatenate([chances[:, : count - STEP], edge], 1)
            )
        grad_chances = tn(grad_aug[:, span], value_aug[:, :count])
        grad_scores = (chances * grad_chances).astype(low)
        to_value = nn(grad[:, span], chances.astype(low))
        to_key = nn(query[:, span], grad_scores)
        to_query = nt(key_head[:, :count], grad_scores)
        dq_ref[:, span] = (to_query * scale).astype(low)
        if step == 0:
            value_sum[:, :count] = to_value
            key_sum[:, :count] = to_key
        elif causal:
            old = count - STEP
            value_sum[:, :old] += to_value[:, :old]
            key_sum[:, :old] += to_key[:, :old]
            value_sum[:, old:count] = to_value[:, old:]
            key_sum[:, old:count] = to_key[:, old:]
        else:
            value_sum[:, :count] += to_value
            key_sum[:, :count] += to_key
    dv_ref[:, :keys] = value_sum[:, :keys].astype(low)
    dk_ref[:, :keys] = key_sum[:, :keys].astype(low)


def gather_into(first, ref, value):
    if first:
        ref[...] = value
    else:
        ref[...] += value


def self_forward_kernel(
    facts, tokens, near, far, vector_rows, token_t, q_ref, k_ref, v_ref, mix_ref, sums_ref, columns,
    q_all, k_all, v_all, held, sem, peaks
):
    step = pl.program_id(0)
    width, length = q_all.shape
    blocks = length // STEP
    head_dim = width // HEADS
    moves = [(held, 0, 3, False)]

    @pl.when(step == 0)
    def prepare():
        start_fetch(facts[3], near, far, moves, sem)
        peaks[0] = 0.0
        peaks[1] = 0.0
        rest = jnp.zeros((128 - vector_rows.shape[0], width), full)
        columns[...] = jnp.concatenate([vector_rows[...], rest], 0).T
        wait_fetch(moves, sem)

    @pl.when((step < blocks) & (step < blocks_of(facts[1])))
    def live():
        embed = jnp.where(facts[0] == 1, columns[:, 14:15], columns[:, 13:14])
        flipped = tokens[...].T
        token_t[...] = flipped
        shared = (flipped.astype(full) + embed).astype(low)
        query = (tn(held[0], shared) + columns[:, 0:1]).astype(low) * (head_dim ** (-0.5))
        key = tn(held[1], shared).astype(low)
        value = (tn(held[2], shared) + columns[:, 1:2]).astype(low)
        spot = pl.ds(pl.multiple_of(step * STEP, STEP), STEP)
        for ref, all_ref, made in (
            (q_ref, q_all, query), (k_ref, k_all, key), (v_ref, v_all, value)
        ):
            ref[...] = made
            all_ref[:, spot] = made
        peaks[0] = jnp.maximum(peaks[0], square_peak(query, head_dim))
        peaks[1] = jnp.maximum(peaks[1], square_peak(key, head_dim))

    head = step - blocks
    safe = peaks[0] * peaks[1] <= SAFE_SQUARE
    pairs = (blocks_of(facts[1]) + 1) // 2
    rows = pl.ds(pl.multiple_of(jnp.maximum(head, 0) * head_dim, head_dim), head_dim)
    for wanted in range(1, length // PAIR + 1):
        for shifted in (False, True):

            @pl.when((step >= blocks) & (pairs == wanted) & (safe != shifted))
            def attend():
                attend_forward(
                    q_all.at[rows], k_all.at[rows], v_all.at[rows], mix_ref, sums_ref, head, None,
                    wanted, wanted * PAIR, shifted,
                )


def fill_mask(mask_ref, visible):
    position = lax.broadcasted_iota(jnp.int32, mask_ref.shape, 1)
    row = lax.broadcasted_iota(jnp.int32, mask_ref.shape, 0)
    hidden = (position >= visible) & (row == 0)
    mask_ref[...] = jnp.where(hidden, mask_fill, 0.0).astype(low)


def cross_forward_kernel(
    facts, token_t, memory, mix, near, far, columns,
    hat_ref, scale_ref, memory_t, q_ref, k_ref, v_ref, mix_ref, sums_ref,
    q_all, k_all, v_all, held, sem, mask_ref, peaks
):
    step = pl.program_id(0)
    width, length = q_all.shape
    others = k_all.shape[1]
    blocks = max(length, others) // STEP
    head_dim = width // HEADS
    moves = [(held, 0, 4, False)]
    spot = pl.ds(pl.multiple_of(jnp.minimum(step, blocks - 1) * STEP, STEP), STEP)

    @pl.when(step == 0)
    def prepare():
        start_fetch(facts[3], near, far, moves, sem)
        fill_mask(mask_ref, facts[2])
        peaks[0] = 0.0
        peaks[1] = 0.0
        wait_fetch(moves, sem)

    @pl.when((step < blocks) & (step < blocks_of(facts[2])))
    def encode():
        flipped = memory[...].T
        memory_t[...] = flipped
        key = tn(held[2], flipped).astype(low)
        value = (tn(held[3], flipped) + columns[:, 4:5]).astype(low)
        k_ref[...] = key
        v_ref[...] = value
        k_all[:, spot] = key
        v_all[:, spot] = value
        peaks[1] = jnp.maximum(peaks[1], square_peak(key, head_dim))

    @pl.when((step < blocks) & (step < blocks_of(facts[1])))
    def first():
        embed = jnp.where(facts[0] == 1, columns[:, 14:15], columns[:, 13:14])
        started = token_t[...].astype(full) + embed
        total = started + tn(held[0], mix[...].astype(low)) + columns[:, 2:3]
        hat, scale = normalize(total)
        hat_ref[...] = hat
        scale_ref[...] = jnp.broadcast_to(scale, scale_ref.shape)
        shared = (hat * columns[:, 7:8] + columns[:, 10:11]).astype(low)
        query = (tn(held[1], shared) + columns[:, 3:4]).astype(low) * (head_dim ** (-0.5))
        q_ref[...] = query
        q_all[:, spot] = query
        peaks[0] = jnp.maximum(peaks[0], square_peak(query, head_dim))

    head = step - blocks
    safe = peaks[0] * peaks[1] <= SAFE_SQUARE
    pairs = (blocks_of(facts[1]) + 1) // 2
    key_count = blocks_of(facts[2])
    rows = pl.ds(pl.multiple_of(jnp.maximum(head, 0) * head_dim, head_dim), head_dim)
    for wanted in range(1, length // PAIR + 1):
        for wanted_keys in range(1, others // STEP + 1):
            for shifted in (False, True):

                @pl.when(
                    (step >= blocks) & (pairs == wanted) & (key_count == wanted_keys)
                    & (safe != shifted)
                )
                def attend():
                    attend_forward(
                        q_all.at[rows], k_all.at[rows], v_all.at[rows], mix_ref, sums_ref, head,
                        mask_ref[...], wanted, wanted_keys * STEP, shifted,
                    )


def gelu_parts(values):
    half = 0.5 * (1.0 + lax.erf(values * (0.5**0.5)))
    bell = jnp.exp(-0.5 * values * values) * 0.3989422804014327
    return values * half, half + values * bell


def ffn_kernel(
    facts, hat_one, cross_mix, cotangent, near_two, far_two, near, far, columns,
    out_ref, dr_ref, dmix_ref, keep, send, g_cross_out, g_rows,
    c_out, f_in, f_out, low_in, low_out, slope, acts, top_ref, result_ref, sems
):
    length, width = top_ref.shape
    parts = f_in.shape[0]
    rows_of = width // parts // UNIT
    moves_two = [(c_out, 4, 5, False)]
    moves_in = [(f_in, 0, parts, False)]
    moves_out = [(f_out, parts, 2 * parts, True)]
    stores_in = [(low_in, 0, parts, False)]
    stores_out = [(low_out, parts, 2 * parts, True)]
    fetch_top = pltpu.make_async_copy(cotangent, top_ref, sems.at[3])
    store_result = pltpu.make_async_copy(result_ref, out_ref, sems.at[4])
    start_fetch(facts[3], near_two, far_two, moves_two, sems.at[0])
    start_fetch(facts[3], near, far, moves_in, sems.at[1])
    start_fetch(facts[3], near, far, moves_out, sems.at[2])
    fetch_top.start()
    g_rows[...] = jnp.zeros_like(g_rows)

    def out_part(part):
        return f_out[part * rows_of : (part + 1) * rows_of].reshape(width, width)

    def live(count):
        span = slice(0, count)
        wait_fetch(moves_two, sems.at[0])
        position = lax.broadcasted_iota(jnp.int32, (1, count), 1)
        alive = position < facts[1]
        valid = alive.astype(full)
        mixed = jnp.where(alive, cross_mix[:, span], 0.0).astype(low)
        hat = jnp.where(alive, hat_one[:, span], 0.0)
        first = hat * columns[:, 7:8] + columns[:, 10:11]
        total = first + tn(c_out[0], mixed) + columns[:, 5:6]
        hat_two, scale_two = normalize(total)
        second = hat_two * columns[:, 8:9] + columns[:, 11:12]
        shared = second.astype(low)
        third = second + columns[:, 6:7]
        wait_fetch(moves_in, sems.at[1])
        wait_fetch(moves_out, sems.at[2])
        for part in range(parts):
            chunk = slice(part * width, (part + 1) * width)
            raw = tn(f_in[part], shared) + columns[:, 15 + part : 16 + part]
            act, slope_part = gelu_parts(raw)
            slope[chunk, span] = slope_part
            acts[chunk, span] = act.astype(low)
            third = third + tn(out_part(part), acts[chunk, span])
        hat_three, scale_three = normalize(third)
        result = (hat_three * columns[:, 9:10] + columns[:, 12:13]) * valid
        result_ref[span, :] = result.astype(low).T
        if count < length:
            result_ref[count:, :] = jnp.zeros((length - count, width), low)
        store_result.start()
        fetch_top.wait()
        top = top_ref[span, :].T.astype(full) * valid
        g_rows[7:8] = lane_total(fold_lanes(top * hat_three))
        g_rows[9:10] = lane_total(fold_lanes(top))
        grad_third = norm_backward(top, hat_three, scale_three, columns[:, 9:10])
        branch = grad_third.astype(low)
        g_rows[4:5] = token_total(branch)
        grad_second = grad_third
        for part in range(parts):
            chunk = slice(part * width, (part + 1) * width)
            back = nn(out_part(part), branch)
            rows = slice(part * rows_of, (part + 1) * rows_of)
            low_out[rows] = nt(acts[chunk, span], branch).astype(low).reshape(
                rows_of, parts, UNIT, width
            )
            acts[chunk, span] = (back * slope[chunk, span]).astype(low)
        start_store(facts[3], keep, send, stores_out, sems.at[2])
        for part in range(parts):
            chunk = slice(part * width, (part + 1) * width)
            grad_hidden = acts[chunk, span]
            g_rows[part : part + 1] = token_total(grad_hidden)
            low_in[part] = nt(shared, grad_hidden).astype(low)
            grad_second = grad_second + nn(f_in[part], grad_hidden)
        start_store(facts[3], keep, send, stores_in, sems.at[1])
        g_rows[6:7] = lane_total(fold_lanes(grad_second * hat_two))
        g_rows[8:9] = lane_total(fold_lanes(grad_second))
        grad_two = norm_backward(grad_second, hat_two, scale_two, columns[:, 8:9])
        dr_ref[:, span] = grad_two
        branch_two = grad_two.astype(low)
        g_rows[5:6] = token_total(branch_two)
        g_cross_out[...] = nt(mixed, branch_two).astype(low)
        dmix_ref[:, span] = nn(c_out[0], branch_two).astype(low)

    live(length)
    wait_fetch(stores_out, sems.at[2])
    wait_fetch(stores_in, sems.at[1])
    store_result.wait()


def cross_backward_kernel(
    facts, q_ref, k_ref, v_ref, cross_mix, sums_ref, dmix, dq_ref, dk_ref, dv_ref,
    key_sum, value_sum, mask_ref
):
    head = pl.program_id(0)
    length = q_ref.shape[1]
    others = k_ref.shape[1]
    count = blocks_of(facts[1])
    key_count = blocks_of(facts[2])

    @pl.when(head == 0)
    def prepare():
        fill_mask(mask_ref, facts[2])

    for wanted in range(1, length // STEP + 1):
        for wanted_keys in range(1, others // STEP + 1):

            @pl.when((count == wanted) & (key_count == wanted_keys))
            def attend():
                attend_backward(
                    q_ref, k_ref, v_ref, cross_mix, sums_ref, head, dmix,
                    dq_ref, dk_ref, dv_ref, key_sum, value_sum, mask_ref[...],
                    wanted, wanted_keys * STEP,
                )


def middle_kernel(
    facts, dq_ref, dk_ref, dv_ref, dr_two, hat_one, scale_one, memory_t, mix, near, far,
    g_cross_out, columns, dr_ref, dself, keep, send, g_rows,
    held, made_low, sum_query, sum_key, sum_value, sum_out, lanes, sem
):
    step = pl.program_id(0)
    moves = [(held, 0, 2, False)]

    @pl.when(step == 0)
    def prepare():
        start_fetch(facts[3], near, far, moves, sem)
        g_rows[...] = jnp.zeros_like(g_rows)
        lanes[...] = jnp.zeros_like(lanes)
        wait_fetch(moves, sem)

    def encode(initial):
        g_rows[1:2] += token_total(dv_ref[...])
        gather_into(initial, sum_key, nt(memory_t[...], dk_ref[...]))
        gather_into(initial, sum_value, nt(memory_t[...], dv_ref[...]))

    def first(initial):
        hat = hat_one[...]
        shared = (hat * columns[:, 7:8] + columns[:, 10:11]).astype(low)
        grad_query = dq_ref[...]
        g_rows[0:1] += token_total(grad_query)
        gather_into(initial, sum_query, nt(shared, grad_query))
        grad = dr_two[...] + nn(held[1], grad_query)
        lanes[0] += fold_lanes(grad * hat)
        lanes[1] += fold_lanes(grad)
        grad_one = norm_backward(grad, hat, scale_one[0:1], columns[:, 7:8])
        dr_ref[...] = grad_one
        lanes[2] += fold_lanes(grad_one)
        branch = grad_one.astype(low)
        g_rows[2:3] += token_total(branch)
        gather_into(initial, sum_out, nt(mix[...].astype(low), branch))
        dself[...] = nn(held[0], branch).astype(low)

    pl.when(step == 0)(lambda: encode(True))
    pl.when((step > 0) & (step < blocks_of(facts[2])))(lambda: encode(False))
    pl.when(step == 0)(lambda: first(True))
    pl.when((step > 0) & (step < blocks_of(facts[1])))(lambda: first(False))

    @pl.when(step == pl.num_programs(0) - 1)
    def close():
        made_low[0] = sum_out[...].astype(low)
        made_low[1] = sum_query[...].astype(low)
        made_low[2] = sum_key[...].astype(low)
        made_low[3] = sum_value[...].astype(low)
        made_low[4] = g_cross_out[...]
        stores = [(made_low, 0, 5, False)]
        start_store(facts[3], keep, send, stores, sem)
        g_rows[3:4] = lane_total(lanes[0])
        g_rows[4:5] = lane_total(lanes[1])
        g_rows[5:6] = lane_total(lanes[2])
        wait_fetch(stores, sem)


def memory_grad_kernel(facts, dk_ref, dv_ref, near, far, d_memory, held, sem):
    step = pl.program_id(0)
    moves = [(held, 2, 4, False)]

    @pl.when(step == 0)
    def prepare():
        start_fetch(facts[3], near, far, moves, sem)
        wait_fetch(moves, sem)

    @pl.when(step < blocks_of(facts[2]))
    def live():
        d_memory[...] = (nn(held[0], dk_ref[...]) + nn(held[1], dv_ref[...])).T

    @pl.when(step >= blocks_of(facts[2]))
    def blank():
        d_memory[...] = jnp.zeros_like(d_memory)


def self_backward_kernel(
    facts, q_ref, k_ref, v_ref, mix, sums_ref, dself, dq_ref, dk_ref, dv_ref, key_sum, value_sum
):
    head = pl.program_id(0)
    count = blocks_of(facts[1])
    for wanted in range(1, q_ref.shape[1] // STEP + 1):

        @pl.when(count == wanted)
        def attend():
            attend_backward(
                q_ref, k_ref, v_ref, mix, sums_ref, head, dself, dq_ref, dk_ref, dv_ref,
                key_sum, value_sum, None, wanted, wanted * STEP,
            )


def self_finish_kernel(
    facts, q_ref, k_ref, v_ref, mix, sums_ref, dself, token_t, dq_one, dk_one, dv_one,
    rows_ffn, rows_cross, near, far, columns,
    grads, keep, send, g_rows,
    key_sum, value_sum, sum_qkv, made_low, made_rows, held, sem, sem_out
):
    step_at = pl.program_id(0)
    last = pl.num_programs(0) - 1
    head = step_at + HEADS // 2
    head_dim, length = q_ref.shape
    width = token_t.shape[0]
    half = width // 2
    count = blocks_of(facts[1])
    moves = [(held, 0, 3, False)]

    @pl.when(step_at == 0)
    def prepare():
        start_fetch(facts[3], near, far, moves, sem)

    def place(part):
        start = pl.multiple_of(part * half + step_at * head_dim, head_dim)
        return grads.at[pl.ds(start, head_dim)]

    for wanted in range(1, length // STEP + 1):

        @pl.when((step_at < last) & (count == wanted))
        def attend():
            attend_backward(
                q_ref, k_ref, v_ref, mix, sums_ref, head, dself,
                place(0), place(1), place(2), key_sum, value_sum, None, wanted, wanted * STEP,
            )

    @pl.when(step_at == last)
    def weights():
        embed = jnp.where(facts[0] == 1, columns[:, 14:15], columns[:, 13:14])
        g_rows[...] = jnp.zeros_like(g_rows)

        def add(step):
            span = block(step)
            shared = (token_t[:, span].astype(full) + embed).astype(low)
            for part, early in enumerate((dq_one, dk_one, dv_one)):
                left = early[:, span]
                right = grads[part * half : (part + 1) * half, span]
                g_rows[part : part + 1, :half] += token_total(left)
                g_rows[part : part + 1, half:] += token_total(right)
                gather_into(step == 0, sum_qkv.at[part, :, :half], nt(shared, left))
                gather_into(step == 0, sum_qkv.at[part, :, half:], nt(shared, right))

        for step in range(length // STEP):
            pl.when(step < count)(lambda: add(step))
        made_low[...] = sum_qkv[...].astype(low)
        stores = [(made_low, 0, 3, False)]
        start_store(facts[3], keep, send, stores, sem_out)
        wait_fetch(moves, sem)
        total = rows_cross[5:6]
        for part in range(3):
            pieces = jnp.concatenate(
                [*split_three(g_rows[part : part + 1]), jnp.zeros((AUG - 3, width), low)], 0
            )
            total = total + jnp.sum(nt(pieces, held[part]), axis=0, keepdims=True)
        g_rows[3:4] = jnp.where(facts[0] == 1, 0.0, total)
        g_rows[4:5] = jnp.where(facts[0] == 1, total, 0.0)
        picks = [
            g_rows[0:1], g_rows[2:3], rows_cross[2:3], rows_cross[0:1], rows_cross[1:2],
            rows_ffn[5:6], rows_ffn[4:5], rows_cross[3:4], rows_ffn[6:7], rows_ffn[7:8],
            rows_cross[4:5], rows_ffn[8:9], rows_ffn[9:10], g_rows[3:4], g_rows[4:5],
            *[rows_ffn[part : part + 1] for part in range(4)],
        ]
        share = len(picks) * width // made_rows.shape[0]
        for owner in range(made_rows.shape[0]):
            row, start = divmod(owner * share, width)
            stop = min(start + share, width)
            pieces = [picks[row][:, start:stop]]
            if stop - start < share:
                pieces.append(picks[row + 1][:, : share - (stop - start)])
            pieces.append(jnp.zeros((1, width - share), full))
            line = jnp.concatenate(pieces, 1)
            made_rows[owner, 0] = jnp.concatenate(
                [line, jnp.zeros((UNIT - 1, width), full)], 0
            ).astype(low)
        more = [(made_rows, 3, 4, True)]
        start_store(facts[3], keep, send, more, sem)
        wait_fetch(stores, sem_out)
        wait_fetch(more, sem)


def token_grad_kernel(
    facts, dq_one, dk_one, dv_one, grads, dr_one, near, far, d_tokens, held, sem
):
    step = pl.program_id(0)
    width = dr_one.shape[0]
    moves = [(held, 0, 3, False)]

    @pl.when(step == 0)
    def prepare():
        start_fetch(facts[3], near, far, moves, sem)
        wait_fetch(moves, sem)

    @pl.when(step < blocks_of(facts[1]))
    def live():
        made = dr_one[...]
        half = width // 2
        for part, early in enumerate((dq_one, dk_one, dv_one)):
            both = jnp.concatenate([early[...], grads[part * half : (part + 1) * half, :]], 0)
            made = made + nn(held[part], both)
        d_tokens[...] = made.T

    @pl.when(step >= blocks_of(facts[1]))
    def blank():
        d_tokens[...] = jnp.zeros_like(d_tokens)


def in_place(shape):
    return pl.BlockSpec(shape, lambda step: (0,) * len(shape))


def columns_block(rows, span=STEP):
    return pl.BlockSpec((rows, span), lambda step: (0, step))


def rows_block(columns, span=STEP):
    return pl.BlockSpec((span, columns), lambda step: (step, 0))


def first_columns(rows, count):
    return pl.BlockSpec((rows, STEP), lambda step: (0, jnp.minimum(step, count - 1)))


def first_rows(columns, count):
    return pl.BlockSpec((STEP, columns), lambda step: (jnp.minimum(step, count - 1), 0))


def later_head(head_dim, columns, count):
    return pl.BlockSpec((head_dim, columns), lambda step: (jnp.maximum(step - count, 0), 0))


def head_block(head_dim, columns, first=0, count=HEADS):
    return pl.BlockSpec(
        (head_dim, columns), lambda step: (first + jnp.minimum(step, count - 1), 0)
    )


def call(kernel, steps, ins, outs, scratch, cost, room=0):
    room = room or (56 if kernel in (self_forward_kernel, cross_forward_kernel) else 20)
    def spec_of(spec, array=None):
        if isinstance(array, list):
            return [spec_of(spec)] * len(array)
        return pl.BlockSpec(memory_space=pl.ANY) if spec is None else spec

    return pl.pallas_call(
        kernel,
        grid=(steps,),
        out_shape=[jax.ShapeDtypeStruct(shape, dtype) for shape, dtype, spec in outs],
        in_specs=[spec_of(spec, array) for array, spec in ins],
        out_specs=[spec_of(spec) for shape, dtype, spec in outs],
        scratch_shapes=scratch,
        compiler_params=pltpu.CompilerParams(
            vmem_limit_bytes=room * 2**20, dimension_semantics=("arbitrary",)
        ),
        cost_estimate=pl.CostEstimate(
            flops=int(cost * 1.0e9), bytes_accessed=4 * 2**20, transcendentals=0
        ),
        name=kernel.__name__,
    )(*[array for array, spec in ins])


SIDES = (0, 2, 4, 6)
DEPTHS = (0, 8, 16, 24)


def swap(values, mask):
    count = lax.axis_size("dp")
    return lax.ppermute(values, "dp", [(spot, spot ^ mask) for spot in range(count)])


def spread_along(held, masks):
    return [held] + [swap(held, mask) for mask in masks[1:]]


def after(value, *earlier):
    return lax.optimization_barrier((value, earlier))[0]


class Staged:
    def deep(self, piece, late=0):
        return spread_along(piece[None], DEPTHS)

    def wide(self, held):
        return spread_along(held, SIDES)

    def both(self, held):
        return [held], [swap(held, 1)]

    def join(self, parts):
        return jnp.concatenate(parts, 0)

    def add_core(self, keep, send, late=0):
        return keep, swap(send, 1)

    def sum_core(self, pair):
        keep, got = pair
        sums = [
            keep[4 * side : 4 * side + 4].astype(full) + got[4 * side : 4 * side + 4].astype(full)
            for side in range(4)
        ]
        return [sums[0]] + [part.astype(keep.dtype) for part in sums[1:]]

    def add_wide(self, sums):
        return [sums[0]] + [swap(sums[side], SIDES[side]) for side in range(1, 4)]

    def total(self, parts):
        total = parts[0]
        for part in parts[1:]:
            total = total + part.astype(full)
        return total

    def sum_wide(self, parts):
        wire = parts[1].dtype
        total = self.total(parts)
        return [total[0]] + [total[deep].astype(wire) for deep in range(1, 4)]

    def add_deep(self, sums):
        return [sums[0]] + [swap(sums[deep], DEPTHS[deep]) for deep in range(1, 4)]

    def finish(self, parts):
        return self.total(parts)


class Plain:
    def __init__(self, devices, chunks, rows, width, order):
        self.devices, self.chunks, self.rows, self.width = devices, chunks, rows, width
        self.order = order

    def arrange(self, gathered, by_row):
        group = self.devices // self.chunks
        split = gathered.reshape(self.chunks, group, -1, self.rows, self.width)
        if not by_row:
            split = split.transpose(0, 2, 1, 3, 4)
        return split.reshape(self.chunks, -1, self.width)

    def spread(self, ordered, by_row):
        group = self.devices // self.chunks
        if by_row:
            return ordered.reshape(self.devices, -1, self.width)
        split = ordered.reshape(self.chunks, -1, group, self.rows, self.width)
        return split.transpose(0, 2, 1, 3, 4).reshape(self.devices, -1, self.width)

    def deep(self, piece, late=0):
        gathered = lax.all_gather(piece, "dp", axis=0)
        plain = piece.shape[0] - late
        ordered = self.arrange(gathered[:, :plain], False)
        if late:
            ordered = jnp.concatenate([ordered, self.arrange(gathered[:, plain:], True)], 1)
        return jnp.take(ordered, jnp.array(self.order), axis=0)

    def wide(self, held):
        return held

    def join(self, held):
        return held

    def both(self, held):
        return [held[: self.chunks // 2]], [held[self.chunks // 2 :]]

    def add_core(self, keep, send, late=0):
        back = [self.order.index(place) for place in range(self.chunks)]
        ordered = jnp.take(jnp.concatenate([keep, send], 0), jnp.array(back), axis=0)
        plain = ordered.shape[1] - late * UNIT
        split = self.spread(ordered[:, :plain], False)
        if late:
            split = jnp.concatenate([split, self.spread(ordered[:, plain:], True)], 1)
        return lax.psum_scatter(split.astype(full), "dp", scatter_dimension=0, tiled=False)

    def sum_core(self, value):
        return value

    def add_wide(self, value):
        return value

    def sum_wide(self, value):
        return value

    def add_deep(self, value):
        return value

    def finish(self, value):
        return value


def body(
    tokens, memory, directions, target_len, memory_len, self_qkv, self_out, cross_query, cross_kv,
    cross_out, ffn_in, ffn_out, vectors, cotangent,
):
    tokens, memory, cotangent = tokens[0], memory[0], cotangent[0]
    length, width = tokens.shape
    others = memory.shape[0]
    devices = lax.axis_size("dp")
    rows = self_out.shape[0] // width
    chunks = width // UNIT
    parts = ffn_in.shape[0] // (rows * width)
    hidden = parts * width
    head_dim = width // HEADS
    order = place_order()
    order = order + [place ^ 1 for place in order]
    nearby = devices == chunks == len(order)
    me = lax.axis_index("dp") if nearby else jnp.int32(0)
    ways = Staged() if nearby else Plain(devices, chunks, rows, width, order)

    def stack(flat, by_row=False):
        if by_row:
            return flat
        return flat.reshape(rows, -1, width).transpose(1, 0, 2).reshape(-1)

    def piece_of(*flats):
        return jnp.concatenate(flats).reshape(-1, width)

    facts = jnp.concatenate([directions, target_len, memory_len, me[None]])
    one = stack(self_qkv)
    if nearby:
        one = jnp.concatenate([one, jnp.pad(vectors, (0, 8 * width - vectors.shape[0]))])
    one = piece_of(one)
    two = piece_of(*[stack(w) for w in (self_out, cross_query, cross_kv, cross_out)])
    if nearby:
        first = one.shape[0]
        slabs = ways.deep(jnp.concatenate([one, two], 0))
        one = ways.join([slab[:, :first] for slab in slabs])
        three = ways.deep(after(piece_of(stack(ffn_in), stack(ffn_out, True)), one))
        one = ways.wide(one)
        two = ways.join([slab[:, first:] for slab in slabs])
        one = [one[0], *after(one[1:], three[1:])]
        one = one, [swap(part, 1) for part in one]
    else:
        one, two = ways.both(ways.deep(one)), ways.deep(two)
        three = ways.deep(piece_of(stack(ffn_in), stack(ffn_out, True)), parts * rows)
    two = after(two, one)
    two_sent = ways.wide(two)

    if nearby:
        held = jnp.concatenate(
            [part[:, 3 * UNIT, : vectors.shape[0]] for side in one for part in side], 0
        )
        wanted = jnp.bitwise_xor(me, lax.iota(jnp.int32, chunks))
        choice = (wanted[:, None] == jnp.array(order, jnp.int32)[None, :]).astype(full)
        vector_full = lax.dot(choice.astype(low), held, preferred_element_type=full)
    else:
        vector_full = lax.all_gather(vectors, "dp", axis=0, tiled=True).astype(full)
    vector_rows = vector_full.reshape(-1, width)

    smem = pl.BlockSpec(memory_space=pltpu.SMEM)
    facts = (facts, smem)
    vector_rows = (vector_rows, in_place(vector_rows.shape))
    sem = pltpu.SemaphoreType.DMA
    vm = pltpu.VMEM
    head_dim = width // HEADS
    steps = length // STEP
    along = columns_block(width)
    by_head, by_head_other = head_block(head_dim, length), head_block(head_dim, others)
    eight = in_place((8, width))

    def units(count):
        return vm((count, width, width), low)

    def stored(count):
        return ((chunks // 2, count * UNIT, width), low, None)

    def remote(pair):
        return [(pair[0], None), (pair[1], None)]

    low_t, full_t = ((width, length), low), ((width, length), full)
    low_m = ((width, others), low)
    sums = ((HEADS, length), full, in_place((HEADS, length)))

    all_t, all_m = vm((width, length), low), vm((width, others), low)
    begin, begin_rows = first_columns(width, steps), first_rows(width, steps)
    token_t, q, k, v, mix, sums_one, columns = call(
        self_forward_kernel, steps + HEADS,
        [facts, (after(tokens, two), begin_rows), *remote(one), vector_rows],
        [(*low_t, begin)] * 4 + [(*full_t, later_head(head_dim, length, steps)), sums,
         ((width, 128), full, in_place((width, 128)))],
        [all_t, all_t, all_t, units(3), sem, pltpu.SMEM((2,), full)],
        8.0,
    )
    columns = (columns, in_place((width, 128)))
    three = ways.join(after(three, sums_one))
    two = ways.both(ways.join(after(two_sent, sums_one)))
    three_sent = ways.wide(three)
    hat, scale, memory_t, cq, ck, cv, cross_mix, sums_two = call(
        cross_forward_kernel, steps + HEADS,
        [facts, (after(token_t, three), begin), (memory, begin_rows), (mix, begin), *remote(two),
         columns],
        [(*full_t, begin), ((8, length), full, first_columns(8, steps)), (*low_m, begin),
         (*low_t, begin), (*low_m, begin), (*low_m, begin),
         (*full_t, later_head(head_dim, length, steps)), sums],
        [all_t, all_m, all_m, units(4), sem, vm((AUG, others), low), pltpu.SMEM((2,), full)],
        12.0,
    )
    three = ways.both(ways.join(after(three_sent, sums_two)))
    whole_t = in_place((width, length))
    out, dr_two, dcross, keep_three, send_three, g_cross_out, rows_ffn = call(
        ffn_kernel, 1,
        [facts, (hat, whole_t), (cross_mix, whole_t), (cotangent, None), *remote(two),
         *remote(three), columns],
        [((length, width), low, None), (*full_t, whole_t), (*low_t, whole_t),
         stored(2 * parts), stored(2 * parts),
         ((width, width), low, in_place((width, width))), ((16, width), full, in_place((16, width)))],
        [units(1), units(parts), vm((chunks, parts, UNIT, width), low), units(parts),
         vm((chunks, parts, UNIT, width), low), vm((hidden, length), full),
         vm((hidden, length), low), vm((length, width), low), vm((length, width), low),
         pltpu.SemaphoreType.DMA((5,))],
        20.0,
        44,
    )
    g_three = ways.add_core(keep_three, send_three, parts)
    dcq, dck, dcv = call(
        cross_backward_kernel, HEADS,
        [facts, (cq, by_head), (ck, by_head_other), (cv, by_head_other), (cross_mix, by_head),
         (sums_two, sums[2]), (dcross, by_head)],
        [(*low_t, by_head), (*low_m, by_head_other), (*low_m, by_head_other)],
        [vm((head_dim, others), full), vm((head_dim, others), full), vm((AUG, others), low)],
        16.0,
    )
    g_three = ways.sum_core(after(g_three, dcq))
    dcq = after(dcq, g_three)
    g_three = ways.add_wide(g_three)
    square = vm((width, width), full)
    dr_one, dself, keep_two, send_two, rows_cross = call(
        middle_kernel, steps,
        [facts, (dcq, along), (dck, along), (dcv, along), (dr_two, along), (hat, along),
         (scale, columns_block(8)), (memory_t, along), (mix, along), *remote(two),
         (g_cross_out, in_place((width, width))), columns],
        [(*full_t, along), (*low_t, along), stored(5), stored(5), ((8, width), full, eight)],
        [units(2), units(5), square, square, square, square, vm((3, width, 128), full), sem],
        5.0,
    )
    g_two = ways.add_core(keep_two, send_two)
    g_three = ways.sum_wide(after(g_three, keep_two))
    dself = after(dself, g_three)
    g_three = ways.add_deep(g_three)
    early, late = (head_block(head_dim, length, at, HEADS // 2) for at in (0, HEADS // 2))
    half_t = (width // 2, length)
    dq_one, dk_one, dv_one = call(
        self_backward_kernel, HEADS // 2,
        [facts, (q, early), (k, early), (v, early), (mix, early), (sums_one, sums[2]),
         (dself, early)],
        [(half_t, low, early)] * 3,
        [vm((head_dim, length), full), vm((head_dim, length), full)],
        6.0,
    )
    g_three = ways.finish(after(g_three, dv_one))
    g_two = ways.sum_core(after(g_two, dv_one))
    dself = after(dself, g_two)
    g_two = ways.add_wide(g_two)
    whole = in_place(half_t)
    grads, keep_one, send_one, rows_self = call(
        self_finish_kernel, HEADS // 2 + 1,
        [facts, (q, late), (k, late), (v, late), (mix, late), (sums_one, sums[2]),
         (after(dself, g_three), late), (token_t, in_place((width, length))), (dq_one, whole),
         (dk_one, whole), (dv_one, whole), (rows_ffn, in_place((16, width))),
         (rows_cross, eight), *remote(one), columns],
        [((3 * width // 2, length), low, in_place((3 * width // 2, length))), stored(4), stored(4),
         ((8, width), full, eight)],
        [vm((head_dim, length), full), vm((head_dim, length), full),
         vm((3, width, width), full), units(3), vm((chunks, 1, UNIT, width), low), units(3), sem, sem],
        8.0,
    )
    if not nearby:
        keep_one, send_one = keep_one[:, : 3 * UNIT], send_one[:, : 3 * UNIT]
    g_one = ways.add_core(keep_one, send_one)
    g_two = ways.sum_wide(after(g_two, keep_one))
    g_one = ways.sum_core(after(g_one, g_two))
    grads = after(grads, g_one)
    g_two = ways.add_deep(g_two)
    g_one = ways.add_wide(g_one)
    (d_memory,) = call(
        memory_grad_kernel, steps,
        [facts, (after(dck, grads), along), (dcv, along), *remote(two)],
        [((others, width), full, rows_block(width))],
        [units(2), sem],
        2.0,
    )
    half_along = columns_block(width // 2)
    (d_tokens,) = call(
        token_grad_kernel, steps,
        [facts, (dq_one, half_along), (dk_one, half_along), (dv_one, half_along),
         (grads, columns_block(3 * width // 2)), (dr_one, along), *remote(one)],
        [((length, width), full, rows_block(width))],
        [units(3), sem],
        3.0,
    )
    g_two = ways.finish(after(g_two, d_tokens, d_memory))
    g_one = ways.finish(ways.add_deep(ways.sum_wide(after(g_one, d_tokens, d_memory))))
    if nearby:
        g_vectors = g_one[3 * UNIT, : vectors.shape[0]]
    else:
        g_vectors = jnp.concatenate(
            [
                rows_self[0:1], rows_self[2:3], rows_cross[2:3], rows_cross[0:2], rows_ffn[5:6],
                rows_ffn[4:5], rows_cross[3:4], rows_ffn[6:8], rows_cross[4:5], rows_ffn[8:10],
                rows_self[3:5], rows_ffn[0:4],
            ],
            0,
        ).reshape(-1)
        g_vectors = lax.psum_scatter(g_vectors, "dp", scatter_dimension=0, tiled=True)

    def flat(grad, first, stop):
        piece = grad[first * rows : stop * rows].reshape(stop - first, rows, width)
        return piece.transpose(1, 0, 2).reshape(-1)

    return (
        out[None], d_tokens[None], d_memory[None],
        flat(g_one, 0, 3), flat(g_two, 0, 1), flat(g_two, 1, 2), flat(g_two, 2, 4),
        flat(g_two, 4, 5), flat(g_three, 0, parts), g_three[parts * rows :].reshape(-1), g_vectors,
    )


def solution(mesh):
    rows, flat = P("dp", None, None), P("dp")
    return jax.shard_map(
        body,
        mesh=mesh,
        in_specs=(rows, rows) + (flat,) * 11 + (rows,),
        out_specs=(rows,) * 3 + (flat,) * 8,
        check_vma=False,
    )
```

```python
import jax
import jax.numpy as jnp
from jax import lax
from jax.experimental import pallas as pl
from jax.experimental.pallas import tpu as pltpu
from jax.sharding import PartitionSpec as P

HEADS = 8
STEP = 256
PAIR = 2 * STEP
AUG = 16
UNIT = 16
SAFE_SQUARE = 3600.0
mask_fill = -1000000000.0
norm_eps = 1e-05
low = jnp.bfloat16
full = jnp.float32


def contract(left, right, left_dim, right_dim):
    return lax.dot_general(
        left, right, (((left_dim,), (right_dim,)), ((), ())), preferred_element_type=full
    )


def nn(left, right):
    return contract(left, right, 1, 0)


def tn(left, right):
    return contract(left, right, 0, 0)


def nt(left, right):
    return contract(left, right, 1, 1)


def block(index):
    return slice(index * STEP, (index + 1) * STEP)


def blocks_of(length):
    return (length + STEP - 1) // STEP


def split_three(values):
    first = values.astype(low)
    rest = values - first.astype(full)
    second = rest.astype(low)
    third = (rest - second.astype(full)).astype(low)
    return first, second, third


def normalize(values):
    center = jnp.mean(values, axis=0, keepdims=True)
    offsets = values - center
    spread = jnp.mean(offsets * offsets, axis=0, keepdims=True)
    scale = lax.rsqrt(spread + norm_eps)
    return offsets * scale, scale


def norm_backward(grad, hat, scale, gain):
    scaled = grad * gain
    center = jnp.mean(scaled, axis=0, keepdims=True)
    along = jnp.mean(scaled * hat, axis=0, keepdims=True)
    return (scaled - center - hat * along) * scale


def fold_lanes(values):
    total = values[:, :128]
    for start in range(128, values.shape[1], 128):
        total = total + values[:, start : start + 128]
    return total


def lane_total(partial):
    ones = jnp.ones((8, 128), full)
    return lax.dot_general(
        ones,
        partial,
        (((1,), (1,)), ((), ())),
        precision=lax.Precision.HIGHEST,
        preferred_element_type=full,
    )[0:1]


def token_total(values):
    return nt(jnp.ones((AUG, values.shape[1]), low), values)[0:1]


def head_rows(head, head_dim):
    return pl.ds(pl.multiple_of(head * head_dim, head_dim), head_dim)


def square_peak(values, head_dim):
    squares = jnp.square(values.astype(full))
    count = values.shape[0] // head_dim
    return jnp.max(jnp.sum(squares.reshape(count, head_dim, values.shape[1]), axis=1))


def place_order():
    return [side ^ deep for side in (0, 2, 4, 6) for deep in (0, 8, 16, 24)]


def unit_spot(whole, owner, by_row):
    if by_row:
        return whole.at[owner]
    return whole.at[:, pl.ds(pl.multiple_of(owner * UNIT, UNIT), UNIT), :]


def unit_part(buffer, index, first, stop):
    part = buffer.at[index, first * UNIT : stop * UNIT]
    return part.reshape(stop - first, UNIT, buffer.shape[2])


def start_fetch(me, near, far, moves, sem):
    for index, relative in enumerate(place_order()):
        for sources, place in ((near, relative), (far, relative ^ 1)):
            owner = jnp.bitwise_xor(me, place)
            each = sources[0].shape[0]
            for target, first, stop, by_row in moves:
                spot = unit_spot(target, owner, by_row)
                part = unit_part(sources[index // each], index % each, first, stop)
                pltpu.make_async_copy(part, spot, sem).start()


def wait_fetch(moves, sem):
    for target, first, stop, by_row in moves:
        pltpu.make_async_copy(target, target, sem).wait()


def start_store(me, near, far, moves, sem):
    for index, relative in enumerate(place_order()):
        for sink, place in ((near, relative), (far, relative ^ 1)):
            owner = jnp.bitwise_xor(me, place)
            for source, first, stop, by_row in moves:
                spot = unit_spot(source, owner, by_row)
                part = unit_part(sink, index, first, stop)
                pltpu.make_async_copy(spot, part, sem).start()


def clear_from(ref, start):
    rows, columns = ref.shape
    if start < columns:
        ref[:, start:] = jnp.zeros((rows, columns - start), ref.dtype)


def attend_forward(
    q_ref, k_ref, v_ref, mix_ref, sums_ref, head, mask_rows, pairs, keys, shifted
):
    causal = mask_rows is None
    head_dim = q_ref.shape[0]
    key_head = k_ref[:, :keys]
    if not causal:
        key_head = jnp.concatenate([key_head, mask_rows[:, :keys]], 0)
    value_head = jnp.concatenate([v_ref[:, :keys], jnp.ones((AUG, keys), low)], 0)
    for pair in range(pairs):
        columns = slice(pair * PAIR, (pair + 1) * PAIR)
        query = q_ref[:, columns]
        if causal:
            main = pair * PAIR + STEP
            scores = tn(key_head[:, :main], query)
            late = tn(key_head[:, main : main + STEP], query[:, STEP:])
            key_pos = lax.broadcasted_iota(jnp.int32, (STEP, STEP), 0)
            query_pos = lax.broadcasted_iota(jnp.int32, (STEP, STEP), 1)
            allowed = key_pos <= query_pos
            edge = scores[main - STEP :]
            edge = jnp.concatenate(
                [jnp.where(allowed, edge[:, :STEP], mask_fill), edge[:, STEP:]], 1
            )
            scores = edge if main == STEP else jnp.concatenate([scores[: main - STEP], edge], 0)
            late = jnp.where(allowed, late, mask_fill)
        else:
            query = jnp.concatenate([query, jnp.ones((AUG, PAIR), low)], 0)
            scores = tn(key_head, query)
        if shifted:
            highest = jnp.max(scores, axis=0, keepdims=True)
            if causal:
                second = jnp.maximum(highest[:, STEP:], jnp.max(late, axis=0, keepdims=True))
                highest = jnp.concatenate([highest[:, :STEP], second], 1)
                late = late - second
            scores = scores - highest
        powered = jnp.exp(scores).astype(low)
        if causal:
            mixed = nn(value_head[:, :main], powered)
            extra = nn(value_head[:, main : main + STEP], jnp.exp(late).astype(low))
            mixed = jnp.concatenate([mixed[:, :STEP], mixed[:, STEP:] + extra], 1)
        else:
            mixed = nn(value_head, powered)
        total = mixed[head_dim : head_dim + 1]
        mix_ref[:, columns] = mixed[:head_dim] / total
        log_sum = jnp.log(total)
        sums_ref[pl.ds(head, 1), columns] = log_sum + highest if shifted else log_sum
    clear_from(mix_ref, pairs * PAIR)


def attend_backward(
    q_ref, k_ref, v_ref, mix_ref, sums_ref, head, grad_ref, dq_ref, dk_ref, dv_ref,
    key_sum, value_sum, mask_rows, steps, keys
):
    causal = mask_rows is None
    length = steps * STEP
    scale = q_ref.shape[0] ** (-0.5)
    key_head = k_ref[:, :keys]
    value_head = v_ref[:, :keys]
    query = q_ref[:, :length]
    grad = grad_ref[:, :length]
    inner = jnp.sum(grad.astype(full) * mix_ref[:, :length], axis=0, keepdims=True)
    one = jnp.ones((1, length), low)
    blank = jnp.zeros((AUG - 4, length), low)
    query_aug = jnp.concatenate(
        [query, *split_three(sums_ref[pl.ds(head, 1), :length]), one, blank], 0
    )
    grad_aug = jnp.concatenate([grad, *split_three(inner), one, blank], 0)
    minus = jnp.full((3, keys), -1.0, low)
    key_blank = jnp.zeros((AUG - 3, keys), low)
    value_aug = jnp.concatenate([value_head, minus, key_blank], 0)
    if causal:
        key_aug = jnp.concatenate([key_head, minus, key_blank], 0)
    else:
        key_aug = jnp.concatenate([key_head, minus, mask_rows[0:1, :keys], key_blank[1:]], 0)
    for step in range(steps):
        span = block(step)
        count = (step + 1) * STEP if causal else keys
        scores = tn(query_aug[:, span], key_aug[:, :count])
        chances = jnp.exp(scores)
        if causal:
            query_pos = lax.broadcasted_iota(jnp.int32, (STEP, STEP), 0)
            key_pos = lax.broadcasted_iota(jnp.int32, (STEP, STEP), 1)
            edge = jnp.where(key_pos <= query_pos, chances[:, count - STEP :], 0.0)
            chances = (
                edge if count == STEP
                else jnp.concatenate([chances[:, : count - STEP], edge], 1)
            )
        grad_chances = tn(grad_aug[:, span], value_aug[:, :count])
        grad_scores = (chances * grad_chances).astype(low)
        to_value = nn(grad[:, span], chances.astype(low))
        to_key = nn(query[:, span], grad_scores)
        to_query = nt(key_head[:, :count], grad_scores)
        dq_ref[:, span] = (to_query * scale).astype(low)
        if step == 0:
            value_sum[:, :count] = to_value
            key_sum[:, :count] = to_key
        elif causal:
            old = count - STEP
            value_sum[:, :old] += to_value[:, :old]
            key_sum[:, :old] += to_key[:, :old]
            value_sum[:, old:count] = to_value[:, old:]
            key_sum[:, old:count] = to_key[:, old:]
        else:
            value_sum[:, :count] += to_value
            key_sum[:, :count] += to_key
    dv_ref[:, :keys] = value_sum[:, :keys].astype(low)
    dk_ref[:, :keys] = key_sum[:, :keys].astype(low)
    clear_from(dq_ref, length)
    clear_from(dk_ref, keys)
    clear_from(dv_ref, keys)


def add_to(first, rows, index, value):
    if first:
        rows[index : index + 1] = value
    else:
        rows[index : index + 1] += value


def gather_into(first, ref, value):
    if first:
        ref[...] = value
    else:
        ref[...] += value


def self_forward_kernel(
    facts, tokens, near, far, vector_rows, token_t, q_ref, k_ref, v_ref, mix_ref, sums_ref, columns,
    q_all, k_all, v_all, held, sem, peaks
):
    step = pl.program_id(0)
    width, length = q_all.shape
    blocks = length // STEP
    head_dim = width // HEADS
    moves = [(held, 0, 3, False)]

    @pl.when(step == 0)
    def prepare():
        start_fetch(facts[3], near, far, moves, sem)
        peaks[0] = 0.0
        peaks[1] = 0.0
        rest = jnp.zeros((128 - vector_rows.shape[0], width), full)
        columns[...] = jnp.concatenate([vector_rows[...], rest], 0).T
        wait_fetch(moves, sem)

    @pl.when((step < blocks) & (step < blocks_of(facts[1])))
    def live():
        embed = jnp.where(facts[0] == 1, columns[:, 14:15], columns[:, 13:14])
        flipped = tokens[...].T
        token_t[...] = flipped
        shared = (flipped.astype(full) + embed).astype(low)
        query = (tn(held[0], shared) + columns[:, 0:1]).astype(low) * (head_dim ** (-0.5))
        key = tn(held[1], shared).astype(low)
        value = (tn(held[2], shared) + columns[:, 1:2]).astype(low)
        spot = pl.ds(pl.multiple_of(step * STEP, STEP), STEP)
        for ref, all_ref, made in (
            (q_ref, q_all, query), (k_ref, k_all, key), (v_ref, v_all, value)
        ):
            ref[...] = made
            all_ref[:, spot] = made
        peaks[0] = jnp.maximum(peaks[0], square_peak(query, head_dim))
        peaks[1] = jnp.maximum(peaks[1], square_peak(key, head_dim))

    @pl.when((step < blocks) & (step >= blocks_of(facts[1])))
    def dead():
        spot = pl.ds(pl.multiple_of(step * STEP, STEP), STEP)
        token_t[...] = jnp.zeros_like(token_t)
        for ref, all_ref in ((q_ref, q_all), (k_ref, k_all), (v_ref, v_all)):
            ref[...] = jnp.zeros_like(ref)
            all_ref[:, spot] = jnp.zeros_like(ref)

    head = step - blocks
    safe = peaks[0] * peaks[1] <= SAFE_SQUARE
    pairs = (blocks_of(facts[1]) + 1) // 2
    rows = pl.ds(pl.multiple_of(jnp.maximum(head, 0) * head_dim, head_dim), head_dim)
    for wanted in range(1, length // PAIR + 1):
        for shifted in (False, True):

            @pl.when((step >= blocks) & (pairs == wanted) & (safe != shifted))
            def attend():
                attend_forward(
                    q_all.at[rows], k_all.at[rows], v_all.at[rows], mix_ref, sums_ref, head, None,
                    wanted, wanted * PAIR, shifted,
                )


def fill_mask(mask_ref, visible):
    position = lax.broadcasted_iota(jnp.int32, mask_ref.shape, 1)
    row = lax.broadcasted_iota(jnp.int32, mask_ref.shape, 0)
    hidden = (position >= visible) & (row == 0)
    mask_ref[...] = jnp.where(hidden, mask_fill, 0.0).astype(low)


def cross_forward_kernel(
    facts, token_t, memory, mix, near, far, columns,
    hat_ref, scale_ref, memory_t, q_ref, k_ref, v_ref, mix_ref, sums_ref,
    q_all, k_all, v_all, held, sem, mask_ref, peaks
):
    step = pl.program_id(0)
    width, length = q_all.shape
    others = k_all.shape[1]
    blocks = max(length, others) // STEP
    head_dim = width // HEADS
    moves = [(held, 0, 4, False)]
    spot = pl.ds(pl.multiple_of(jnp.minimum(step, blocks - 1) * STEP, STEP), STEP)

    @pl.when(step == 0)
    def prepare():
        start_fetch(facts[3], near, far, moves, sem)
        fill_mask(mask_ref, facts[2])
        peaks[0] = 0.0
        peaks[1] = 0.0
        wait_fetch(moves, sem)

    @pl.when((step < blocks) & (step < blocks_of(facts[2])))
    def encode():
        flipped = memory[...].T
        memory_t[...] = flipped
        key = tn(held[2], flipped).astype(low)
        value = (tn(held[3], flipped) + columns[:, 4:5]).astype(low)
        k_ref[...] = key
        v_ref[...] = value
        k_all[:, spot] = key
        v_all[:, spot] = value
        peaks[1] = jnp.maximum(peaks[1], square_peak(key, head_dim))

    @pl.when((step < blocks) & (step < blocks_of(facts[1])))
    def first():
        embed = jnp.where(facts[0] == 1, columns[:, 14:15], columns[:, 13:14])
        started = token_t[...].astype(full) + embed
        total = started + tn(held[0], mix[...].astype(low)) + columns[:, 2:3]
        hat, scale = normalize(total)
        hat_ref[...] = hat
        scale_ref[...] = jnp.broadcast_to(scale, scale_ref.shape)
        shared = (hat * columns[:, 7:8] + columns[:, 10:11]).astype(low)
        query = (tn(held[1], shared) + columns[:, 3:4]).astype(low) * (head_dim ** (-0.5))
        q_ref[...] = query
        q_all[:, spot] = query
        peaks[0] = jnp.maximum(peaks[0], square_peak(query, head_dim))

    @pl.when((step < blocks) & (step >= blocks_of(facts[2])))
    def hidden():
        memory_t[...] = jnp.zeros_like(memory_t)
        for ref, all_ref in ((k_ref, k_all), (v_ref, v_all)):
            ref[...] = jnp.zeros_like(ref)
            all_ref[:, spot] = jnp.zeros_like(ref)

    @pl.when((step < blocks) & (step >= blocks_of(facts[1])))
    def dead():
        hat_ref[...] = jnp.zeros_like(hat_ref)
        scale_ref[...] = jnp.zeros_like(scale_ref)
        q_ref[...] = jnp.zeros_like(q_ref)
        q_all[:, spot] = jnp.zeros_like(q_ref)

    head = step - blocks
    safe = peaks[0] * peaks[1] <= SAFE_SQUARE
    pairs = (blocks_of(facts[1]) + 1) // 2
    key_count = blocks_of(facts[2])
    rows = pl.ds(pl.multiple_of(jnp.maximum(head, 0) * head_dim, head_dim), head_dim)
    for wanted in range(1, length // PAIR + 1):
        for wanted_keys in range(1, others // STEP + 1):
            for shifted in (False, True):

                @pl.when(
                    (step >= blocks) & (pairs == wanted) & (key_count == wanted_keys)
                    & (safe != shifted)
                )
                def attend():
                    attend_forward(
                        q_all.at[rows], k_all.at[rows], v_all.at[rows], mix_ref, sums_ref, head,
                        mask_ref[...], wanted, wanted_keys * STEP, shifted,
                    )


def gelu_parts(values):
    half = 0.5 * (1.0 + lax.erf(values * (0.5**0.5)))
    bell = jnp.exp(-0.5 * values * values) * 0.3989422804014327
    return values * half, half + values * bell


def ffn_kernel(
    facts, hat_one, cross_mix, cotangent, near_two, far_two, near, far, columns,
    out_ref, dr_ref, dmix_ref, keep, send, g_cross_out, g_rows,
    c_out, f_in, f_out, low_in, low_out, slope, acts, top_ref, result_ref, sems
):
    length, width = top_ref.shape
    parts = f_in.shape[0]
    rows_of = width // parts // UNIT
    moves_two = [(c_out, 4, 5, False)]
    moves_in = [(f_in, 0, parts, False)]
    moves_out = [(f_out, parts, 2 * parts, True)]
    stores_in = [(low_in, 0, parts, False)]
    stores_out = [(low_out, parts, 2 * parts, True)]
    fetch_top = pltpu.make_async_copy(cotangent, top_ref, sems.at[3])
    store_result = pltpu.make_async_copy(result_ref, out_ref, sems.at[4])
    start_fetch(facts[3], near_two, far_two, moves_two, sems.at[0])
    start_fetch(facts[3], near, far, moves_in, sems.at[1])
    start_fetch(facts[3], near, far, moves_out, sems.at[2])
    fetch_top.start()
    g_rows[...] = jnp.zeros_like(g_rows)

    def out_part(part):
        return f_out[part * rows_of : (part + 1) * rows_of].reshape(width, width)

    def live(count):
        span = slice(0, count)
        wait_fetch(moves_two, sems.at[0])
        position = lax.broadcasted_iota(jnp.int32, (1, count), 1)
        valid = (position < facts[1]).astype(full)
        mixed = cross_mix[:, span].astype(low)
        first = hat_one[:, span] * columns[:, 7:8] + columns[:, 10:11]
        total = first + tn(c_out[0], mixed) + columns[:, 5:6]
        hat_two, scale_two = normalize(total)
        second = hat_two * columns[:, 8:9] + columns[:, 11:12]
        shared = second.astype(low)
        third = second + columns[:, 6:7]
        wait_fetch(moves_in, sems.at[1])
        wait_fetch(moves_out, sems.at[2])
        for part in range(parts):
            chunk = slice(part * width, (part + 1) * width)
            raw = tn(f_in[part], shared) + columns[:, 15 + part : 16 + part]
            act, slope_part = gelu_parts(raw)
            slope[chunk, span] = slope_part
            acts[chunk, span] = act.astype(low)
            third = third + tn(out_part(part), acts[chunk, span])
        hat_three, scale_three = normalize(third)
        result = (hat_three * columns[:, 9:10] + columns[:, 12:13]) * valid
        result_ref[span, :] = result.astype(low).T
        if count < length:
            result_ref[count:, :] = jnp.zeros((length - count, width), low)
        store_result.start()
        fetch_top.wait()
        top = top_ref[span, :].T.astype(full) * valid
        g_rows[7:8] = lane_total(fold_lanes(top * hat_three))
        g_rows[9:10] = lane_total(fold_lanes(top))
        grad_third = norm_backward(top, hat_three, scale_three, columns[:, 9:10])
        branch = grad_third.astype(low)
        g_rows[4:5] = token_total(branch)
        grad_second = grad_third
        for part in range(parts):
            chunk = slice(part * width, (part + 1) * width)
            back = nn(out_part(part), branch)
            rows = slice(part * rows_of, (part + 1) * rows_of)
            low_out[rows] = nt(acts[chunk, span], branch).astype(low).reshape(
                rows_of, parts, UNIT, width
            )
            acts[chunk, span] = (back * slope[chunk, span]).astype(low)
        start_store(facts[3], keep, send, stores_out, sems.at[2])
        for part in range(parts):
            chunk = slice(part * width, (part + 1) * width)
            grad_hidden = acts[chunk, span]
            g_rows[part : part + 1] = token_total(grad_hidden)
            low_in[part] = nt(shared, grad_hidden).astype(low)
            grad_second = grad_second + nn(f_in[part], grad_hidden)
        start_store(facts[3], keep, send, stores_in, sems.at[1])
        g_rows[6:7] = lane_total(fold_lanes(grad_second * hat_two))
        g_rows[8:9] = lane_total(fold_lanes(grad_second))
        grad_two = norm_backward(grad_second, hat_two, scale_two, columns[:, 8:9])
        dr_ref[:, span] = grad_two
        branch_two = grad_two.astype(low)
        g_rows[5:6] = token_total(branch_two)
        g_cross_out[...] = nt(mixed, branch_two).astype(low)
        dmix_ref[:, span] = nn(c_out[0], branch_two).astype(low)

    live(length)
    wait_fetch(stores_out, sems.at[2])
    wait_fetch(stores_in, sems.at[1])
    store_result.wait()


def cross_backward_kernel(
    facts, q_ref, k_ref, v_ref, cross_mix, sums_ref, dmix, dq_ref, dk_ref, dv_ref,
    key_sum, value_sum, mask_ref
):
    head = pl.program_id(0)
    length = q_ref.shape[1]
    others = k_ref.shape[1]
    count = blocks_of(facts[1])
    key_count = blocks_of(facts[2])

    @pl.when(head == 0)
    def prepare():
        fill_mask(mask_ref, facts[2])

    for wanted in range(1, length // STEP + 1):
        for wanted_keys in range(1, others // STEP + 1):

            @pl.when((count == wanted) & (key_count == wanted_keys))
            def attend():
                attend_backward(
                    q_ref, k_ref, v_ref, cross_mix, sums_ref, head, dmix,
                    dq_ref, dk_ref, dv_ref, key_sum, value_sum, mask_ref[...],
                    wanted, wanted_keys * STEP,
                )


def middle_kernel(
    facts, dq_ref, dk_ref, dv_ref, dr_two, hat_one, scale_one, memory_t, mix, near, far,
    g_cross_out, columns, dr_ref, dself, keep, send, g_rows,
    held, made_low, sum_query, sum_key, sum_value, sum_out, lanes, sem
):
    step = pl.program_id(0)
    moves = [(held, 0, 2, False)]

    @pl.when(step == 0)
    def prepare():
        start_fetch(facts[3], near, far, moves, sem)
        g_rows[...] = jnp.zeros_like(g_rows)
        lanes[...] = jnp.zeros_like(lanes)
        wait_fetch(moves, sem)

    span = dq_ref.shape[1]

    def encode(initial):
        add_to(initial, g_rows, 1, token_total(dv_ref[...]))
        gather_into(initial, sum_key, nt(memory_t[...], dk_ref[...]))
        gather_into(initial, sum_value, nt(memory_t[...], dv_ref[...]))

    def first(initial):
        hat = hat_one[...]
        shared = (hat * columns[:, 7:8] + columns[:, 10:11]).astype(low)
        grad_query = dq_ref[...]
        add_to(initial, g_rows, 0, token_total(grad_query))
        gather_into(initial, sum_query, nt(shared, grad_query))
        grad = dr_two[...] + nn(held[1], grad_query)
        lanes[0] += fold_lanes(grad * hat)
        lanes[1] += fold_lanes(grad)
        grad_one = norm_backward(grad, hat, scale_one[0:1], columns[:, 7:8])
        dr_ref[...] = grad_one
        lanes[2] += fold_lanes(grad_one)
        branch = grad_one.astype(low)
        add_to(initial, g_rows, 2, token_total(branch))
        gather_into(initial, sum_out, nt(mix[...].astype(low), branch))
        dself[...] = nn(held[0], branch).astype(low)

    pl.when(step == 0)(lambda: encode(True))
    pl.when((step > 0) & (step * span < facts[2]))(lambda: encode(False))
    pl.when(step == 0)(lambda: first(True))
    pl.when((step > 0) & (step * span < facts[1]))(lambda: first(False))

    @pl.when((step > 0) & (step * span >= facts[1]))
    def dead():
        dr_ref[...] = jnp.zeros_like(dr_ref)
        dself[...] = jnp.zeros_like(dself)


    @pl.when(step == pl.num_programs(0) - 1)
    def close():
        made_low[0] = sum_out[...].astype(low)
        made_low[1] = sum_query[...].astype(low)
        made_low[2] = sum_key[...].astype(low)
        made_low[3] = sum_value[...].astype(low)
        made_low[4] = g_cross_out[...]
        stores = [(made_low, 0, 5, False)]
        start_store(facts[3], keep, send, stores, sem)
        g_rows[3:4] = lane_total(lanes[0])
        g_rows[4:5] = lane_total(lanes[1])
        g_rows[5:6] = lane_total(lanes[2])
        wait_fetch(stores, sem)


def memory_grad_kernel(facts, dk_ref, dv_ref, near, far, d_memory, held, sem):
    step = pl.program_id(0)
    moves = [(held, 2, 4, False)]

    @pl.when(step == 0)
    def prepare():
        start_fetch(facts[3], near, far, moves, sem)
        wait_fetch(moves, sem)

    @pl.when(step < blocks_of(facts[2]))
    def live():
        d_memory[...] = (nn(held[0], dk_ref[...]) + nn(held[1], dv_ref[...])).T

    @pl.when(step >= blocks_of(facts[2]))
    def blank():
        d_memory[...] = jnp.zeros_like(d_memory)


def self_backward_kernel(
    facts, q_ref, k_ref, v_ref, mix, sums_ref, dself, dq_ref, dk_ref, dv_ref, key_sum, value_sum
):
    head = pl.program_id(0)
    count = blocks_of(facts[1])
    for wanted in range(1, q_ref.shape[1] // STEP + 1):

        @pl.when(count == wanted)
        def attend():
            attend_backward(
                q_ref, k_ref, v_ref, mix, sums_ref, head, dself, dq_ref, dk_ref, dv_ref,
                key_sum, value_sum, None, wanted, wanted * STEP,
            )


def self_finish_kernel(
    facts, q_ref, k_ref, v_ref, mix, sums_ref, dself, token_t, dq_one, dk_one, dv_one,
    rows_ffn, rows_cross, near, far, columns,
    grads, keep, send, g_rows,
    key_sum, value_sum, made_low, made_rows, held, sem, sem_out
):
    step_at = pl.program_id(0)
    last = pl.num_programs(0) - 1
    head = step_at + HEADS // 2
    head_dim, length = q_ref.shape
    width = token_t.shape[0]
    half = width // 2
    count = blocks_of(facts[1])
    moves = [(held, 0, 3, False)]

    @pl.when(step_at == 0)
    def prepare():
        start_fetch(facts[3], near, far, moves, sem)

    def place(part):
        start = pl.multiple_of(part * half + step_at * head_dim, head_dim)
        return grads.at[pl.ds(start, head_dim)]

    for wanted in range(1, length // STEP + 1):

        @pl.when((step_at < last) & (count == wanted))
        def attend():
            attend_backward(
                q_ref, k_ref, v_ref, mix, sums_ref, head, dself,
                place(0), place(1), place(2), key_sum, value_sum, None, wanted, wanted * STEP,
            )

    @pl.when(step_at == last)
    def weights():
        embed = jnp.where(facts[0] == 1, columns[:, 14:15], columns[:, 13:14])
        g_rows[...] = jnp.zeros_like(g_rows)

        shared = (token_t[...].astype(full) + embed).astype(low)
        for part, early in enumerate((dq_one, dk_one, dv_one)):
            both = jnp.concatenate([early[...], grads[part * half : (part + 1) * half, :]], 0)
            g_rows[part : part + 1] = token_total(both)
            made_low[part] = nt(shared, both).astype(low)
        stores = [(made_low, 0, 3, False)]
        start_store(facts[3], keep, send, stores, sem_out)
        wait_fetch(moves, sem)
        total = rows_cross[5:6]
        for part in range(3):
            pieces = jnp.concatenate(
                [*split_three(g_rows[part : part + 1]), jnp.zeros((AUG - 3, width), low)], 0
            )
            total = total + jnp.sum(nt(pieces, held[part]), axis=0, keepdims=True)
        g_rows[3:4] = jnp.where(facts[0] == 1, 0.0, total)
        g_rows[4:5] = jnp.where(facts[0] == 1, total, 0.0)
        picks = [
            g_rows[0:1], g_rows[2:3], rows_cross[2:3], rows_cross[0:1], rows_cross[1:2],
            rows_ffn[5:6], rows_ffn[4:5], rows_cross[3:4], rows_ffn[6:7], rows_ffn[7:8],
            rows_cross[4:5], rows_ffn[8:9], rows_ffn[9:10], g_rows[3:4], g_rows[4:5],
            *[rows_ffn[part : part + 1] for part in range(4)],
        ]
        share = len(picks) * width // made_rows.shape[0]
        for owner in range(made_rows.shape[0]):
            row, start = divmod(owner * share, width)
            stop = min(start + share, width)
            pieces = [picks[row][:, start:stop]]
            if stop - start < share:
                pieces.append(picks[row + 1][:, : share - (stop - start)])
            pieces.append(jnp.zeros((1, width - share), full))
            line = jnp.concatenate(pieces, 1)
            made_rows[owner, 0] = jnp.concatenate(
                [line, jnp.zeros((UNIT - 1, width), full)], 0
            ).astype(low)
        more = [(made_rows, 3, 4, True)]
        start_store(facts[3], keep, send, more, sem)
        wait_fetch(stores, sem_out)
        wait_fetch(more, sem)


def token_grad_kernel(
    facts, dq_one, dk_one, dv_one, grads, dr_one, near, far, d_tokens, held, sem
):
    step = pl.program_id(0)
    width = dr_one.shape[0]
    moves = [(held, 0, 3, False)]

    @pl.when(step == 0)
    def prepare():
        start_fetch(facts[3], near, far, moves, sem)
        wait_fetch(moves, sem)

    @pl.when(step < blocks_of(facts[1]))
    def live():
        made = dr_one[...]
        half = width // 2
        for part, early in enumerate((dq_one, dk_one, dv_one)):
            both = jnp.concatenate([early[...], grads[part * half : (part + 1) * half, :]], 0)
            made = made + nn(held[part], both)
        d_tokens[...] = made.T

    @pl.when(step >= blocks_of(facts[1]))
    def blank():
        d_tokens[...] = jnp.zeros_like(d_tokens)


def in_place(shape):
    return pl.BlockSpec(shape, lambda step: (0,) * len(shape))


def columns_block(rows, span=STEP):
    return pl.BlockSpec((rows, span), lambda step: (0, step))


def rows_block(columns, span=STEP):
    return pl.BlockSpec((span, columns), lambda step: (step, 0))


def first_columns(rows, count):
    return pl.BlockSpec((rows, STEP), lambda step: (0, jnp.minimum(step, count - 1)))


def first_rows(columns, count):
    return pl.BlockSpec((STEP, columns), lambda step: (jnp.minimum(step, count - 1), 0))


def later_head(head_dim, columns, count):
    return pl.BlockSpec((head_dim, columns), lambda step: (jnp.maximum(step - count, 0), 0))


def head_block(head_dim, columns, first=0, count=HEADS):
    return pl.BlockSpec(
        (head_dim, columns), lambda step: (first + jnp.minimum(step, count - 1), 0)
    )


def call(kernel, steps, ins, outs, scratch, cost, room=0):
    room = room or (56 if kernel in (self_forward_kernel, cross_forward_kernel) else 20)
    def spec_of(spec, array=None):
        if isinstance(array, list):
            return [spec_of(spec)] * len(array)
        return pl.BlockSpec(memory_space=pl.ANY) if spec is None else spec

    return pl.pallas_call(
        kernel,
        grid=(steps,),
        out_shape=[jax.ShapeDtypeStruct(shape, dtype) for shape, dtype, spec in outs],
        in_specs=[spec_of(spec, array) for array, spec in ins],
        out_specs=[spec_of(spec) for shape, dtype, spec in outs],
        scratch_shapes=scratch,
        compiler_params=pltpu.CompilerParams(
            vmem_limit_bytes=room * 2**20, dimension_semantics=("arbitrary",)
        ),
        cost_estimate=pl.CostEstimate(
            flops=int(cost * 1.0e9), bytes_accessed=4 * 2**20, transcendentals=0
        ),
        name=kernel.__name__,
    )(*[array for array, spec in ins])


SIDES = (0, 2, 4, 6)
DEPTHS = (0, 8, 16, 24)


def swap(values, mask):
    count = lax.axis_size("dp")
    return lax.ppermute(values, "dp", [(spot, spot ^ mask) for spot in range(count)])


def spread_along(held, masks):
    return [held] + [swap(held, mask) for mask in masks[1:]]


def after(value, *earlier):
    return lax.optimization_barrier((value, earlier))[0]


class Staged:
    def deep(self, piece, late=0):
        return spread_along(piece[None], DEPTHS)

    def wide(self, held):
        return spread_along(held, SIDES)

    def both(self, held):
        return [held], [swap(held, 1)]

    def join(self, parts):
        return jnp.concatenate(parts, 0)

    def cross(self, parts, ready):
        far = [swap(parts[0], 1)]
        parts = [parts[0], *after(parts[1:], ready)]
        return parts, far + [swap(part, 1) for part in parts[1:]]

    def add_core(self, keep, send, late=0):
        return keep, swap(send, 1)

    def sum_core(self, pair):
        keep, got = pair
        sums = [
            keep[4 * side : 4 * side + 4].astype(full) + got[4 * side : 4 * side + 4].astype(full)
            for side in range(4)
        ]
        return [sums[0]] + [part.astype(keep.dtype) for part in sums[1:]]

    def add_wide(self, sums):
        return [sums[0]] + [swap(sums[side], SIDES[side]) for side in range(1, 4)]

    def total(self, parts):
        total = parts[0]
        for part in parts[1:]:
            total = total + part.astype(full)
        return total

    def sum_wide(self, parts):
        wire = parts[1].dtype
        total = self.total(parts)
        return [total[0]] + [total[deep].astype(wire) for deep in range(1, 4)]

    def add_deep(self, sums):
        return [sums[0]] + [swap(sums[deep], DEPTHS[deep]) for deep in range(1, 4)]

    def finish(self, parts):
        return self.total(parts)


class Plain:
    def __init__(self, devices, chunks, rows, width, order):
        self.devices, self.chunks, self.rows, self.width = devices, chunks, rows, width
        self.order = order

    def arrange(self, gathered, by_row):
        group = self.devices // self.chunks
        split = gathered.reshape(self.chunks, group, -1, self.rows, self.width)
        if not by_row:
            split = split.transpose(0, 2, 1, 3, 4)
        return split.reshape(self.chunks, -1, self.width)

    def spread(self, ordered, by_row):
        group = self.devices // self.chunks
        if by_row:
            return ordered.reshape(self.devices, -1, self.width)
        split = ordered.reshape(self.chunks, -1, group, self.rows, self.width)
        return split.transpose(0, 2, 1, 3, 4).reshape(self.devices, -1, self.width)

    def deep(self, piece, late=0):
        gathered = lax.all_gather(piece, "dp", axis=0)
        plain = piece.shape[0] - late
        ordered = self.arrange(gathered[:, :plain], False)
        if late:
            ordered = jnp.concatenate([ordered, self.arrange(gathered[:, plain:], True)], 1)
        return jnp.take(ordered, jnp.array(self.order), axis=0)

    def wide(self, held):
        return held

    def join(self, held):
        return held

    def both(self, held):
        return [held[: self.chunks // 2]], [held[self.chunks // 2 :]]

    def cross(self, held, ready):
        return self.both(held)

    def add_core(self, keep, send, late=0):
        back = [self.order.index(place) for place in range(self.chunks)]
        ordered = jnp.take(jnp.concatenate([keep, send], 0), jnp.array(back), axis=0)
        plain = ordered.shape[1] - late * UNIT
        split = self.spread(ordered[:, :plain], False)
        if late:
            split = jnp.concatenate([split, self.spread(ordered[:, plain:], True)], 1)
        return lax.psum_scatter(split.astype(full), "dp", scatter_dimension=0, tiled=False)

    def sum_core(self, value):
        return value

    def add_wide(self, value):
        return value

    def sum_wide(self, value):
        return value

    def add_deep(self, value):
        return value

    def finish(self, value):
        return value


def body(
    tokens, memory, directions, target_len, memory_len, self_qkv, self_out, cross_query, cross_kv,
    cross_out, ffn_in, ffn_out, vectors, cotangent,
):
    tokens, memory, cotangent = tokens[0], memory[0], cotangent[0]
    length, width = tokens.shape
    others = memory.shape[0]
    devices = lax.axis_size("dp")
    rows = self_out.shape[0] // width
    chunks = width // UNIT
    parts = ffn_in.shape[0] // (rows * width)
    hidden = parts * width
    head_dim = width // HEADS
    order = place_order()
    order = order + [place ^ 1 for place in order]
    nearby = devices == chunks == len(order)
    me = lax.axis_index("dp") if nearby else jnp.int32(0)
    ways = Staged() if nearby else Plain(devices, chunks, rows, width, order)

    def stack(flat, by_row=False):
        if by_row:
            return flat
        return flat.reshape(rows, -1, width).transpose(1, 0, 2).reshape(-1)

    def piece_of(*flats):
        return jnp.concatenate(flats).reshape(-1, width)

    facts = jnp.concatenate([directions, target_len, memory_len, me[None]])
    one = stack(self_qkv)
    if nearby:
        one = jnp.concatenate([one, jnp.pad(vectors, (0, 8 * width - vectors.shape[0]))])
    one = piece_of(one)
    two = piece_of(*[stack(w) for w in (self_out, cross_query, cross_kv, cross_out)])
    if nearby:
        first = one.shape[0]
        slabs = ways.deep(jnp.concatenate([one, two], 0))
        one = ways.join([slab[:, :first] for slab in slabs])
        three = ways.deep(after(piece_of(stack(ffn_in), stack(ffn_out, True)), one))
        one = ways.wide(one)
        two = ways.join([slab[:, first:] for slab in slabs])
        one = [one[0], *after(one[1:], three[1:])]
        one = one, [swap(part, 1) for part in one]
    else:
        one, two = ways.both(ways.deep(one)), ways.deep(two)
        three = ways.deep(piece_of(stack(ffn_in), stack(ffn_out, True)), parts * rows)
    two = after(two, one)
    two_sent = ways.wide(two)

    if nearby:
        held = jnp.concatenate(
            [part[:, 3 * UNIT, : vectors.shape[0]] for side in one for part in side], 0
        )
        wanted = jnp.bitwise_xor(me, lax.iota(jnp.int32, chunks))
        choice = (wanted[:, None] == jnp.array(order, jnp.int32)[None, :]).astype(full)
        vector_full = lax.dot(choice.astype(low), held, preferred_element_type=full)
    else:
        vector_full = lax.all_gather(vectors, "dp", axis=0, tiled=True).astype(full)
    vector_rows = vector_full.reshape(-1, width)

    smem = pl.BlockSpec(memory_space=pltpu.SMEM)
    facts = (facts, smem)
    vector_rows = (vector_rows, in_place(vector_rows.shape))
    sem = pltpu.SemaphoreType.DMA
    vm = pltpu.VMEM
    head_dim = width // HEADS
    steps = length // STEP
    along = columns_block(width)
    by_head, by_head_other = head_block(head_dim, length), head_block(head_dim, others)
    eight = in_place((8, width))

    def units(count):
        return vm((count, width, width), low)

    def stored(count):
        return ((chunks // 2, count * UNIT, width), low, None)

    def remote(pair):
        return [(pair[0], None), (pair[1], None)]

    low_t, full_t = ((width, length), low), ((width, length), full)
    low_m = ((width, others), low)
    sums = ((HEADS, length), full, in_place((HEADS, length)))

    all_t, all_m = vm((width, length), low), vm((width, others), low)
    begin, begin_rows = first_columns(width, steps), first_rows(width, steps)
    token_t, q, k, v, mix, sums_one, columns = call(
        self_forward_kernel, steps + HEADS,
        [facts, (after(tokens, two), begin_rows), *remote(one), vector_rows],
        [(*low_t, begin)] * 4 + [(*full_t, later_head(head_dim, length, steps)), sums,
         ((width, 128), full, in_place((width, 128)))],
        [all_t, all_t, all_t, units(3), sem, pltpu.SMEM((2,), full)],
        8.0,
    )
    columns = (columns, in_place((width, 128)))
    three = ways.join(after(three, sums_one))
    two = ways.cross(two_sent, sums_one)
    three_sent = ways.wide(three)
    hat, scale, memory_t, cq, ck, cv, cross_mix, sums_two = call(
        cross_forward_kernel, steps + HEADS,
        [facts, (after(token_t, three), begin), (memory, begin_rows), (mix, begin), *remote(two),
         columns],
        [(*full_t, begin), ((8, length), full, first_columns(8, steps)), (*low_m, begin),
         (*low_t, begin), (*low_m, begin), (*low_m, begin),
         (*full_t, later_head(head_dim, length, steps)), sums],
        [all_t, all_m, all_m, units(4), sem, vm((AUG, others), low), pltpu.SMEM((2,), full)],
        12.0,
    )
    three = ways.cross(three_sent, sums_two)
    whole_t = in_place((width, length))
    out, dr_two, dcross, keep_three, send_three, g_cross_out, rows_ffn = call(
        ffn_kernel, 1,
        [facts, (hat, whole_t), (cross_mix, whole_t), (cotangent, None), *remote(two),
         *remote(three), columns],
        [((length, width), low, None), (*full_t, whole_t), (*low_t, whole_t),
         stored(2 * parts), stored(2 * parts),
         ((width, width), low, in_place((width, width))), ((16, width), full, in_place((16, width)))],
        [units(1), units(parts), vm((chunks, parts, UNIT, width), low), units(parts),
         vm((chunks, parts, UNIT, width), low), vm((hidden, length), full),
         vm((hidden, length), low), vm((length, width), low), vm((length, width), low),
         pltpu.SemaphoreType.DMA((5,))],
        20.0,
        56,
    )
    g_three = ways.add_core(keep_three, send_three, parts)
    dcq, dck, dcv = call(
        cross_backward_kernel, HEADS,
        [facts, (cq, by_head), (ck, by_head_other), (cv, by_head_other), (cross_mix, by_head),
         (sums_two, sums[2]), (dcross, by_head)],
        [(*low_t, by_head), (*low_m, by_head_other), (*low_m, by_head_other)],
        [vm((head_dim, others), full), vm((head_dim, others), full), vm((AUG, others), low)],
        16.0,
    )
    g_three = ways.sum_core(after(g_three, dcq))
    dcq = after(dcq, g_three)
    g_three = ways.add_wide(g_three)
    square = vm((width, width), full)
    broad = columns_block(width, PAIR)
    dr_one, dself, keep_two, send_two, rows_cross = call(
        middle_kernel, length // PAIR,
        [facts, (dcq, broad), (dck, broad), (dcv, broad), (dr_two, broad), (hat, broad),
         (scale, columns_block(8, PAIR)), (memory_t, broad), (mix, broad), *remote(two),
         (g_cross_out, in_place((width, width))), columns],
        [(*full_t, broad), (*low_t, broad), stored(5), stored(5), ((8, width), full, eight)],
        [units(2), units(5), square, square, square, square, vm((3, width, 128), full), sem],
        5.0,
        30,
    )
    g_two = ways.add_core(keep_two, send_two)
    early, late = (head_block(head_dim, length, at, HEADS // 2) for at in (0, HEADS // 2))
    half_t = (width // 2, length)
    dq_one, dk_one, dv_one = call(
        self_backward_kernel, HEADS // 2,
        [facts, (q, early), (k, early), (v, early), (mix, early), (sums_one, sums[2]),
         (dself, early)],
        [(half_t, low, early)] * 3,
        [vm((head_dim, length), full), vm((head_dim, length), full)],
        6.0,
    )
    g_three = ways.sum_wide(after(g_three, dv_one))
    g_two = ways.sum_core(after(g_two, dv_one))
    dself = after(dself, g_two, g_three)
    g_three = ways.add_deep(g_three)
    g_two = ways.add_wide(g_two)
    whole = in_place(half_t)
    grads, keep_one, send_one, rows_self = call(
        self_finish_kernel, HEADS // 2 + 1,
        [facts, (q, late), (k, late), (v, late), (mix, late), (sums_one, sums[2]),
         (dself, late), (token_t, in_place((width, length))), (dq_one, whole),
         (dk_one, whole), (dv_one, whole), (rows_ffn, in_place((16, width))),
         (rows_cross, eight), *remote(one), columns],
        [((3 * width // 2, length), low, in_place((3 * width // 2, length))), stored(4), stored(4),
         ((8, width), full, eight)],
        [vm((head_dim, length), full), vm((head_dim, length), full),
         units(3), vm((chunks, 1, UNIT, width), low), units(3), sem, sem],
        8.0,
    )
    if not nearby:
        keep_one, send_one = keep_one[:, : 3 * UNIT], send_one[:, : 3 * UNIT]
    g_one = ways.add_core(keep_one, send_one)
    g_two = ways.sum_wide(after(g_two, keep_one))
    g_three = ways.finish(after(g_three, keep_one))
    g_one = ways.sum_core(after(g_one, g_two))
    grads = after(grads, g_one)
    g_two = ways.add_deep(g_two)
    g_one = ways.add_wide(g_one)
    (d_memory,) = call(
        memory_grad_kernel, steps,
        [facts, (after(dck, grads), along), (dcv, along), *remote(two)],
        [((others, width), full, rows_block(width))],
        [units(2), sem],
        2.0,
    )
    half_along = columns_block(width // 2)
    (d_tokens,) = call(
        token_grad_kernel, steps,
        [facts, (dq_one, half_along), (dk_one, half_along), (dv_one, half_along),
         (grads, columns_block(3 * width // 2)), (dr_one, along), *remote(one)],
        [((length, width), full, rows_block(width))],
        [units(3), sem],
        3.0,
    )
    g_two = ways.finish(after(g_two, d_tokens, d_memory))
    g_one = ways.finish(ways.add_deep(ways.sum_wide(after(g_one, d_tokens, d_memory))))
    if nearby:
        g_vectors = g_one[3 * UNIT, : vectors.shape[0]]
    else:
        g_vectors = jnp.concatenate(
            [
                rows_self[0:1], rows_self[2:3], rows_cross[2:3], rows_cross[0:2], rows_ffn[5:6],
                rows_ffn[4:5], rows_cross[3:4], rows_ffn[6:8], rows_cross[4:5], rows_ffn[8:10],
                rows_self[3:5], rows_ffn[0:4],
            ],
            0,
        ).reshape(-1)
        g_vectors = lax.psum_scatter(g_vectors, "dp", scatter_dimension=0, tiled=True)

    def flat(grad, first, stop):
        piece = grad[first * rows : stop * rows].reshape(stop - first, rows, width)
        return piece.transpose(1, 0, 2).reshape(-1)

    return (
        out[None], d_tokens[None], d_memory[None],
        flat(g_one, 0, 3), flat(g_two, 0, 1), flat(g_two, 1, 2), flat(g_two, 2, 4),
        flat(g_two, 4, 5), flat(g_three, 0, parts), g_three[parts * rows :].reshape(-1), g_vectors,
    )


def solution(mesh):
    rows, flat = P("dp", None, None), P("dp")
    return jax.shard_map(
        body,
        mesh=mesh,
        in_specs=(rows, rows) + (flat,) * 11 + (rows,),
        out_specs=(rows,) * 3 + (flat,) * 8,
        check_vma=False,
    )
```

```python
import jax
import jax.numpy as jnp
from jax import lax
from jax.experimental import pallas as pl
from jax.experimental.pallas import tpu as pltpu
from jax.sharding import PartitionSpec as P

HEADS = 8
STEP = 256
PAIR = 2 * STEP
AUG = 16
UNIT = 16
SAFE_SQUARE = 3600.0
mask_fill = -1000000000.0
norm_eps = 1e-05
low = jnp.bfloat16
full = jnp.float32


def contract(left, right, left_dim, right_dim):
    return lax.dot_general(
        left, right, (((left_dim,), (right_dim,)), ((), ())), preferred_element_type=full
    )


def nn(left, right):
    return contract(left, right, 1, 0)


def tn(left, right):
    return contract(left, right, 0, 0)


def nt(left, right):
    return contract(left, right, 1, 1)


def block(index):
    return slice(index * STEP, (index + 1) * STEP)


def blocks_of(length):
    return (length + STEP - 1) // STEP


def split_three(values):
    first = values.astype(low)
    rest = values - first.astype(full)
    second = rest.astype(low)
    third = (rest - second.astype(full)).astype(low)
    return first, second, third


def normalize(values):
    center = jnp.mean(values, axis=0, keepdims=True)
    offsets = values - center
    spread = jnp.mean(offsets * offsets, axis=0, keepdims=True)
    scale = lax.rsqrt(spread + norm_eps)
    return offsets * scale, scale


def norm_backward(grad, hat, scale, gain):
    scaled = grad * gain
    center = jnp.mean(scaled, axis=0, keepdims=True)
    along = jnp.mean(scaled * hat, axis=0, keepdims=True)
    return (scaled - center - hat * along) * scale


def fold_lanes(values):
    total = values[:, :128]
    for start in range(128, values.shape[1], 128):
        total = total + values[:, start : start + 128]
    return total


def lane_total(partial):
    ones = jnp.ones((8, 128), full)
    return lax.dot_general(
        ones,
        partial,
        (((1,), (1,)), ((), ())),
        precision=lax.Precision.HIGHEST,
        preferred_element_type=full,
    )[0:1]


def token_total(values):
    return nt(jnp.ones((AUG, values.shape[1]), low), values)[0:1]


def head_rows(head, head_dim):
    return pl.ds(pl.multiple_of(head * head_dim, head_dim), head_dim)


def square_peak(values, head_dim):
    squares = jnp.square(values.astype(full))
    count = values.shape[0] // head_dim
    return jnp.max(jnp.sum(squares.reshape(count, head_dim, values.shape[1]), axis=1))


def place_order():
    return [side ^ deep for side in (0, 2, 4, 6) for deep in (0, 8, 16, 24)]


def unit_spot(whole, owner, by_row):
    if by_row:
        return whole.at[owner]
    return whole.at[:, pl.ds(pl.multiple_of(owner * UNIT, UNIT), UNIT), :]


def unit_part(buffer, index, first, stop):
    part = buffer.at[index, first * UNIT : stop * UNIT]
    return part.reshape(stop - first, UNIT, buffer.shape[2])


def start_fetch(me, near, far, moves, sem):
    for index, relative in enumerate(place_order()):
        for sources, place in ((near, relative), (far, relative ^ 1)):
            owner = jnp.bitwise_xor(me, place)
            each = sources[0].shape[0]
            for target, first, stop, by_row in moves:
                spot = unit_spot(target, owner, by_row)
                part = unit_part(sources[index // each], index % each, first, stop)
                pltpu.make_async_copy(part, spot, sem).start()


def wait_fetch(moves, sem):
    for target, first, stop, by_row in moves:
        pltpu.make_async_copy(target, target, sem).wait()


def start_store(me, near, far, moves, sem):
    for index, relative in enumerate(place_order()):
        for sink, place in ((near, relative), (far, relative ^ 1)):
            owner = jnp.bitwise_xor(me, place)
            for source, first, stop, by_row in moves:
                spot = unit_spot(source, owner, by_row)
                part = unit_part(sink, index, first, stop)
                pltpu.make_async_copy(spot, part, sem).start()


def clear_from(ref, start):
    rows, columns = ref.shape
    if start < columns:
        ref[:, start:] = jnp.zeros((rows, columns - start), ref.dtype)


def attend_forward(
    q_ref, k_ref, v_ref, mix_ref, sums_ref, head, mask_rows, pairs, keys, shifted
):
    causal = mask_rows is None
    head_dim = q_ref.shape[0]
    key_head = k_ref[:, :keys]
    if not causal:
        key_head = jnp.concatenate([key_head, mask_rows[:, :keys]], 0)
    value_head = jnp.concatenate([v_ref[:, :keys], jnp.ones((AUG, keys), low)], 0)
    for pair in range(pairs):
        columns = slice(pair * PAIR, (pair + 1) * PAIR)
        query = q_ref[:, columns]
        if causal:
            main = pair * PAIR + STEP
            scores = tn(key_head[:, :main], query)
            late = tn(key_head[:, main : main + STEP], query[:, STEP:])
            key_pos = lax.broadcasted_iota(jnp.int32, (STEP, STEP), 0)
            query_pos = lax.broadcasted_iota(jnp.int32, (STEP, STEP), 1)
            allowed = key_pos <= query_pos
            edge = scores[main - STEP :]
            edge = jnp.concatenate(
                [jnp.where(allowed, edge[:, :STEP], mask_fill), edge[:, STEP:]], 1
            )
            scores = edge if main == STEP else jnp.concatenate([scores[: main - STEP], edge], 0)
            late = jnp.where(allowed, late, mask_fill)
        else:
            query = jnp.concatenate([query, jnp.ones((AUG, PAIR), low)], 0)
            scores = tn(key_head, query)
        if shifted:
            highest = jnp.max(scores, axis=0, keepdims=True)
            if causal:
                second = jnp.maximum(highest[:, STEP:], jnp.max(late, axis=0, keepdims=True))
                highest = jnp.concatenate([highest[:, :STEP], second], 1)
                late = late - second
            scores = scores - highest
        powered = jnp.exp(scores).astype(low)
        if causal:
            mixed = nn(value_head[:, :main], powered)
            extra = nn(value_head[:, main : main + STEP], jnp.exp(late).astype(low))
            mixed = jnp.concatenate([mixed[:, :STEP], mixed[:, STEP:] + extra], 1)
        else:
            mixed = nn(value_head, powered)
        total = mixed[head_dim : head_dim + 1]
        mix_ref[:, columns] = mixed[:head_dim] / total
        log_sum = jnp.log(total)
        sums_ref[pl.ds(head, 1), columns] = log_sum + highest if shifted else log_sum
    clear_from(mix_ref, pairs * PAIR)


def attend_backward(
    q_ref, k_ref, v_ref, mix_ref, sums_ref, head, grad_ref, dq_ref, dk_ref, dv_ref,
    key_sum, value_sum, mask_rows, steps, keys
):
    causal = mask_rows is None
    length = steps * STEP
    scale = q_ref.shape[0] ** (-0.5)
    key_head = k_ref[:, :keys]
    value_head = v_ref[:, :keys]
    query = q_ref[:, :length]
    grad = grad_ref[:, :length]
    inner = jnp.sum(grad.astype(full) * mix_ref[:, :length], axis=0, keepdims=True)
    one = jnp.ones((1, length), low)
    blank = jnp.zeros((AUG - 4, length), low)
    query_aug = jnp.concatenate(
        [query, *split_three(sums_ref[pl.ds(head, 1), :length]), one, blank], 0
    )
    grad_aug = jnp.concatenate([grad, *split_three(inner), one, blank], 0)
    minus = jnp.full((3, keys), -1.0, low)
    key_blank = jnp.zeros((AUG - 3, keys), low)
    value_aug = jnp.concatenate([value_head, minus, key_blank], 0)
    if causal:
        key_aug = jnp.concatenate([key_head, minus, key_blank], 0)
    else:
        key_aug = jnp.concatenate([key_head, minus, mask_rows[0:1, :keys], key_blank[1:]], 0)
    for step in range(steps):
        span = block(step)
        count = (step + 1) * STEP if causal else keys
        scores = tn(query_aug[:, span], key_aug[:, :count])
        chances = jnp.exp(scores)
        if causal:
            query_pos = lax.broadcasted_iota(jnp.int32, (STEP, STEP), 0)
            key_pos = lax.broadcasted_iota(jnp.int32, (STEP, STEP), 1)
            edge = jnp.where(key_pos <= query_pos, chances[:, count - STEP :], 0.0)
            chances = (
                edge if count == STEP
                else jnp.concatenate([chances[:, : count - STEP], edge], 1)
            )
        grad_chances = tn(grad_aug[:, span], value_aug[:, :count])
        grad_scores = (chances * grad_chances).astype(low)
        to_value = nn(grad[:, span], chances.astype(low))
        to_key = nn(query[:, span], grad_scores)
        to_query = nt(key_head[:, :count], grad_scores)
        dq_ref[:, span] = (to_query * scale).astype(low)
        if step == 0:
            value_sum[:, :count] = to_value
            key_sum[:, :count] = to_key
        elif causal:
            old = count - STEP
            value_sum[:, :old] += to_value[:, :old]
            key_sum[:, :old] += to_key[:, :old]
            value_sum[:, old:count] = to_value[:, old:]
            key_sum[:, old:count] = to_key[:, old:]
        else:
            value_sum[:, :count] += to_value
            key_sum[:, :count] += to_key
    dv_ref[:, :keys] = value_sum[:, :keys].astype(low)
    dk_ref[:, :keys] = key_sum[:, :keys].astype(low)
    clear_from(dq_ref, length)
    clear_from(dk_ref, keys)
    clear_from(dv_ref, keys)


def add_to(first, rows, index, value):
    if first:
        rows[index : index + 1] = value
    else:
        rows[index : index + 1] += value


def gather_into(first, ref, value):
    if first:
        ref[...] = value
    else:
        ref[...] += value


def self_forward_kernel(
    facts, tokens, near, far, vector_rows, token_t, q_ref, k_ref, v_ref, mix_ref, sums_ref, columns,
    q_all, k_all, v_all, held, sem, peaks
):
    step = pl.program_id(0)
    width, length = q_all.shape
    blocks = length // STEP
    head_dim = width // HEADS
    moves = [(held, 0, 3, False)]

    @pl.when(step == 0)
    def prepare():
        start_fetch(facts[3], near, far, moves, sem)
        peaks[0] = 0.0
        peaks[1] = 0.0
        rest = jnp.zeros((128 - vector_rows.shape[0], width), full)
        columns[...] = jnp.concatenate([vector_rows[...], rest], 0).T
        wait_fetch(moves, sem)

    @pl.when((step < blocks) & (step < blocks_of(facts[1])))
    def live():
        embed = jnp.where(facts[0] == 1, columns[:, 14:15], columns[:, 13:14])
        flipped = tokens[...].T
        token_t[...] = flipped
        shared = (flipped.astype(full) + embed).astype(low)
        query = (tn(held[0], shared) + columns[:, 0:1]).astype(low) * (head_dim ** (-0.5))
        key = tn(held[1], shared).astype(low)
        value = (tn(held[2], shared) + columns[:, 1:2]).astype(low)
        spot = pl.ds(pl.multiple_of(step * STEP, STEP), STEP)
        for ref, all_ref, made in (
            (q_ref, q_all, query), (k_ref, k_all, key), (v_ref, v_all, value)
        ):
            ref[...] = made
            all_ref[:, spot] = made
        peaks[0] = jnp.maximum(peaks[0], square_peak(query, head_dim))
        peaks[1] = jnp.maximum(peaks[1], square_peak(key, head_dim))

    @pl.when((step < blocks) & (step >= blocks_of(facts[1])))
    def dead():
        spot = pl.ds(pl.multiple_of(step * STEP, STEP), STEP)
        token_t[...] = jnp.zeros_like(token_t)
        for ref, all_ref in ((q_ref, q_all), (k_ref, k_all), (v_ref, v_all)):
            ref[...] = jnp.zeros_like(ref)
            all_ref[:, spot] = jnp.zeros_like(ref)

    head = step - blocks
    safe = peaks[0] * peaks[1] <= SAFE_SQUARE
    pairs = (blocks_of(facts[1]) + 1) // 2
    rows = pl.ds(pl.multiple_of(jnp.maximum(head, 0) * head_dim, head_dim), head_dim)
    for wanted in range(1, length // PAIR + 1):
        for shifted in (False, True):

            @pl.when((step >= blocks) & (pairs == wanted) & (safe != shifted))
            def attend():
                attend_forward(
                    q_all.at[rows], k_all.at[rows], v_all.at[rows], mix_ref, sums_ref, head, None,
                    wanted, wanted * PAIR, shifted,
                )


def fill_mask(mask_ref, visible):
    position = lax.broadcasted_iota(jnp.int32, mask_ref.shape, 1)
    row = lax.broadcasted_iota(jnp.int32, mask_ref.shape, 0)
    hidden = (position >= visible) & (row == 0)
    mask_ref[...] = jnp.where(hidden, mask_fill, 0.0).astype(low)


def cross_forward_kernel(
    facts, token_t, memory, mix, near, far, columns,
    hat_ref, scale_ref, memory_t, q_ref, k_ref, v_ref, mix_ref, sums_ref,
    q_all, k_all, v_all, held, sem, mask_ref, peaks
):
    step = pl.program_id(0)
    width, length = q_all.shape
    others = k_all.shape[1]
    blocks = max(length, others) // STEP
    head_dim = width // HEADS
    moves = [(held, 0, 4, False)]
    spot = pl.ds(pl.multiple_of(jnp.minimum(step, blocks - 1) * STEP, STEP), STEP)

    @pl.when(step == 0)
    def prepare():
        start_fetch(facts[3], near, far, moves, sem)
        fill_mask(mask_ref, facts[2])
        peaks[0] = 0.0
        peaks[1] = 0.0
        wait_fetch(moves, sem)

    @pl.when((step < blocks) & (step < blocks_of(facts[2])))
    def encode():
        flipped = memory[...].T
        memory_t[...] = flipped
        key = tn(held[2], flipped).astype(low)
        value = (tn(held[3], flipped) + columns[:, 4:5]).astype(low)
        k_ref[...] = key
        v_ref[...] = value
        k_all[:, spot] = key
        v_all[:, spot] = value
        peaks[1] = jnp.maximum(peaks[1], square_peak(key, head_dim))

    @pl.when((step < blocks) & (step < blocks_of(facts[1])))
    def first():
        embed = jnp.where(facts[0] == 1, columns[:, 14:15], columns[:, 13:14])
        started = token_t[...].astype(full) + embed
        total = started + tn(held[0], mix[...].astype(low)) + columns[:, 2:3]
        hat, scale = normalize(total)
        hat_ref[...] = hat
        scale_ref[...] = jnp.broadcast_to(scale, scale_ref.shape)
        shared = (hat * columns[:, 7:8] + columns[:, 10:11]).astype(low)
        query = (tn(held[1], shared) + columns[:, 3:4]).astype(low) * (head_dim ** (-0.5))
        q_ref[...] = query
        q_all[:, spot] = query
        peaks[0] = jnp.maximum(peaks[0], square_peak(query, head_dim))

    @pl.when((step < blocks) & (step >= blocks_of(facts[2])))
    def hidden():
        memory_t[...] = jnp.zeros_like(memory_t)
        for ref, all_ref in ((k_ref, k_all), (v_ref, v_all)):
            ref[...] = jnp.zeros_like(ref)
            all_ref[:, spot] = jnp.zeros_like(ref)

    @pl.when((step < blocks) & (step >= blocks_of(facts[1])))
    def dead():
        hat_ref[...] = jnp.zeros_like(hat_ref)
        scale_ref[...] = jnp.zeros_like(scale_ref)
        q_ref[...] = jnp.zeros_like(q_ref)
        q_all[:, spot] = jnp.zeros_like(q_ref)

    head = step - blocks
    safe = peaks[0] * peaks[1] <= SAFE_SQUARE
    pairs = (blocks_of(facts[1]) + 1) // 2
    key_count = blocks_of(facts[2])
    rows = pl.ds(pl.multiple_of(jnp.maximum(head, 0) * head_dim, head_dim), head_dim)
    for wanted in range(1, length // PAIR + 1):
        for wanted_keys in range(1, others // STEP + 1):
            for shifted in (False, True):

                @pl.when(
                    (step >= blocks) & (pairs == wanted) & (key_count == wanted_keys)
                    & (safe != shifted)
                )
                def attend():
                    attend_forward(
                        q_all.at[rows], k_all.at[rows], v_all.at[rows], mix_ref, sums_ref, head,
                        mask_ref[...], wanted, wanted_keys * STEP, shifted,
                    )


def gelu_parts(values):
    half = 0.5 * (1.0 + lax.erf(values * (0.5**0.5)))
    bell = jnp.exp(-0.5 * values * values) * 0.3989422804014327
    return values * half, half + values * bell


def ffn_kernel(
    facts, hat_one, cross_mix, cotangent, near_two, far_two, near, far, columns,
    out_ref, dr_ref, dmix_ref, keep, send, g_cross_out, g_rows,
    c_out, f_in, f_out, low_in, low_out, slope, acts, top_ref, result_ref, sems
):
    length, width = top_ref.shape
    parts = f_in.shape[0]
    rows_of = width // parts // UNIT
    moves_two = [(c_out, 4, 5, False)]
    moves_in = [(f_in, 0, parts, False)]
    moves_out = [(f_out, parts, 2 * parts, True)]
    stores_in = [(low_in, 0, parts, False)]
    stores_out = [(low_out, parts, 2 * parts, True)]
    fetch_top = pltpu.make_async_copy(cotangent, top_ref, sems.at[3])
    store_result = pltpu.make_async_copy(result_ref, out_ref, sems.at[4])
    start_fetch(facts[3], near_two, far_two, moves_two, sems.at[0])
    start_fetch(facts[3], near, far, moves_in, sems.at[1])
    start_fetch(facts[3], near, far, moves_out, sems.at[2])
    fetch_top.start()
    g_rows[...] = jnp.zeros_like(g_rows)

    def out_part(part):
        return f_out[part * rows_of : (part + 1) * rows_of].reshape(width, width)

    def live(count):
        span = slice(0, count)
        wait_fetch(moves_two, sems.at[0])
        position = lax.broadcasted_iota(jnp.int32, (1, count), 1)
        valid = (position < facts[1]).astype(full)
        mixed = cross_mix[:, span].astype(low)
        first = hat_one[:, span] * columns[:, 7:8] + columns[:, 10:11]
        total = first + tn(c_out[0], mixed) + columns[:, 5:6]
        hat_two, scale_two = normalize(total)
        second = hat_two * columns[:, 8:9] + columns[:, 11:12]
        shared = second.astype(low)
        third = second + columns[:, 6:7]
        wait_fetch(moves_in, sems.at[1])
        wait_fetch(moves_out, sems.at[2])
        for part in range(parts):
            chunk = slice(part * width, (part + 1) * width)
            raw = tn(f_in[part], shared) + columns[:, 15 + part : 16 + part]
            act, slope_part = gelu_parts(raw)
            slope[chunk, span] = slope_part
            acts[chunk, span] = act.astype(low)
            third = third + tn(out_part(part), acts[chunk, span])
        hat_three, scale_three = normalize(third)
        result = (hat_three * columns[:, 9:10] + columns[:, 12:13]) * valid
        result_ref[span, :] = result.astype(low).T
        if count < length:
            result_ref[count:, :] = jnp.zeros((length - count, width), low)
        store_result.start()
        fetch_top.wait()
        top = top_ref[span, :].T.astype(full) * valid
        g_rows[7:8] = lane_total(fold_lanes(top * hat_three))
        g_rows[9:10] = lane_total(fold_lanes(top))
        grad_third = norm_backward(top, hat_three, scale_three, columns[:, 9:10])
        branch = grad_third.astype(low)
        g_rows[4:5] = token_total(branch)
        grad_second = grad_third
        for part in range(parts):
            chunk = slice(part * width, (part + 1) * width)
            back = nn(out_part(part), branch)
            rows = slice(part * rows_of, (part + 1) * rows_of)
            low_out[rows] = nt(acts[chunk, span], branch).astype(low).reshape(
                rows_of, parts, UNIT, width
            )
            acts[chunk, span] = (back * slope[chunk, span]).astype(low)
        start_store(facts[3], keep, send, stores_out, sems.at[2])
        for part in range(parts):
            chunk = slice(part * width, (part + 1) * width)
            grad_hidden = acts[chunk, span]
            g_rows[part : part + 1] = token_total(grad_hidden)
            low_in[part] = nt(shared, grad_hidden).astype(low)
            grad_second = grad_second + nn(f_in[part], grad_hidden)
        start_store(facts[3], keep, send, stores_in, sems.at[1])
        g_rows[6:7] = lane_total(fold_lanes(grad_second * hat_two))
        g_rows[8:9] = lane_total(fold_lanes(grad_second))
        grad_two = norm_backward(grad_second, hat_two, scale_two, columns[:, 8:9])
        dr_ref[:, span] = grad_two
        branch_two = grad_two.astype(low)
        g_rows[5:6] = token_total(branch_two)
        g_cross_out[...] = nt(mixed, branch_two).astype(low)
        dmix_ref[:, span] = nn(c_out[0], branch_two).astype(low)

    live(length)
    wait_fetch(stores_out, sems.at[2])
    wait_fetch(stores_in, sems.at[1])
    store_result.wait()


def cross_backward_kernel(
    facts, q_ref, k_ref, v_ref, cross_mix, sums_ref, dmix, dq_ref, dk_ref, dv_ref,
    key_sum, value_sum, mask_ref
):
    head = pl.program_id(0)
    length = q_ref.shape[1]
    others = k_ref.shape[1]
    count = blocks_of(facts[1])
    key_count = blocks_of(facts[2])

    @pl.when(head == 0)
    def prepare():
        fill_mask(mask_ref, facts[2])

    for wanted in range(1, length // STEP + 1):
        for wanted_keys in range(1, others // STEP + 1):

            @pl.when((count == wanted) & (key_count == wanted_keys))
            def attend():
                attend_backward(
                    q_ref, k_ref, v_ref, cross_mix, sums_ref, head, dmix,
                    dq_ref, dk_ref, dv_ref, key_sum, value_sum, mask_ref[...],
                    wanted, wanted_keys * STEP,
                )


def middle_kernel(
    facts, dq_ref, dk_ref, dv_ref, dr_two, hat_one, scale_one, memory_t, mix, near, far,
    g_cross_out, columns, dr_ref, dself, keep, send, g_rows,
    held, made_low, sum_query, sum_key, sum_value, sum_out, lanes, sem
):
    step = pl.program_id(0)
    moves = [(held, 0, 2, False)]

    @pl.when(step == 0)
    def prepare():
        start_fetch(facts[3], near, far, moves, sem)
        g_rows[...] = jnp.zeros_like(g_rows)
        lanes[...] = jnp.zeros_like(lanes)
        wait_fetch(moves, sem)

    span = dq_ref.shape[1]

    def encode(initial):
        add_to(initial, g_rows, 1, token_total(dv_ref[...]))
        gather_into(initial, sum_key, nt(memory_t[...], dk_ref[...]))
        gather_into(initial, sum_value, nt(memory_t[...], dv_ref[...]))

    def first(initial):
        hat = hat_one[...]
        shared = (hat * columns[:, 7:8] + columns[:, 10:11]).astype(low)
        grad_query = dq_ref[...]
        add_to(initial, g_rows, 0, token_total(grad_query))
        gather_into(initial, sum_query, nt(shared, grad_query))
        grad = dr_two[...] + nn(held[1], grad_query)
        lanes[0] += fold_lanes(grad * hat)
        lanes[1] += fold_lanes(grad)
        grad_one = norm_backward(grad, hat, scale_one[0:1], columns[:, 7:8])
        dr_ref[...] = grad_one
        lanes[2] += fold_lanes(grad_one)
        branch = grad_one.astype(low)
        add_to(initial, g_rows, 2, token_total(branch))
        gather_into(initial, sum_out, nt(mix[...].astype(low), branch))
        dself[...] = nn(held[0], branch).astype(low)

    pl.when(step == 0)(lambda: encode(True))
    pl.when((step > 0) & (step * span < facts[2]))(lambda: encode(False))
    pl.when(step == 0)(lambda: first(True))
    pl.when((step > 0) & (step * span < facts[1]))(lambda: first(False))

    @pl.when((step > 0) & (step * span >= facts[1]))
    def dead():
        dr_ref[...] = jnp.zeros_like(dr_ref)
        dself[...] = jnp.zeros_like(dself)


    @pl.when(step == pl.num_programs(0) - 1)
    def close():
        made_low[0] = sum_out[...].astype(low)
        made_low[1] = sum_query[...].astype(low)
        made_low[2] = sum_key[...].astype(low)
        made_low[3] = sum_value[...].astype(low)
        made_low[4] = g_cross_out[...]
        stores = [(made_low, 0, 5, False)]
        start_store(facts[3], keep, send, stores, sem)
        g_rows[3:4] = lane_total(lanes[0])
        g_rows[4:5] = lane_total(lanes[1])
        g_rows[5:6] = lane_total(lanes[2])
        wait_fetch(stores, sem)


def memory_grad_kernel(facts, dk_ref, dv_ref, near, far, d_memory, held, sem):
    step = pl.program_id(0)
    moves = [(held, 2, 4, False)]

    @pl.when(step == 0)
    def prepare():
        start_fetch(facts[3], near, far, moves, sem)
        wait_fetch(moves, sem)

    @pl.when(step < blocks_of(facts[2]))
    def live():
        d_memory[...] = (nn(held[0], dk_ref[...]) + nn(held[1], dv_ref[...])).T

    @pl.when(step >= blocks_of(facts[2]))
    def blank():
        d_memory[...] = jnp.zeros_like(d_memory)


def self_backward_kernel(
    facts, q_ref, k_ref, v_ref, mix, sums_ref, dself, dq_ref, dk_ref, dv_ref, key_sum, value_sum
):
    head = pl.program_id(0)
    count = blocks_of(facts[1])
    for wanted in range(1, q_ref.shape[1] // STEP + 1):

        @pl.when(count == wanted)
        def attend():
            attend_backward(
                q_ref, k_ref, v_ref, mix, sums_ref, head, dself, dq_ref, dk_ref, dv_ref,
                key_sum, value_sum, None, wanted, wanted * STEP,
            )


def self_finish_kernel(
    facts, q_ref, k_ref, v_ref, mix, sums_ref, dself, token_t, dq_one, dk_one, dv_one,
    rows_ffn, rows_cross, near, far, columns,
    grads, keep, send, g_rows,
    key_sum, value_sum, made_low, made_rows, held, sem, sem_out
):
    step_at = pl.program_id(0)
    last = pl.num_programs(0) - 1
    head = step_at + HEADS // 2
    head_dim, length = q_ref.shape
    width = token_t.shape[0]
    half = width // 2
    count = blocks_of(facts[1])
    moves = [(held, 0, 3, False)]

    @pl.when(step_at == 0)
    def prepare():
        start_fetch(facts[3], near, far, moves, sem)

    def place(part):
        start = pl.multiple_of(part * half + step_at * head_dim, head_dim)
        return grads.at[pl.ds(start, head_dim)]

    for wanted in range(1, length // STEP + 1):

        @pl.when((step_at < last) & (count == wanted))
        def attend():
            attend_backward(
                q_ref, k_ref, v_ref, mix, sums_ref, head, dself,
                place(0), place(1), place(2), key_sum, value_sum, None, wanted, wanted * STEP,
            )

    @pl.when(step_at == last)
    def weights():
        embed = jnp.where(facts[0] == 1, columns[:, 14:15], columns[:, 13:14])
        g_rows[...] = jnp.zeros_like(g_rows)

        shared = (token_t[...].astype(full) + embed).astype(low)
        for part, early in enumerate((dq_one, dk_one, dv_one)):
            both = jnp.concatenate([early[...], grads[part * half : (part + 1) * half, :]], 0)
            g_rows[part : part + 1] = token_total(both)
            made_low[part] = nt(shared, both).astype(low)
        stores = [(made_low, 0, 3, False)]
        start_store(facts[3], keep, send, stores, sem_out)
        wait_fetch(moves, sem)
        total = rows_cross[5:6]
        for part in range(3):
            pieces = jnp.concatenate(
                [*split_three(g_rows[part : part + 1]), jnp.zeros((AUG - 3, width), low)], 0
            )
            total = total + jnp.sum(nt(pieces, held[part]), axis=0, keepdims=True)
        g_rows[3:4] = jnp.where(facts[0] == 1, 0.0, total)
        g_rows[4:5] = jnp.where(facts[0] == 1, total, 0.0)
        picks = [
            g_rows[0:1], g_rows[2:3], rows_cross[2:3], rows_cross[0:1], rows_cross[1:2],
            rows_ffn[5:6], rows_ffn[4:5], rows_cross[3:4], rows_ffn[6:7], rows_ffn[7:8],
            rows_cross[4:5], rows_ffn[8:9], rows_ffn[9:10], g_rows[3:4], g_rows[4:5],
            *[rows_ffn[part : part + 1] for part in range(4)],
        ]
        share = len(picks) * width // made_rows.shape[0]
        for owner in range(made_rows.shape[0]):
            row, start = divmod(owner * share, width)
            stop = min(start + share, width)
            pieces = [picks[row][:, start:stop]]
            if stop - start < share:
                pieces.append(picks[row + 1][:, : share - (stop - start)])
            pieces.append(jnp.zeros((1, width - share), full))
            line = jnp.concatenate(pieces, 1)
            made_rows[owner, 0] = jnp.concatenate(
                [line, jnp.zeros((UNIT - 1, width), full)], 0
            ).astype(low)
        more = [(made_rows, 3, 4, True)]
        start_store(facts[3], keep, send, more, sem)
        wait_fetch(stores, sem_out)
        wait_fetch(more, sem)


def token_grad_kernel(
    facts, dq_one, dk_one, dv_one, grads, dr_one, near, far, d_tokens, held, sem
):
    step = pl.program_id(0)
    width = dr_one.shape[0]
    moves = [(held, 0, 3, False)]

    @pl.when(step == 0)
    def prepare():
        start_fetch(facts[3], near, far, moves, sem)
        wait_fetch(moves, sem)

    @pl.when(step < blocks_of(facts[1]))
    def live():
        made = dr_one[...]
        half = width // 2
        for part, early in enumerate((dq_one, dk_one, dv_one)):
            both = jnp.concatenate([early[...], grads[part * half : (part + 1) * half, :]], 0)
            made = made + nn(held[part], both)
        d_tokens[...] = made.T

    @pl.when(step >= blocks_of(facts[1]))
    def blank():
        d_tokens[...] = jnp.zeros_like(d_tokens)


def in_place(shape):
    return pl.BlockSpec(shape, lambda step: (0,) * len(shape))


def columns_block(rows, span=STEP):
    return pl.BlockSpec((rows, span), lambda step: (0, step))


def rows_block(columns, span=STEP):
    return pl.BlockSpec((span, columns), lambda step: (step, 0))


def first_columns(rows, count):
    return pl.BlockSpec((rows, STEP), lambda step: (0, jnp.minimum(step, count - 1)))


def first_rows(columns, count):
    return pl.BlockSpec((STEP, columns), lambda step: (jnp.minimum(step, count - 1), 0))


def later_head(head_dim, columns, count):
    return pl.BlockSpec((head_dim, columns), lambda step: (jnp.maximum(step - count, 0), 0))


def head_block(head_dim, columns, first=0, count=HEADS):
    return pl.BlockSpec(
        (head_dim, columns), lambda step: (first + jnp.minimum(step, count - 1), 0)
    )


def call(kernel, steps, ins, outs, scratch, cost, room=0):
    room = room or (56 if kernel in (self_forward_kernel, cross_forward_kernel) else 20)
    def spec_of(spec, array=None):
        if isinstance(array, list):
            return [spec_of(spec)] * len(array)
        return pl.BlockSpec(memory_space=pl.ANY) if spec is None else spec

    return pl.pallas_call(
        kernel,
        grid=(steps,),
        out_shape=[jax.ShapeDtypeStruct(shape, dtype) for shape, dtype, spec in outs],
        in_specs=[spec_of(spec, array) for array, spec in ins],
        out_specs=[spec_of(spec) for shape, dtype, spec in outs],
        scratch_shapes=scratch,
        compiler_params=pltpu.CompilerParams(
            vmem_limit_bytes=room * 2**20, dimension_semantics=("arbitrary",)
        ),
        cost_estimate=pl.CostEstimate(
            flops=int(cost * 1.0e9), bytes_accessed=4 * 2**20, transcendentals=0
        ),
        name=kernel.__name__,
    )(*[array for array, spec in ins])


SIDES = (0, 2, 4, 6)
DEPTHS = (0, 8, 16, 24)


def swap(values, mask):
    count = lax.axis_size("dp")
    return lax.ppermute(values, "dp", [(spot, spot ^ mask) for spot in range(count)])


def spread_along(held, masks):
    return [held] + [swap(held, mask) for mask in masks[1:]]


def after(value, *earlier):
    return lax.optimization_barrier((value, earlier))[0]


class Staged:
    def deep(self, piece, late=0):
        return spread_along(piece[None], DEPTHS)

    def wide(self, held):
        return spread_along(held, SIDES)

    def both(self, held):
        return [held], [swap(held, 1)]

    def join(self, parts):
        return jnp.concatenate(parts, 0)

    def cross(self, parts, ready):
        far = [swap(parts[0], 1)]
        parts = [parts[0], *after(parts[1:], ready)]
        return parts, far + [swap(part, 1) for part in parts[1:]]

    def add_core(self, keep, send, late=0):
        return keep, swap(send, 1)

    def sum_core(self, pair):
        keep, got = pair
        sums = [
            keep[4 * side : 4 * side + 4].astype(full) + got[4 * side : 4 * side + 4].astype(full)
            for side in range(4)
        ]
        return [sums[0]] + [part.astype(keep.dtype) for part in sums[1:]]

    def add_wide(self, sums):
        return [sums[0]] + [swap(sums[side], SIDES[side]) for side in range(1, 4)]

    def total(self, parts):
        total = parts[0]
        for part in parts[1:]:
            total = total + part.astype(full)
        return total

    def sum_wide(self, parts):
        wire = parts[1].dtype
        total = self.total(parts)
        return [total[0]] + [total[deep].astype(wire) for deep in range(1, 4)]

    def add_deep(self, sums):
        return [sums[0]] + [swap(sums[deep], DEPTHS[deep]) for deep in range(1, 4)]

    def some(self, parts):
        return parts[3]

    def add_far(self, sums):
        return sums[:2] + [swap(sums[deep], DEPTHS[deep]) for deep in (2, 3)]

    def sum_far(self, parts):
        return self.total([parts[0], *parts[2:]]), parts[1]

    def add_pair(self, first, second):
        both = jnp.concatenate([first[1], second[1]], 0)
        return first[0], second[0], swap(both, DEPTHS[1]), swap(second[2], DEPTHS[2]), second[3]

    def last_far(self, pair, ready):
        return *pair[:4], swap(after(pair[4], ready), DEPTHS[3])

    def finish_pair(self, pair, split):
        first, second, both, *rest = pair
        return self.total([first, both[:split]]), self.total([second, both[split:], *rest])

    def finish(self, parts):
        return self.total(parts)


class Plain:
    def __init__(self, devices, chunks, rows, width, order):
        self.devices, self.chunks, self.rows, self.width = devices, chunks, rows, width
        self.order = order

    def arrange(self, gathered, by_row):
        group = self.devices // self.chunks
        split = gathered.reshape(self.chunks, group, -1, self.rows, self.width)
        if not by_row:
            split = split.transpose(0, 2, 1, 3, 4)
        return split.reshape(self.chunks, -1, self.width)

    def spread(self, ordered, by_row):
        group = self.devices // self.chunks
        if by_row:
            return ordered.reshape(self.devices, -1, self.width)
        split = ordered.reshape(self.chunks, -1, group, self.rows, self.width)
        return split.transpose(0, 2, 1, 3, 4).reshape(self.devices, -1, self.width)

    def deep(self, piece, late=0):
        gathered = lax.all_gather(piece, "dp", axis=0)
        plain = piece.shape[0] - late
        ordered = self.arrange(gathered[:, :plain], False)
        if late:
            ordered = jnp.concatenate([ordered, self.arrange(gathered[:, plain:], True)], 1)
        return jnp.take(ordered, jnp.array(self.order), axis=0)

    def wide(self, held):
        return held

    def join(self, held):
        return held

    def both(self, held):
        return [held[: self.chunks // 2]], [held[self.chunks // 2 :]]

    def cross(self, held, ready):
        return self.both(held)

    def add_core(self, keep, send, late=0):
        back = [self.order.index(place) for place in range(self.chunks)]
        ordered = jnp.take(jnp.concatenate([keep, send], 0), jnp.array(back), axis=0)
        plain = ordered.shape[1] - late * UNIT
        split = self.spread(ordered[:, :plain], False)
        if late:
            split = jnp.concatenate([split, self.spread(ordered[:, plain:], True)], 1)
        return lax.psum_scatter(split.astype(full), "dp", scatter_dimension=0, tiled=False)

    def sum_core(self, value):
        return value

    def add_wide(self, value):
        return value

    def sum_wide(self, value):
        return value

    def add_deep(self, value):
        return value

    def some(self, value):
        return value

    def add_far(self, value):
        return value

    def sum_far(self, value):
        return (value,)

    def add_pair(self, first, second):
        return first[0], second

    def last_far(self, pair, ready):
        return pair

    def finish_pair(self, pair, split):
        return pair

    def finish(self, value):
        return value


def body(
    tokens, memory, directions, target_len, memory_len, self_qkv, self_out, cross_query, cross_kv,
    cross_out, ffn_in, ffn_out, vectors, cotangent,
):
    tokens, memory, cotangent = tokens[0], memory[0], cotangent[0]
    length, width = tokens.shape
    others = memory.shape[0]
    devices = lax.axis_size("dp")
    rows = self_out.shape[0] // width
    chunks = width // UNIT
    parts = ffn_in.shape[0] // (rows * width)
    hidden = parts * width
    head_dim = width // HEADS
    order = place_order()
    order = order + [place ^ 1 for place in order]
    nearby = devices == chunks == len(order)
    me = lax.axis_index("dp") if nearby else jnp.int32(0)
    ways = Staged() if nearby else Plain(devices, chunks, rows, width, order)

    def stack(flat, by_row=False):
        if by_row:
            return flat
        return flat.reshape(rows, -1, width).transpose(1, 0, 2).reshape(-1)

    def piece_of(*flats):
        return jnp.concatenate(flats).reshape(-1, width)

    facts = jnp.concatenate([directions, target_len, memory_len, me[None]])
    one = stack(self_qkv)
    if nearby:
        one = jnp.concatenate([one, jnp.pad(vectors, (0, 8 * width - vectors.shape[0]))])
    one = piece_of(one)
    two = piece_of(*[stack(w) for w in (self_out, cross_query, cross_kv, cross_out)])
    if nearby:
        first = one.shape[0]
        slabs = ways.deep(jnp.concatenate([one, two], 0))
        one = ways.join([slab[:, :first] for slab in slabs])
        three = ways.deep(after(piece_of(stack(ffn_in), stack(ffn_out, True)), one))
        one = ways.wide(one)
        two = ways.join([slab[:, first:] for slab in slabs])
        one = [one[0], *after(one[1:], three[1:])]
        one = one, [swap(part, 1) for part in one]
    else:
        one, two = ways.both(ways.deep(one)), ways.deep(two)
        three = ways.deep(piece_of(stack(ffn_in), stack(ffn_out, True)), parts * rows)
    two = after(two, one)
    two_sent = ways.wide(two)

    if nearby:
        held = jnp.concatenate(
            [part[:, 3 * UNIT, : vectors.shape[0]] for side in one for part in side], 0
        )
        wanted = jnp.bitwise_xor(me, lax.iota(jnp.int32, chunks))
        choice = (wanted[:, None] == jnp.array(order, jnp.int32)[None, :]).astype(full)
        vector_full = lax.dot(choice.astype(low), held, preferred_element_type=full)
    else:
        vector_full = lax.all_gather(vectors, "dp", axis=0, tiled=True).astype(full)
    vector_rows = vector_full.reshape(-1, width)

    smem = pl.BlockSpec(memory_space=pltpu.SMEM)
    facts = (facts, smem)
    vector_rows = (vector_rows, in_place(vector_rows.shape))
    sem = pltpu.SemaphoreType.DMA
    vm = pltpu.VMEM
    head_dim = width // HEADS
    steps = length // STEP
    along = columns_block(width)
    by_head, by_head_other = head_block(head_dim, length), head_block(head_dim, others)
    eight = in_place((8, width))

    def units(count):
        return vm((count, width, width), low)

    def stored(count):
        return ((chunks // 2, count * UNIT, width), low, None)

    def remote(pair):
        return [(pair[0], None), (pair[1], None)]

    low_t, full_t = ((width, length), low), ((width, length), full)
    low_m = ((width, others), low)
    sums = ((HEADS, length), full, in_place((HEADS, length)))

    all_t, all_m = vm((width, length), low), vm((width, others), low)
    begin, begin_rows = first_columns(width, steps), first_rows(width, steps)
    token_t, q, k, v, mix, sums_one, columns = call(
        self_forward_kernel, steps + HEADS,
        [facts, (after(tokens, two), begin_rows), *remote(one), vector_rows],
        [(*low_t, begin)] * 4 + [(*full_t, later_head(head_dim, length, steps)), sums,
         ((width, 128), full, in_place((width, 128)))],
        [all_t, all_t, all_t, units(3), sem, pltpu.SMEM((2,), full)],
        8.0,
    )
    columns = (columns, in_place((width, 128)))
    three = ways.join(after(three, sums_one))
    two = ways.cross(two_sent, sums_one)
    three_sent = ways.wide(three)
    hat, scale, memory_t, cq, ck, cv, cross_mix, sums_two = call(
        cross_forward_kernel, steps + HEADS,
        [facts, (after(token_t, three), begin), (memory, begin_rows), (mix, begin), *remote(two),
         columns],
        [(*full_t, begin), ((8, length), full, first_columns(8, steps)), (*low_m, begin),
         (*low_t, begin), (*low_m, begin), (*low_m, begin),
         (*full_t, later_head(head_dim, length, steps)), sums],
        [all_t, all_m, all_m, units(4), sem, vm((AUG, others), low), pltpu.SMEM((2,), full)],
        12.0,
    )
    three = ways.cross(three_sent, sums_two)
    whole_t = in_place((width, length))
    out, dr_two, dcross, keep_three, send_three, g_cross_out, rows_ffn = call(
        ffn_kernel, 1,
        [facts, (hat, whole_t), (cross_mix, whole_t), (cotangent, None), *remote(two),
         *remote(three), columns],
        [((length, width), low, None), (*full_t, whole_t), (*low_t, whole_t),
         stored(2 * parts), stored(2 * parts),
         ((width, width), low, in_place((width, width))), ((16, width), full, in_place((16, width)))],
        [units(1), units(parts), vm((chunks, parts, UNIT, width), low), units(parts),
         vm((chunks, parts, UNIT, width), low), vm((hidden, length), full),
         vm((hidden, length), low), vm((length, width), low), vm((length, width), low),
         pltpu.SemaphoreType.DMA((5,))],
        20.0,
        56,
    )
    g_three = ways.add_core(keep_three, send_three, parts)
    dcq, dck, dcv = call(
        cross_backward_kernel, HEADS,
        [facts, (cq, by_head), (ck, by_head_other), (cv, by_head_other), (cross_mix, by_head),
         (sums_two, sums[2]), (dcross, by_head)],
        [(*low_t, by_head), (*low_m, by_head_other), (*low_m, by_head_other)],
        [vm((head_dim, others), full), vm((head_dim, others), full), vm((AUG, others), low)],
        16.0,
    )
    g_three = ways.sum_core(after(g_three, dcq))
    dcq = after(dcq, g_three)
    g_three = ways.add_wide(g_three)
    square = vm((width, width), full)
    broad = columns_block(width, PAIR)
    dr_one, dself, keep_two, send_two, rows_cross = call(
        middle_kernel, length // PAIR,
        [facts, (dcq, broad), (dck, broad), (dcv, broad), (dr_two, broad), (hat, broad),
         (scale, columns_block(8, PAIR)), (memory_t, broad), (mix, broad), *remote(two),
         (g_cross_out, in_place((width, width))), columns],
        [(*full_t, broad), (*low_t, broad), stored(5), stored(5), ((8, width), full, eight)],
        [units(2), units(5), square, square, square, square, vm((3, width, 128), full), sem],
        5.0,
        30,
    )
    g_two = ways.add_core(keep_two, send_two)
    early, late = (head_block(head_dim, length, at, HEADS // 2) for at in (0, HEADS // 2))
    half_t = (width // 2, length)
    dq_one, dk_one, dv_one = call(
        self_backward_kernel, HEADS // 2,
        [facts, (q, early), (k, early), (v, early), (mix, early), (sums_one, sums[2]),
         (dself, early)],
        [(half_t, low, early)] * 3,
        [vm((head_dim, length), full), vm((head_dim, length), full)],
        6.0,
    )
    g_three = ways.sum_wide(after(g_three, dv_one))
    g_two = ways.sum_core(after(g_two, dv_one))
    dself = after(dself, g_two, g_three)
    g_two = ways.add_wide(g_two)
    g_three = ways.add_far(g_three)
    whole = in_place(half_t)
    grads, keep_one, send_one, rows_self = call(
        self_finish_kernel, HEADS // 2 + 1,
        [facts, (q, late), (k, late), (v, late), (mix, late), (sums_one, sums[2]),
         (dself, late), (token_t, in_place((width, length))), (dq_one, whole),
         (dk_one, whole), (dv_one, whole), (rows_ffn, in_place((16, width))),
         (rows_cross, eight), *remote(one), columns],
        [((3 * width // 2, length), low, in_place((3 * width // 2, length))), stored(4), stored(4),
         ((8, width), full, eight)],
        [vm((head_dim, length), full), vm((head_dim, length), full),
         units(3), vm((chunks, 1, UNIT, width), low), units(3), sem, sem],
        8.0,
    )
    if not nearby:
        keep_one, send_one = keep_one[:, : 3 * UNIT], send_one[:, : 3 * UNIT]
    g_two = ways.sum_wide(after(g_two, keep_one))
    g_three = ways.sum_far(after(g_three, keep_one))
    split = g_three[0].shape[0]
    g_one = ways.add_core(after(keep_one, g_two, g_three), send_one)
    pair = ways.add_pair(g_three, g_two)
    g_one = ways.sum_core(g_one)
    grads = after(grads, g_one)
    g_one = ways.add_wide(g_one)
    half_along = columns_block(width // 2)
    (d_tokens,) = call(
        token_grad_kernel, steps,
        [facts, (dq_one, half_along), (dk_one, half_along), (dv_one, half_along),
         (grads, columns_block(3 * width // 2)), (dr_one, along), *remote(one)],
        [((length, width), full, rows_block(width))],
        [units(3), sem],
        3.0,
    )
    pair = ways.last_far(pair, d_tokens)
    (d_memory,) = call(
        memory_grad_kernel, steps,
        [facts, (after(dck, d_tokens, ways.some(g_one)), along), (dcv, along), *remote(two)],
        [((others, width), full, rows_block(width))],
        [units(2), sem],
        2.0,
    )
    g_one = ways.sum_wide(after(g_one, d_memory))
    def flat(grad, first, stop):
        piece = grad[first * rows : stop * rows].reshape(stop - first, rows, width)
        return piece.transpose(1, 0, 2).reshape(-1)

    g_three, g_two = ways.finish_pair(after(pair, g_one), split)
    ready = (
        flat(g_two, 0, 1), flat(g_two, 1, 2), flat(g_two, 2, 4), flat(g_two, 4, 5),
        flat(g_three, 0, parts), g_three[parts * rows :].reshape(-1),
    )
    g_one = ways.add_deep(g_one)
    g_one = ways.finish(after(g_one, ready))
    if nearby:
        g_vectors = g_one[3 * UNIT, : vectors.shape[0]]
    else:
        g_vectors = jnp.concatenate(
            [
                rows_self[0:1], rows_self[2:3], rows_cross[2:3], rows_cross[0:2], rows_ffn[5:6],
                rows_ffn[4:5], rows_cross[3:4], rows_ffn[6:8], rows_cross[4:5], rows_ffn[8:10],
                rows_self[3:5], rows_ffn[0:4],
            ],
            0,
        ).reshape(-1)
        g_vectors = lax.psum_scatter(g_vectors, "dp", scatter_dimension=0, tiled=True)

    return (
        out[None], d_tokens[None], d_memory[None],
        flat(g_one, 0, 3), *ready, g_vectors,
    )


def solution(mesh):
    rows, flat = P("dp", None, None), P("dp")
    return jax.shard_map(
        body,
        mesh=mesh,
        in_specs=(rows, rows) + (flat,) * 11 + (rows,),
        out_specs=(rows,) * 3 + (flat,) * 8,
        check_vma=False,
    )
```

```python
import jax
import jax.numpy as jnp
from jax import lax
from jax.experimental import pallas as pl
from jax.experimental.pallas import tpu as pltpu
from jax.sharding import PartitionSpec as P

HEADS = 8
STEP = 256
PAIR = 2 * STEP
AUG = 16
UNIT = 16
SAFE_SQUARE = 3600.0
mask_fill = -1000000000.0
norm_eps = 1e-05
low = jnp.bfloat16
full = jnp.float32


def contract(left, right, left_dim, right_dim):
    return lax.dot_general(
        left, right, (((left_dim,), (right_dim,)), ((), ())), preferred_element_type=full
    )


def nn(left, right):
    return contract(left, right, 1, 0)


def tn(left, right):
    return contract(left, right, 0, 0)


def nt(left, right):
    return contract(left, right, 1, 1)


def block(index):
    return slice(index * STEP, (index + 1) * STEP)


def blocks_of(length):
    return (length + STEP - 1) // STEP


def split_three(values):
    first = values.astype(low)
    rest = values - first.astype(full)
    second = rest.astype(low)
    third = (rest - second.astype(full)).astype(low)
    return first, second, third


def normalize(values):
    center = jnp.mean(values, axis=0, keepdims=True)
    offsets = values - center
    spread = jnp.mean(offsets * offsets, axis=0, keepdims=True)
    scale = lax.rsqrt(spread + norm_eps)
    return offsets * scale, scale


def norm_backward(grad, hat, scale, gain):
    scaled = grad * gain
    center = jnp.mean(scaled, axis=0, keepdims=True)
    along = jnp.mean(scaled * hat, axis=0, keepdims=True)
    return (scaled - center - hat * along) * scale


def fold_lanes(values):
    total = values[:, :128]
    for start in range(128, values.shape[1], 128):
        total = total + values[:, start : start + 128]
    return total


def lane_total(partial):
    ones = jnp.ones((8, 128), full)
    return lax.dot_general(
        ones,
        partial,
        (((1,), (1,)), ((), ())),
        precision=lax.Precision.HIGHEST,
        preferred_element_type=full,
    )[0:1]


def token_total(values):
    return nt(jnp.ones((AUG, values.shape[1]), low), values)[0:1]


def head_rows(head, head_dim):
    return pl.ds(pl.multiple_of(head * head_dim, head_dim), head_dim)


def square_peak(values, head_dim):
    squares = jnp.square(values.astype(full))
    count = values.shape[0] // head_dim
    return jnp.max(jnp.sum(squares.reshape(count, head_dim, values.shape[1]), axis=1))


def place_order():
    return [side ^ deep for side in (0, 2, 4, 6) for deep in (0, 8, 16, 24)]


def unit_spot(whole, owner, by_row):
    if by_row:
        return whole.at[owner]
    return whole.at[:, pl.ds(pl.multiple_of(owner * UNIT, UNIT), UNIT), :]


def unit_part(buffer, index, first, stop):
    part = buffer.at[index, first * UNIT : stop * UNIT]
    return part.reshape(stop - first, UNIT, buffer.shape[2])


def start_fetch(me, near, far, moves, sem):
    for index, relative in enumerate(place_order()):
        for sources, place in ((near, relative), (far, relative ^ 1)):
            owner = jnp.bitwise_xor(me, place)
            each = sources[0].shape[0]
            for target, first, stop, by_row in moves:
                spot = unit_spot(target, owner, by_row)
                part = unit_part(sources[index // each], index % each, first, stop)
                pltpu.make_async_copy(part, spot, sem).start()


def wait_fetch(moves, sem):
    for target, first, stop, by_row in moves:
        pltpu.make_async_copy(target, target, sem).wait()


def start_store(me, near, far, moves, sem):
    for index, relative in enumerate(place_order()):
        for sink, place in ((near, relative), (far, relative ^ 1)):
            owner = jnp.bitwise_xor(me, place)
            for source, first, stop, by_row in moves:
                spot = unit_spot(source, owner, by_row)
                part = unit_part(sink, index, first, stop)
                pltpu.make_async_copy(spot, part, sem).start()


def clear_from(ref, start):
    rows, columns = ref.shape
    if start < columns:
        ref[:, start:] = jnp.zeros((rows, columns - start), ref.dtype)


def attend_forward(
    q_ref, k_ref, v_ref, mix_ref, sums_ref, head, mask_rows, pairs, keys, shifted
):
    causal = mask_rows is None
    head_dim = q_ref.shape[0]
    key_head = k_ref[:, :keys]
    if not causal:
        key_head = jnp.concatenate([key_head, mask_rows[:, :keys]], 0)
    value_head = jnp.concatenate([v_ref[:, :keys], jnp.ones((AUG, keys), low)], 0)
    for pair in range(pairs):
        columns = slice(pair * PAIR, (pair + 1) * PAIR)
        query = q_ref[:, columns]
        if causal:
            main = pair * PAIR + STEP
            scores = tn(key_head[:, :main], query)
            late = tn(key_head[:, main : main + STEP], query[:, STEP:])
            key_pos = lax.broadcasted_iota(jnp.int32, (STEP, STEP), 0)
            query_pos = lax.broadcasted_iota(jnp.int32, (STEP, STEP), 1)
            allowed = key_pos <= query_pos
            edge = scores[main - STEP :]
            edge = jnp.concatenate(
                [jnp.where(allowed, edge[:, :STEP], mask_fill), edge[:, STEP:]], 1
            )
            scores = edge if main == STEP else jnp.concatenate([scores[: main - STEP], edge], 0)
            late = jnp.where(allowed, late, mask_fill)
        else:
            query = jnp.concatenate([query, jnp.ones((AUG, PAIR), low)], 0)
            scores = tn(key_head, query)
        if shifted:
            highest = jnp.max(scores, axis=0, keepdims=True)
            if causal:
                second = jnp.maximum(highest[:, STEP:], jnp.max(late, axis=0, keepdims=True))
                highest = jnp.concatenate([highest[:, :STEP], second], 1)
                late = late - second
            scores = scores - highest
        powered = jnp.exp(scores).astype(low)
        if causal:
            mixed = nn(value_head[:, :main], powered)
            extra = nn(value_head[:, main : main + STEP], jnp.exp(late).astype(low))
            mixed = jnp.concatenate([mixed[:, :STEP], mixed[:, STEP:] + extra], 1)
        else:
            mixed = nn(value_head, powered)
        total = mixed[head_dim : head_dim + 1]
        mix_ref[:, columns] = mixed[:head_dim] / total
        log_sum = jnp.log(total)
        sums_ref[pl.ds(head, 1), columns] = log_sum + highest if shifted else log_sum
    clear_from(mix_ref, pairs * PAIR)


def attend_backward(
    q_ref, k_ref, v_ref, mix_ref, sums_ref, head, grad_ref, dq_ref, dk_ref, dv_ref,
    key_sum, value_sum, mask_rows, steps, keys
):
    causal = mask_rows is None
    length = steps * STEP
    scale = q_ref.shape[0] ** (-0.5)
    key_head = k_ref[:, :keys]
    value_head = v_ref[:, :keys]
    query = q_ref[:, :length]
    grad = grad_ref[:, :length]
    inner = jnp.sum(grad.astype(full) * mix_ref[:, :length], axis=0, keepdims=True)
    one = jnp.ones((1, length), low)
    blank = jnp.zeros((AUG - 4, length), low)
    query_aug = jnp.concatenate(
        [query, *split_three(sums_ref[pl.ds(head, 1), :length]), one, blank], 0
    )
    grad_aug = jnp.concatenate([grad, *split_three(inner), one, blank], 0)
    minus = jnp.full((3, keys), -1.0, low)
    key_blank = jnp.zeros((AUG - 3, keys), low)
    value_aug = jnp.concatenate([value_head, minus, key_blank], 0)
    if causal:
        key_aug = jnp.concatenate([key_head, minus, key_blank], 0)
    else:
        key_aug = jnp.concatenate([key_head, minus, mask_rows[0:1, :keys], key_blank[1:]], 0)
    for step in range(steps):
        span = block(step)
        count = (step + 1) * STEP if causal else keys
        scores = tn(query_aug[:, span], key_aug[:, :count])
        chances = jnp.exp(scores)
        if causal:
            query_pos = lax.broadcasted_iota(jnp.int32, (STEP, STEP), 0)
            key_pos = lax.broadcasted_iota(jnp.int32, (STEP, STEP), 1)
            edge = jnp.where(key_pos <= query_pos, chances[:, count - STEP :], 0.0)
            chances = (
                edge if count == STEP
                else jnp.concatenate([chances[:, : count - STEP], edge], 1)
            )
        grad_chances = tn(grad_aug[:, span], value_aug[:, :count])
        grad_scores = (chances * grad_chances).astype(low)
        to_value = nn(grad[:, span], chances.astype(low))
        to_key = nn(query[:, span], grad_scores)
        to_query = nt(key_head[:, :count], grad_scores)
        dq_ref[:, span] = (to_query * scale).astype(low)
        if step == 0:
            value_sum[:, :count] = to_value
            key_sum[:, :count] = to_key
        elif causal:
            old = count - STEP
            value_sum[:, :old] += to_value[:, :old]
            key_sum[:, :old] += to_key[:, :old]
            value_sum[:, old:count] = to_value[:, old:]
            key_sum[:, old:count] = to_key[:, old:]
        else:
            value_sum[:, :count] += to_value
            key_sum[:, :count] += to_key
    dv_ref[:, :keys] = value_sum[:, :keys].astype(low)
    dk_ref[:, :keys] = key_sum[:, :keys].astype(low)
    clear_from(dq_ref, length)
    clear_from(dk_ref, keys)
    clear_from(dv_ref, keys)


def add_to(first, rows, index, value):
    if first:
        rows[index : index + 1] = value
    else:
        rows[index : index + 1] += value


def gather_into(first, ref, value):
    if first:
        ref[...] = value
    else:
        ref[...] += value


def self_forward_kernel(
    facts, tokens, near, far, vector_rows, token_t, q_ref, k_ref, v_ref, mix_ref, sums_ref, columns,
    q_all, k_all, v_all, held, sem, peaks
):
    step = pl.program_id(0)
    width, length = q_all.shape
    blocks = length // STEP
    head_dim = width // HEADS
    moves = [(held, 0, 3, False)]

    @pl.when(step == 0)
    def prepare():
        start_fetch(facts[3], near, far, moves, sem)
        peaks[0] = 0.0
        peaks[1] = 0.0
        rest = jnp.zeros((128 - vector_rows.shape[0], width), full)
        columns[...] = jnp.concatenate([vector_rows[...], rest], 0).T

    @pl.when((step < blocks) & (step < blocks_of(facts[1])))
    def live():
        embed = jnp.where(facts[0] == 1, columns[:, 14:15], columns[:, 13:14])
        flipped = tokens[...].T
        token_t[...] = flipped
        shared = (flipped.astype(full) + embed).astype(low)
        pl.when(step == 0)(lambda: wait_fetch(moves, sem))
        query = (tn(held[0], shared) + columns[:, 0:1]).astype(low) * (head_dim ** (-0.5))
        key = tn(held[1], shared).astype(low)
        value = (tn(held[2], shared) + columns[:, 1:2]).astype(low)
        spot = pl.ds(pl.multiple_of(step * STEP, STEP), STEP)
        for ref, all_ref, made in (
            (q_ref, q_all, query), (k_ref, k_all, key), (v_ref, v_all, value)
        ):
            ref[...] = made
            all_ref[:, spot] = made
        peaks[0] = jnp.maximum(peaks[0], square_peak(query, head_dim))
        peaks[1] = jnp.maximum(peaks[1], square_peak(key, head_dim))

    @pl.when((step < blocks) & (step >= blocks_of(facts[1])))
    def dead():
        spot = pl.ds(pl.multiple_of(step * STEP, STEP), STEP)
        token_t[...] = jnp.zeros_like(token_t)
        for ref, all_ref in ((q_ref, q_all), (k_ref, k_all), (v_ref, v_all)):
            ref[...] = jnp.zeros_like(ref)
            all_ref[:, spot] = jnp.zeros_like(ref)

    head = step - blocks
    safe = peaks[0] * peaks[1] <= SAFE_SQUARE
    pairs = (blocks_of(facts[1]) + 1) // 2
    rows = pl.ds(pl.multiple_of(jnp.maximum(head, 0) * head_dim, head_dim), head_dim)
    for wanted in range(1, length // PAIR + 1):
        for shifted in (False, True):

            @pl.when((step >= blocks) & (pairs == wanted) & (safe != shifted))
            def attend():
                attend_forward(
                    q_all.at[rows], k_all.at[rows], v_all.at[rows], mix_ref, sums_ref, head, None,
                    wanted, wanted * PAIR, shifted,
                )


def fill_mask(mask_ref, visible):
    position = lax.broadcasted_iota(jnp.int32, mask_ref.shape, 1)
    row = lax.broadcasted_iota(jnp.int32, mask_ref.shape, 0)
    hidden = (position >= visible) & (row == 0)
    mask_ref[...] = jnp.where(hidden, mask_fill, 0.0).astype(low)


def cross_forward_kernel(
    facts, token_t, memory, mix, near, far, columns,
    hat_ref, scale_ref, memory_t, q_ref, k_ref, v_ref, mix_ref, sums_ref,
    q_all, k_all, v_all, held, sem, mask_ref, peaks
):
    step = pl.program_id(0)
    width, length = q_all.shape
    others = k_all.shape[1]
    blocks = max(length, others) // STEP
    head_dim = width // HEADS
    moves = [(held, 0, 4, False)]
    spot = pl.ds(pl.multiple_of(jnp.minimum(step, blocks - 1) * STEP, STEP), STEP)

    @pl.when(step == 0)
    def prepare():
        start_fetch(facts[3], near, far, moves, sem)
        fill_mask(mask_ref, facts[2])
        peaks[0] = 0.0
        peaks[1] = 0.0

    @pl.when((step < blocks) & (step < blocks_of(facts[2])))
    def encode():
        flipped = memory[...].T
        memory_t[...] = flipped
        pl.when(step == 0)(lambda: wait_fetch(moves, sem))
        key = tn(held[2], flipped).astype(low)
        value = (tn(held[3], flipped) + columns[:, 4:5]).astype(low)
        k_ref[...] = key
        v_ref[...] = value
        k_all[:, spot] = key
        v_all[:, spot] = value
        peaks[1] = jnp.maximum(peaks[1], square_peak(key, head_dim))

    @pl.when((step < blocks) & (step < blocks_of(facts[1])))
    def first():
        embed = jnp.where(facts[0] == 1, columns[:, 14:15], columns[:, 13:14])
        started = token_t[...].astype(full) + embed
        total = started + tn(held[0], mix[...].astype(low)) + columns[:, 2:3]
        hat, scale = normalize(total)
        hat_ref[...] = hat
        scale_ref[...] = jnp.broadcast_to(scale, scale_ref.shape)
        shared = (hat * columns[:, 7:8] + columns[:, 10:11]).astype(low)
        query = (tn(held[1], shared) + columns[:, 3:4]).astype(low) * (head_dim ** (-0.5))
        q_ref[...] = query
        q_all[:, spot] = query
        peaks[0] = jnp.maximum(peaks[0], square_peak(query, head_dim))

    @pl.when((step < blocks) & (step >= blocks_of(facts[2])))
    def hidden():
        memory_t[...] = jnp.zeros_like(memory_t)
        for ref, all_ref in ((k_ref, k_all), (v_ref, v_all)):
            ref[...] = jnp.zeros_like(ref)
            all_ref[:, spot] = jnp.zeros_like(ref)

    @pl.when((step < blocks) & (step >= blocks_of(facts[1])))
    def dead():
        hat_ref[...] = jnp.zeros_like(hat_ref)
        scale_ref[...] = jnp.zeros_like(scale_ref)
        q_ref[...] = jnp.zeros_like(q_ref)
        q_all[:, spot] = jnp.zeros_like(q_ref)

    head = step - blocks
    safe = peaks[0] * peaks[1] <= SAFE_SQUARE
    pairs = (blocks_of(facts[1]) + 1) // 2
    key_count = blocks_of(facts[2])
    rows = pl.ds(pl.multiple_of(jnp.maximum(head, 0) * head_dim, head_dim), head_dim)
    for wanted in range(1, length // PAIR + 1):
        for wanted_keys in range(1, others // STEP + 1):
            for shifted in (False, True):

                @pl.when(
                    (step >= blocks) & (pairs == wanted) & (key_count == wanted_keys)
                    & (safe != shifted)
                )
                def attend():
                    attend_forward(
                        q_all.at[rows], k_all.at[rows], v_all.at[rows], mix_ref, sums_ref, head,
                        mask_ref[...], wanted, wanted_keys * STEP, shifted,
                    )


def gelu_parts(values):
    half = 0.5 * (1.0 + lax.erf(values * (0.5**0.5)))
    bell = jnp.exp(-0.5 * values * values) * 0.3989422804014327
    return values * half, half + values * bell


def ffn_kernel(
    facts, hat_one, cross_mix, cotangent, near_two, far_two, near, far, columns,
    out_ref, dr_ref, dmix_ref, keep, send, g_cross_out, g_rows,
    c_out, f_in, f_out, low_in, low_out, slope, acts, top_ref, result_ref, sems
):
    length, width = top_ref.shape
    parts = f_in.shape[0]
    rows_of = width // parts // UNIT
    moves_two = [(c_out, 4, 5, False)]
    moves_in = [(f_in, 0, parts, False)]
    moves_out = [(f_out, parts, 2 * parts, True)]
    stores_in = [(low_in, 0, parts, False)]
    stores_out = [(low_out, parts, 2 * parts, True)]
    fetch_top = pltpu.make_async_copy(cotangent, top_ref, sems.at[3])
    store_result = pltpu.make_async_copy(result_ref, out_ref, sems.at[4])
    start_fetch(facts[3], near_two, far_two, moves_two, sems.at[0])
    start_fetch(facts[3], near, far, moves_in, sems.at[1])
    start_fetch(facts[3], near, far, moves_out, sems.at[2])
    fetch_top.start()
    g_rows[...] = jnp.zeros_like(g_rows)

    def out_part(part):
        return f_out[part * rows_of : (part + 1) * rows_of].reshape(width, width)

    def live(count):
        span = slice(0, count)
        wait_fetch(moves_two, sems.at[0])
        position = lax.broadcasted_iota(jnp.int32, (1, count), 1)
        valid = (position < facts[1]).astype(full)
        mixed = cross_mix[:, span].astype(low)
        first = hat_one[:, span] * columns[:, 7:8] + columns[:, 10:11]
        total = first + tn(c_out[0], mixed) + columns[:, 5:6]
        hat_two, scale_two = normalize(total)
        second = hat_two * columns[:, 8:9] + columns[:, 11:12]
        shared = second.astype(low)
        third = second + columns[:, 6:7]
        wait_fetch(moves_in, sems.at[1])
        for part in range(parts):
            chunk = slice(part * width, (part + 1) * width)
            raw = tn(f_in[part], shared) + columns[:, 15 + part : 16 + part]
            act, slope_part = gelu_parts(raw)
            slope[chunk, span] = slope_part
            acts[chunk, span] = act.astype(low)
            if part == 0:
                wait_fetch(moves_out, sems.at[2])
            third = third + tn(out_part(part), acts[chunk, span])
        hat_three, scale_three = normalize(third)
        result = (hat_three * columns[:, 9:10] + columns[:, 12:13]) * valid
        result_ref[span, :] = result.astype(low).T
        if count < length:
            result_ref[count:, :] = jnp.zeros((length - count, width), low)
        store_result.start()
        fetch_top.wait()
        top = top_ref[span, :].T.astype(full) * valid
        g_rows[7:8] = lane_total(fold_lanes(top * hat_three))
        g_rows[9:10] = lane_total(fold_lanes(top))
        grad_third = norm_backward(top, hat_three, scale_three, columns[:, 9:10])
        branch = grad_third.astype(low)
        g_rows[4:5] = token_total(branch)
        grad_second = grad_third
        for part in range(parts):
            chunk = slice(part * width, (part + 1) * width)
            back = nn(out_part(part), branch)
            rows = slice(part * rows_of, (part + 1) * rows_of)
            low_out[rows] = nt(acts[chunk, span], branch).astype(low).reshape(
                rows_of, parts, UNIT, width
            )
            acts[chunk, span] = (back * slope[chunk, span]).astype(low)
        start_store(facts[3], keep, send, stores_out, sems.at[2])
        for part in range(parts):
            chunk = slice(part * width, (part + 1) * width)
            grad_hidden = acts[chunk, span]
            g_rows[part : part + 1] = token_total(grad_hidden)
            low_in[part] = nt(shared, grad_hidden).astype(low)
            grad_second = grad_second + nn(f_in[part], grad_hidden)
        start_store(facts[3], keep, send, stores_in, sems.at[1])
        g_rows[6:7] = lane_total(fold_lanes(grad_second * hat_two))
        g_rows[8:9] = lane_total(fold_lanes(grad_second))
        grad_two = norm_backward(grad_second, hat_two, scale_two, columns[:, 8:9])
        dr_ref[:, span] = grad_two
        branch_two = grad_two.astype(low)
        g_rows[5:6] = token_total(branch_two)
        g_cross_out[...] = nt(mixed, branch_two).astype(low)
        dmix_ref[:, span] = nn(c_out[0], branch_two).astype(low)

    live(length)
    wait_fetch(stores_out, sems.at[2])
    wait_fetch(stores_in, sems.at[1])
    store_result.wait()


def cross_backward_kernel(
    facts, q_ref, k_ref, v_ref, cross_mix, sums_ref, dmix, dq_ref, dk_ref, dv_ref,
    key_sum, value_sum, mask_ref
):
    head = pl.program_id(0)
    length = q_ref.shape[1]
    others = k_ref.shape[1]
    count = blocks_of(facts[1])
    key_count = blocks_of(facts[2])

    @pl.when(head == 0)
    def prepare():
        fill_mask(mask_ref, facts[2])

    for wanted in range(1, length // STEP + 1):
        for wanted_keys in range(1, others // STEP + 1):

            @pl.when((count == wanted) & (key_count == wanted_keys))
            def attend():
                attend_backward(
                    q_ref, k_ref, v_ref, cross_mix, sums_ref, head, dmix,
                    dq_ref, dk_ref, dv_ref, key_sum, value_sum, mask_ref[...],
                    wanted, wanted_keys * STEP,
                )


def middle_kernel(
    facts, dq_ref, dk_ref, dv_ref, dr_two, hat_one, scale_one, memory_t, mix, near, far,
    g_cross_out, columns, dr_ref, dself, keep, send, g_rows,
    held, made_low, sum_query, sum_key, sum_value, sum_out, lanes, sem
):
    step = pl.program_id(0)
    moves = [(held, 0, 2, False)]

    @pl.when(step == 0)
    def prepare():
        start_fetch(facts[3], near, far, moves, sem)
        g_rows[...] = jnp.zeros_like(g_rows)
        lanes[...] = jnp.zeros_like(lanes)
        wait_fetch(moves, sem)

    span = dq_ref.shape[1]

    def encode(initial):
        add_to(initial, g_rows, 1, token_total(dv_ref[...]))
        gather_into(initial, sum_key, nt(memory_t[...], dk_ref[...]))
        gather_into(initial, sum_value, nt(memory_t[...], dv_ref[...]))

    def first(initial):
        hat = hat_one[...]
        shared = (hat * columns[:, 7:8] + columns[:, 10:11]).astype(low)
        grad_query = dq_ref[...]
        add_to(initial, g_rows, 0, token_total(grad_query))
        gather_into(initial, sum_query, nt(shared, grad_query))
        grad = dr_two[...] + nn(held[1], grad_query)
        lanes[0] += fold_lanes(grad * hat)
        lanes[1] += fold_lanes(grad)
        grad_one = norm_backward(grad, hat, scale_one[0:1], columns[:, 7:8])
        dr_ref[...] = grad_one
        lanes[2] += fold_lanes(grad_one)
        branch = grad_one.astype(low)
        add_to(initial, g_rows, 2, token_total(branch))
        gather_into(initial, sum_out, nt(mix[...].astype(low), branch))
        dself[...] = nn(held[0], branch).astype(low)

    pl.when(step == 0)(lambda: encode(True))
    pl.when((step > 0) & (step * span < facts[2]))(lambda: encode(False))
    pl.when(step == 0)(lambda: first(True))
    pl.when((step > 0) & (step * span < facts[1]))(lambda: first(False))

    @pl.when((step > 0) & (step * span >= facts[1]))
    def dead():
        dr_ref[...] = jnp.zeros_like(dr_ref)
        dself[...] = jnp.zeros_like(dself)


    @pl.when(step == pl.num_programs(0) - 1)
    def close():
        made_low[0] = sum_out[...].astype(low)
        made_low[1] = sum_query[...].astype(low)
        made_low[2] = sum_key[...].astype(low)
        made_low[3] = sum_value[...].astype(low)
        made_low[4] = g_cross_out[...]
        stores = [(made_low, 0, 5, False)]
        start_store(facts[3], keep, send, stores, sem)
        g_rows[3:4] = lane_total(lanes[0])
        g_rows[4:5] = lane_total(lanes[1])
        g_rows[5:6] = lane_total(lanes[2])
        wait_fetch(stores, sem)


def memory_grad_kernel(facts, dk_ref, dv_ref, near, far, d_memory, held, sem):
    step = pl.program_id(0)
    moves = [(held, 2, 4, False)]

    @pl.when(step == 0)
    def prepare():
        start_fetch(facts[3], near, far, moves, sem)
        wait_fetch(moves, sem)

    @pl.when(step < blocks_of(facts[2]))
    def live():
        d_memory[...] = (nn(held[0], dk_ref[...]) + nn(held[1], dv_ref[...])).T

    @pl.when(step >= blocks_of(facts[2]))
    def blank():
        d_memory[...] = jnp.zeros_like(d_memory)


def self_backward_kernel(
    facts, q_ref, k_ref, v_ref, mix, sums_ref, dself, dq_ref, dk_ref, dv_ref, key_sum, value_sum
):
    head = pl.program_id(0)
    count = blocks_of(facts[1])
    for wanted in range(1, q_ref.shape[1] // STEP + 1):

        @pl.when(count == wanted)
        def attend():
            attend_backward(
                q_ref, k_ref, v_ref, mix, sums_ref, head, dself, dq_ref, dk_ref, dv_ref,
                key_sum, value_sum, None, wanted, wanted * STEP,
            )


def self_finish_kernel(
    facts, q_ref, k_ref, v_ref, mix, sums_ref, dself, token_t, dq_one, dk_one, dv_one,
    rows_ffn, rows_cross, near, far, columns,
    grads, keep, send, g_rows,
    key_sum, value_sum, made_low, made_rows, held, sem, sem_out
):
    step_at = pl.program_id(0)
    last = pl.num_programs(0) - 1
    head = step_at + HEADS // 2
    head_dim, length = q_ref.shape
    width = token_t.shape[0]
    half = width // 2
    count = blocks_of(facts[1])
    moves = [(held, 0, 3, False)]

    @pl.when(step_at == 0)
    def prepare():
        start_fetch(facts[3], near, far, moves, sem)

    def place(part):
        start = pl.multiple_of(part * half + step_at * head_dim, head_dim)
        return grads.at[pl.ds(start, head_dim)]

    for wanted in range(1, length // STEP + 1):

        @pl.when((step_at < last) & (count == wanted))
        def attend():
            attend_backward(
                q_ref, k_ref, v_ref, mix, sums_ref, head, dself,
                place(0), place(1), place(2), key_sum, value_sum, None, wanted, wanted * STEP,
            )

    @pl.when(step_at == last)
    def weights():
        embed = jnp.where(facts[0] == 1, columns[:, 14:15], columns[:, 13:14])
        g_rows[...] = jnp.zeros_like(g_rows)

        shared = (token_t[...].astype(full) + embed).astype(low)
        for part, early in enumerate((dq_one, dk_one, dv_one)):
            both = jnp.concatenate([early[...], grads[part * half : (part + 1) * half, :]], 0)
            g_rows[part : part + 1] = token_total(both)
            made_low[part] = nt(shared, both).astype(low)
        stores = [(made_low, 0, 3, False)]
        start_store(facts[3], keep, send, stores, sem_out)
        wait_fetch(moves, sem)
        total = rows_cross[5:6]
        for part in range(3):
            pieces = jnp.concatenate(
                [*split_three(g_rows[part : part + 1]), jnp.zeros((AUG - 3, width), low)], 0
            )
            total = total + jnp.sum(nt(pieces, held[part]), axis=0, keepdims=True)
        g_rows[3:4] = jnp.where(facts[0] == 1, 0.0, total)
        g_rows[4:5] = jnp.where(facts[0] == 1, total, 0.0)
        picks = [
            g_rows[0:1], g_rows[2:3], rows_cross[2:3], rows_cross[0:1], rows_cross[1:2],
            rows_ffn[5:6], rows_ffn[4:5], rows_cross[3:4], rows_ffn[6:7], rows_ffn[7:8],
            rows_cross[4:5], rows_ffn[8:9], rows_ffn[9:10], g_rows[3:4], g_rows[4:5],
            *[rows_ffn[part : part + 1] for part in range(4)],
        ]
        share = len(picks) * width // made_rows.shape[0]
        for owner in range(made_rows.shape[0]):
            row, start = divmod(owner * share, width)
            stop = min(start + share, width)
            pieces = [picks[row][:, start:stop]]
            if stop - start < share:
                pieces.append(picks[row + 1][:, : share - (stop - start)])
            pieces.append(jnp.zeros((1, width - share), full))
            line = jnp.concatenate(pieces, 1)
            made_rows[owner, 0] = jnp.concatenate(
                [line, jnp.zeros((UNIT - 1, width), full)], 0
            ).astype(low)
        more = [(made_rows, 3, 4, True)]
        start_store(facts[3], keep, send, more, sem)
        wait_fetch(stores, sem_out)
        wait_fetch(more, sem)


def token_grad_kernel(
    facts, dq_one, dk_one, dv_one, grads, dr_one, near, far, d_tokens, held, sem
):
    step = pl.program_id(0)
    width = dr_one.shape[0]
    moves = [(held, 0, 3, False)]

    @pl.when(step == 0)
    def prepare():
        start_fetch(facts[3], near, far, moves, sem)
        wait_fetch(moves, sem)

    @pl.when(step < blocks_of(facts[1]))
    def live():
        made = dr_one[...]
        half = width // 2
        for part, early in enumerate((dq_one, dk_one, dv_one)):
            both = jnp.concatenate([early[...], grads[part * half : (part + 1) * half, :]], 0)
            made = made + nn(held[part], both)
        d_tokens[...] = made.T

    @pl.when(step >= blocks_of(facts[1]))
    def blank():
        d_tokens[...] = jnp.zeros_like(d_tokens)


def in_place(shape):
    return pl.BlockSpec(shape, lambda step: (0,) * len(shape))


def columns_block(rows, span=STEP):
    return pl.BlockSpec((rows, span), lambda step: (0, step))


def rows_block(columns, span=STEP):
    return pl.BlockSpec((span, columns), lambda step: (step, 0))


def first_columns(rows, count):
    return pl.BlockSpec((rows, STEP), lambda step: (0, jnp.minimum(step, count - 1)))


def first_rows(columns, count):
    return pl.BlockSpec((STEP, columns), lambda step: (jnp.minimum(step, count - 1), 0))


def later_head(head_dim, columns, count):
    return pl.BlockSpec((head_dim, columns), lambda step: (jnp.maximum(step - count, 0), 0))


def head_block(head_dim, columns, first=0, count=HEADS):
    return pl.BlockSpec(
        (head_dim, columns), lambda step: (first + jnp.minimum(step, count - 1), 0)
    )


def call(kernel, steps, ins, outs, scratch, cost, room=0):
    room = room or (56 if kernel in (self_forward_kernel, cross_forward_kernel) else 20)
    def spec_of(spec, array=None):
        if isinstance(array, list):
            return [spec_of(spec)] * len(array)
        return pl.BlockSpec(memory_space=pl.ANY) if spec is None else spec

    return pl.pallas_call(
        kernel,
        grid=(steps,),
        out_shape=[jax.ShapeDtypeStruct(shape, dtype) for shape, dtype, spec in outs],
        in_specs=[spec_of(spec, array) for array, spec in ins],
        out_specs=[spec_of(spec) for shape, dtype, spec in outs],
        scratch_shapes=scratch,
        compiler_params=pltpu.CompilerParams(
            vmem_limit_bytes=room * 2**20, dimension_semantics=("arbitrary",)
        ),
        cost_estimate=pl.CostEstimate(
            flops=int(cost * 1.0e9), bytes_accessed=4 * 2**20, transcendentals=0
        ),
        name=kernel.__name__,
    )(*[array for array, spec in ins])


SIDES = (0, 2, 4, 6)
DEPTHS = (0, 8, 16, 24)


def swap(values, mask):
    count = lax.axis_size("dp")
    return lax.ppermute(values, "dp", [(spot, spot ^ mask) for spot in range(count)])


def spread_along(held, masks):
    return [held] + [swap(held, mask) for mask in masks[1:]]


def after(value, *earlier):
    return lax.optimization_barrier((value, earlier))[0]


class Staged:
    def deep(self, piece, late=0):
        return spread_along(piece[None], DEPTHS)

    def wide(self, held):
        return spread_along(held, SIDES)

    def both(self, held):
        return [held], [swap(held, 1)]

    def join(self, parts):
        return jnp.concatenate(parts, 0)

    def cross(self, parts, ready):
        far = [swap(parts[0], 1)]
        parts = [parts[0], *after(parts[1:], ready)]
        return parts, far + [swap(part, 1) for part in parts[1:]]

    def add_core(self, keep, send, late=0):
        return keep, swap(send, 1)

    def sum_core(self, pair):
        keep, got = pair
        sums = [
            keep[4 * side : 4 * side + 4].astype(full) + got[4 * side : 4 * side + 4].astype(full)
            for side in range(4)
        ]
        return [sums[0]] + [part.astype(keep.dtype) for part in sums[1:]]

    def add_wide(self, sums):
        return [sums[0]] + [swap(sums[side], SIDES[side]) for side in range(1, 4)]

    def total(self, parts):
        total = parts[0]
        for part in parts[1:]:
            total = total + part.astype(full)
        return total

    def sum_wide(self, parts):
        wire = parts[1].dtype
        total = self.total(parts)
        return [total[0]] + [total[deep].astype(wire) for deep in range(1, 4)]

    def add_deep(self, sums):
        return [sums[0]] + [swap(sums[deep], DEPTHS[deep]) for deep in range(1, 4)]

    def some(self, parts):
        return parts[3]

    def add_far(self, sums):
        return sums[:2] + [swap(sums[deep], DEPTHS[deep]) for deep in (2, 3)]

    def sum_far(self, parts):
        return self.total([parts[0], *parts[2:]]), parts[1]

    def add_pair(self, first, second):
        both = jnp.concatenate([first[1], second[1]], 0)
        return first[0], second[0], swap(both, DEPTHS[1]), swap(second[2], DEPTHS[2]), second[3]

    def last_far(self, pair, ready):
        return *pair[:4], swap(after(pair[4], ready), DEPTHS[3])

    def finish_pair(self, pair, split):
        first, second, both, *rest = pair
        return self.total([first, both[:split]]), self.total([second, both[split:], *rest])

    def finish(self, parts):
        return self.total(parts)


class Plain:
    def __init__(self, devices, chunks, rows, width, order):
        self.devices, self.chunks, self.rows, self.width = devices, chunks, rows, width
        self.order = order

    def arrange(self, gathered, by_row):
        group = self.devices // self.chunks
        split = gathered.reshape(self.chunks, group, -1, self.rows, self.width)
        if not by_row:
            split = split.transpose(0, 2, 1, 3, 4)
        return split.reshape(self.chunks, -1, self.width)

    def spread(self, ordered, by_row):
        group = self.devices // self.chunks
        if by_row:
            return ordered.reshape(self.devices, -1, self.width)
        split = ordered.reshape(self.chunks, -1, group, self.rows, self.width)
        return split.transpose(0, 2, 1, 3, 4).reshape(self.devices, -1, self.width)

    def deep(self, piece, late=0):
        gathered = lax.all_gather(piece, "dp", axis=0)
        plain = piece.shape[0] - late
        ordered = self.arrange(gathered[:, :plain], False)
        if late:
            ordered = jnp.concatenate([ordered, self.arrange(gathered[:, plain:], True)], 1)
        return jnp.take(ordered, jnp.array(self.order), axis=0)

    def wide(self, held):
        return held

    def join(self, held):
        return held

    def both(self, held):
        return [held[: self.chunks // 2]], [held[self.chunks // 2 :]]

    def cross(self, held, ready):
        return self.both(held)

    def add_core(self, keep, send, late=0):
        back = [self.order.index(place) for place in range(self.chunks)]
        ordered = jnp.take(jnp.concatenate([keep, send], 0), jnp.array(back), axis=0)
        plain = ordered.shape[1] - late * UNIT
        split = self.spread(ordered[:, :plain], False)
        if late:
            split = jnp.concatenate([split, self.spread(ordered[:, plain:], True)], 1)
        return lax.psum_scatter(split.astype(full), "dp", scatter_dimension=0, tiled=False)

    def sum_core(self, value):
        return value

    def add_wide(self, value):
        return value

    def sum_wide(self, value):
        return value

    def add_deep(self, value):
        return value

    def some(self, value):
        return value

    def add_far(self, value):
        return value

    def sum_far(self, value):
        return (value,)

    def add_pair(self, first, second):
        return first[0], second

    def last_far(self, pair, ready):
        return pair

    def finish_pair(self, pair, split):
        return pair

    def finish(self, value):
        return value


def body(
    tokens, memory, directions, target_len, memory_len, self_qkv, self_out, cross_query, cross_kv,
    cross_out, ffn_in, ffn_out, vectors, cotangent,
):
    tokens, memory, cotangent = tokens[0], memory[0], cotangent[0]
    length, width = tokens.shape
    others = memory.shape[0]
    devices = lax.axis_size("dp")
    rows = self_out.shape[0] // width
    chunks = width // UNIT
    parts = ffn_in.shape[0] // (rows * width)
    hidden = parts * width
    head_dim = width // HEADS
    order = place_order()
    order = order + [place ^ 1 for place in order]
    nearby = devices == chunks == len(order)
    me = lax.axis_index("dp") if nearby else jnp.int32(0)
    ways = Staged() if nearby else Plain(devices, chunks, rows, width, order)

    def stack(flat, by_row=False):
        if by_row:
            return flat
        return flat.reshape(rows, -1, width).transpose(1, 0, 2).reshape(-1)

    def piece_of(*flats):
        return jnp.concatenate(flats).reshape(-1, width)

    facts = jnp.concatenate([directions, target_len, memory_len, me[None]])
    one = stack(self_qkv)
    if nearby:
        one = jnp.concatenate([one, jnp.pad(vectors, (0, 8 * width - vectors.shape[0]))])
    one = piece_of(one)
    two = piece_of(*[stack(w) for w in (self_out, cross_query, cross_kv, cross_out)])
    if nearby:
        first = one.shape[0]
        slabs = ways.deep(jnp.concatenate([one, two], 0))
        one = ways.join([slab[:, :first] for slab in slabs])
        three = ways.deep(after(piece_of(stack(ffn_in), stack(ffn_out, True)), one))
        one = ways.wide(one)
        two = ways.join([slab[:, first:] for slab in slabs])
        one = [one[0], *after(one[1:], three[1:])]
        one = one, [swap(part, 1) for part in one]
    else:
        one, two = ways.both(ways.deep(one)), ways.deep(two)
        three = ways.deep(piece_of(stack(ffn_in), stack(ffn_out, True)), parts * rows)
    two = after(two, one)
    two_sent = ways.wide(two)

    if nearby:
        held = jnp.concatenate(
            [part[:, 3 * UNIT, : vectors.shape[0]] for side in one for part in side], 0
        )
        wanted = jnp.bitwise_xor(me, lax.iota(jnp.int32, chunks))
        choice = (wanted[:, None] == jnp.array(order, jnp.int32)[None, :]).astype(full)
        vector_full = lax.dot(choice.astype(low), held, preferred_element_type=full)
    else:
        vector_full = lax.all_gather(vectors, "dp", axis=0, tiled=True).astype(full)
    vector_rows = vector_full.reshape(-1, width)

    smem = pl.BlockSpec(memory_space=pltpu.SMEM)
    facts = (facts, smem)
    vector_rows = (vector_rows, in_place(vector_rows.shape))
    sem = pltpu.SemaphoreType.DMA
    vm = pltpu.VMEM
    head_dim = width // HEADS
    steps = length // STEP
    along = columns_block(width)
    by_head, by_head_other = head_block(head_dim, length), head_block(head_dim, others)
    eight = in_place((8, width))

    def units(count):
        return vm((count, width, width), low)

    def stored(count):
        return ((chunks // 2, count * UNIT, width), low, None)

    def remote(pair):
        return [(pair[0], None), (pair[1], None)]

    low_t, full_t = ((width, length), low), ((width, length), full)
    low_m = ((width, others), low)
    sums = ((HEADS, length), full, in_place((HEADS, length)))

    all_t, all_m = vm((width, length), low), vm((width, others), low)
    begin, begin_rows = first_columns(width, steps), first_rows(width, steps)
    token_t, q, k, v, mix, sums_one, columns = call(
        self_forward_kernel, steps + HEADS,
        [facts, (after(tokens, two), begin_rows), *remote(one), vector_rows],
        [(*low_t, begin)] * 4 + [(*full_t, later_head(head_dim, length, steps)), sums,
         ((width, 128), full, in_place((width, 128)))],
        [all_t, all_t, all_t, units(3), sem, pltpu.SMEM((2,), full)],
        8.0,
    )
    columns = (columns, in_place((width, 128)))
    three = ways.join(after(three, sums_one))
    two = ways.cross(two_sent, sums_one)
    three_sent = ways.wide(three)
    hat, scale, memory_t, cq, ck, cv, cross_mix, sums_two = call(
        cross_forward_kernel, steps + HEADS,
        [facts, (after(token_t, three), begin), (memory, begin_rows), (mix, begin), *remote(two),
         columns],
        [(*full_t, begin), ((8, length), full, first_columns(8, steps)), (*low_m, begin),
         (*low_t, begin), (*low_m, begin), (*low_m, begin),
         (*full_t, later_head(head_dim, length, steps)), sums],
        [all_t, all_m, all_m, units(4), sem, vm((AUG, others), low), pltpu.SMEM((2,), full)],
        12.0,
    )
    three = ways.cross(three_sent, sums_two)
    whole_t = in_place((width, length))
    out, dr_two, dcross, keep_three, send_three, g_cross_out, rows_ffn = call(
        ffn_kernel, 1,
        [facts, (hat, whole_t), (cross_mix, whole_t), (cotangent, None), *remote(two),
         *remote(three), columns],
        [((length, width), low, None), (*full_t, whole_t), (*low_t, whole_t),
         stored(2 * parts), stored(2 * parts),
         ((width, width), low, in_place((width, width))), ((16, width), full, in_place((16, width)))],
        [units(1), units(parts), vm((chunks, parts, UNIT, width), low), units(parts),
         vm((chunks, parts, UNIT, width), low), vm((hidden, length), full),
         vm((hidden, length), low), vm((length, width), low), vm((length, width), low),
         pltpu.SemaphoreType.DMA((5,))],
        20.0,
        56,
    )
    g_three = ways.add_core(keep_three, send_three, parts)
    dcq, dck, dcv = call(
        cross_backward_kernel, HEADS,
        [facts, (cq, by_head), (ck, by_head_other), (cv, by_head_other), (cross_mix, by_head),
         (sums_two, sums[2]), (dcross, by_head)],
        [(*low_t, by_head), (*low_m, by_head_other), (*low_m, by_head_other)],
        [vm((head_dim, others), full), vm((head_dim, others), full), vm((AUG, others), low)],
        16.0,
    )
    g_three = ways.sum_core(after(g_three, dcq))
    dcq = after(dcq, g_three)
    g_three = ways.add_wide(g_three)
    square = vm((width, width), full)
    broad = columns_block(width, PAIR)
    dr_one, dself, keep_two, send_two, rows_cross = call(
        middle_kernel, length // PAIR,
        [facts, (dcq, broad), (dck, broad), (dcv, broad), (dr_two, broad), (hat, broad),
         (scale, columns_block(8, PAIR)), (memory_t, broad), (mix, broad), *remote(two),
         (g_cross_out, in_place((width, width))), columns],
        [(*full_t, broad), (*low_t, broad), stored(5), stored(5), ((8, width), full, eight)],
        [units(2), units(5), square, square, square, square, vm((3, width, 128), full), sem],
        5.0,
        30,
    )
    g_two = ways.add_core(keep_two, send_two)
    early, late = (head_block(head_dim, length, at, HEADS // 2) for at in (0, HEADS // 2))
    half_t = (width // 2, length)
    dq_one, dk_one, dv_one = call(
        self_backward_kernel, HEADS // 2,
        [facts, (q, early), (k, early), (v, early), (mix, early), (sums_one, sums[2]),
         (dself, early)],
        [(half_t, low, early)] * 3,
        [vm((head_dim, length), full), vm((head_dim, length), full)],
        6.0,
    )
    g_three = ways.sum_wide(after(g_three, dv_one))
    g_two = ways.sum_core(after(g_two, dv_one))
    dself = after(dself, g_two, g_three)
    g_two = ways.add_wide(g_two)
    g_three = ways.add_far(g_three)
    whole = in_place(half_t)
    grads, keep_one, send_one, rows_self = call(
        self_finish_kernel, HEADS // 2 + 1,
        [facts, (q, late), (k, late), (v, late), (mix, late), (sums_one, sums[2]),
         (dself, late), (token_t, in_place((width, length))), (dq_one, whole),
         (dk_one, whole), (dv_one, whole), (rows_ffn, in_place((16, width))),
         (rows_cross, eight), *remote(one), columns],
        [((3 * width // 2, length), low, in_place((3 * width // 2, length))), stored(4), stored(4),
         ((8, width), full, eight)],
        [vm((head_dim, length), full), vm((head_dim, length), full),
         units(3), vm((chunks, 1, UNIT, width), low), units(3), sem, sem],
        8.0,
    )
    if not nearby:
        keep_one, send_one = keep_one[:, : 3 * UNIT], send_one[:, : 3 * UNIT]
    g_two = ways.sum_wide(after(g_two, keep_one))
    g_three = ways.sum_far(after(g_three, keep_one))
    split = g_three[0].shape[0]
    g_one = ways.add_core(after(keep_one, g_two, g_three), send_one)
    pair = ways.add_pair(g_three, g_two)
    g_one = ways.sum_core(g_one)
    grads = after(grads, g_one)
    g_one = ways.add_wide(g_one)
    half_along = columns_block(width // 2)
    (d_tokens,) = call(
        token_grad_kernel, steps,
        [facts, (dq_one, half_along), (dk_one, half_along), (dv_one, half_along),
         (grads, columns_block(3 * width // 2)), (dr_one, along), *remote(one)],
        [((length, width), full, rows_block(width))],
        [units(3), sem],
        3.0,
    )
    pair = ways.last_far(pair, d_tokens)
    (d_memory,) = call(
        memory_grad_kernel, steps,
        [facts, (after(dck, d_tokens, ways.some(g_one)), along), (dcv, along), *remote(two)],
        [((others, width), full, rows_block(width))],
        [units(2), sem],
        2.0,
    )
    g_one = ways.sum_wide(after(g_one, d_memory))
    def flat(grad, first, stop):
        piece = grad[first * rows : stop * rows].reshape(stop - first, rows, width)
        return piece.transpose(1, 0, 2).reshape(-1)

    g_three, g_two = ways.finish_pair(after(pair, g_one), split)
    ready = (
        flat(g_two, 0, 1), flat(g_two, 1, 2), flat(g_two, 2, 4), flat(g_two, 4, 5),
        flat(g_three, 0, parts), g_three[parts * rows :].reshape(-1),
    )
    g_one = ways.add_deep(g_one)
    g_one = ways.finish(after(g_one, ready))
    if nearby:
        g_vectors = g_one[3 * UNIT, : vectors.shape[0]]
    else:
        g_vectors = jnp.concatenate(
            [
                rows_self[0:1], rows_self[2:3], rows_cross[2:3], rows_cross[0:2], rows_ffn[5:6],
                rows_ffn[4:5], rows_cross[3:4], rows_ffn[6:8], rows_cross[4:5], rows_ffn[8:10],
                rows_self[3:5], rows_ffn[0:4],
            ],
            0,
        ).reshape(-1)
        g_vectors = lax.psum_scatter(g_vectors, "dp", scatter_dimension=0, tiled=True)

    return (
        out[None], d_tokens[None], d_memory[None],
        flat(g_one, 0, 3), *ready, g_vectors,
    )


def solution(mesh):
    rows, flat = P("dp", None, None), P("dp")
    return jax.shard_map(
        body,
        mesh=mesh,
        in_specs=(rows, rows) + (flat,) * 11 + (rows,),
        out_specs=(rows,) * 3 + (flat,) * 8,
        check_vma=False,
    )
```
